128 devices in a mesh: aa: 4 (over z), ba: 16 (over x, y), ma: 2 (over core).
Axes of the slice: x: 4, y: 4, z: 4, core: 2. Of those that a mesh axis runs over, the one named last changes fastest.
Arguments:
- docs: bfloat16 [1024, 16, 1024], P(('aa', 'ba')), may hold values from -6 to 6
- cot: bfloat16 [1024, 16, 1024], P(('aa', 'ba')), may hold values from -6 to 6
- route: int32 [1024, 1], P(('aa', 'ba')), may hold values from 0 to 15; in each aligned block of 16 rows (0 to 15, 16 to 31, ...) at most 2 rows name the same one
- doc_len: int32 [1024], P(('aa', 'ba')), may hold values from 1 to 16
- wt1: float32 [4, 2, 1024, 4096], P('aa', None, 'ba', 'ma'), may hold values from -0.1875 to 0.1875
- mom1: float32 [4, 2, 1024, 4096], P('aa', None, 'ba', 'ma'), may hold values from -6 to 6
- wt2: float32 [16, 2, 1024, 4096], P('ba', None, 'aa', 'ma'), may hold values from -0.1875 to 0.1875
- mom2: float32 [16, 2, 1024, 4096], P('ba', None, 'aa', 'ma'), may hold values from -6 to 6
Outputs:
- new_wt1: float32 [4, 2, 1024, 4096], P('aa', None, 'ba', 'ma')
- new_mom1: float32 [4, 2, 1024, 4096], P('aa', None, 'ba', 'ma')
- new_wt2: float32 [16, 2, 1024, 4096], P('ba', None, 'aa', 'ma')
- new_mom2: float32 [16, 2, 1024, 4096], P('ba', None, 'aa', 'ma')
The draws below stay inside these ranges and needn't reach their ends.
Inputs may be any that keep to these rules, and one draw needn't show every extreme that they name: `route`: among the 16 documents of one group, no level-2 module is named more than 2 times.
All inputs are finite; a program needn't handle non-finite values.
Results may differ from the reference program's by a relative error of at most 0.023.
Values may be sent and summed in bfloat16 or wider, within the bound.
A program may use at most 256 MiB of HBM per device.

```python
import math
import jax
import jax.numpy as jnp
import numpy as np
from jax import lax

D = 1024
FF = 4096
BLOCK = 16
SLOT = 2
DOC_DEV = 16
DOCS = 1024
MODS1 = 4
MODS2 = 16
N_AA = 4
N_BA = 16
N_MA = 2


def plant(drawn, own_key, low, high):
    longest = drawn.shape.index(max(drawn.shape))
    spots = []
    for shift in (0, 1):
        where = [jax.random.randint(jax.random.fold_in(own_key, axis), (), 0, length) for axis, length in enumerate(drawn.shape)]
        where[longest] = (where[longest] + shift) % drawn.shape[longest]
        spots.append(tuple(where))
    return drawn.at[spots[0]].set(low).at[spots[1]].set(high)


def steps_of(key, extent, split, smallest, largest):
    def one(position, shards_of):
        steps = jax.random.uniform(jax.random.fold_in(jax.random.fold_in(key, 6), position), (shards_of,), jnp.float32, smallest / len(split), largest / len(split))
        return jnp.repeat(jnp.exp(steps), extent[position] // shards_of).reshape((-1,) + (1,) * (len(extent) - position - 1))

    level = one(*split[0])
    for cut in split[1:]:
        level = level * one(*cut)
    return level


def routed_block(key, own, number, rows, number_of, top, bound, lean):
    sequence = jax.random.permutation(key, number_of)
    crowded, usual = portions_of(number_of, rows * top, bound, lean, True), portions_of(number_of, rows * top, bound, lean, False)
    places = jnp.arange(number_of)

    def named(tallies, rotation):
        used = int((tallies > 0).sum())
        fixed = max(1, used // 4)
        shifted = fixed + (places - fixed + rotation * (used - fixed)) % max(1, number_of - fixed)
        return jnp.zeros((number_of,), jnp.int32).at[sequence[jnp.where(places < fixed, places, shifted)]].set(jnp.asarray(tallies, jnp.int32))

    tallies = jnp.where(number % 4 == 0, named(crowded, number // 4), named(usual, number - number // 4 - 1))
    mixed = jax.random.permutation(jax.random.fold_in(own, 3), number_of)
    donor, taker = mixed[0:number_of // 2 * 2:2], mixed[1:number_of // 2 * 2:2]
    slack = jnp.minimum(tallies[donor] - 1, bound - tallies[taker]) // 2
    slack = jnp.where((donor == sequence[0]) | (taker == sequence[0]) | (tallies[taker] == 0), 0, jnp.maximum(slack, 0))
    shifted = jax.random.randint(jax.random.fold_in(own, 4), (number_of // 2,), 0, 1 << 20) % (slack + 1)
    tallies = tallies.at[donor].add(-shifted).at[taker].add(shifted)
    items = jnp.searchsorted(jnp.cumsum(tallies), jnp.arange(rows * top), side="right").astype(jnp.int32)
    grid = items.reshape(top, rows).T
    grid = grid[jax.random.permutation(jax.random.fold_in(own, 1), rows)]
    rotation = jax.random.randint(jax.random.fold_in(own, 2), (rows, 1), 0, top)
    return jnp.take_along_axis(grid, (jnp.arange(top)[None, :] + rotation) % top, axis=1)


def portions_of(number_of, total, reach, slope, full):
    portions = [(1 << 20) // math.isqrt(rank ** slope) + 1 for rank in range(1, number_of + 1)]
    largest = reach if full else min(reach, max(-(-total // number_of), total * portions[0] // sum(portions)))
    least = 1 if total - largest >= number_of - 1 else 0
    given, surplus = [largest] + [least] * (number_of - 1), total - largest - least * (number_of - 1)
    while surplus > 0:
        free = [i for i in range(1, number_of) if given[i] < largest] or [i for i in range(1, number_of) if given[i] < reach]
        mass, left = sum([portions[i] for i in free]), surplus
        for i in free:
            more = min(reach - given[i], max(1, left * portions[i] // mass), surplus)
            given[i] = given[i] + more
            surplus = surplus - more
    return np.array(given)


def normal_values(key, shape, width, reach, cuts=(), kind=jnp.bfloat16):
    drawn = jax.random.normal(key, shape, jnp.float32) * width
    if len(cuts) > 0:
        drawn = steps_of(key, shape, cuts, -0.22, 0.18) * drawn
    return jnp.clip(drawn, min=-reach, max=reach).astype(kind)


def setup_inputs(seed: int = 0) -> dict:
    splits = jax.random.split(jax.random.key(seed), 9)
    docs = normal_values(splits[0], (DOCS, BLOCK, D), 1.0, 6.0, ((0, 64),))
    cot = normal_values(splits[1], (DOCS, BLOCK, D), 1.0, 6.0, ((0, 64),))
    route_keys = jax.random.split(jax.random.fold_in(splits[2], 1), DOCS // DOC_DEV)
    route_turns = jax.random.permutation(jax.random.fold_in(splits[2], 3), DOCS // DOC_DEV)
    route = jax.vmap(lambda own, number: routed_block(jax.random.fold_in(splits[2], 2), own, number, DOC_DEV, MODS2, 1, SLOT, 2))(route_keys, route_turns).reshape((DOCS, 1))
    doc_len = plant(jax.random.randint(splits[3], (DOCS,), 1, BLOCK + 1), jax.random.fold_in(splits[3], 1), 1, BLOCK).astype(jnp.int32)
    wt1 = normal_values(splits[4], (MODS1, 2, D, FF), D ** -0.5, 0.1875, ((0, 4), (2, 16), (3, 2)), jnp.float32)
    mom1 = normal_values(splits[5], (MODS1, 2, D, FF), 1.0, 6.0, ((0, 4), (2, 16), (3, 2)), jnp.float32)
    wt2 = normal_values(splits[6], (MODS2, 2, D, FF), D ** -0.5, 0.1875, ((0, 16), (2, 4), (3, 2)), jnp.float32)
    mom2 = normal_values(splits[7], (MODS2, 2, D, FF), 1.0, 6.0, ((0, 16), (2, 4), (3, 2)), jnp.float32)
    return dict(docs=docs, cot=cot, route=route, doc_len=doc_len, wt1=wt1, mom1=mom1, wt2=wt2, mom2=mom2)


EPS = 1e-05
MOMENTUM = 0.9
OUTER_RATE = 0.7

def normalize(inputs):
    floated = inputs.astype(jnp.float32)
    factor = lax.rsqrt(lax.optimization_barrier(jnp.mean(floated * floated, axis=-1, keepdims=True)) + EPS)
    normed = floated * factor
    return (floated, factor, normed, normed.astype(jnp.bfloat16))

def split_sum(left, weight):
    pieces = FF // N_MA
    total = jnp.zeros((left.shape[0], weight.shape[0]), jnp.float32)
    for index in range(N_MA):
        lhs = left[:, index * pieces:(index + 1) * pieces]
        rhs = weight[:, index * pieces:(index + 1) * pieces]
        partial_value = lax.dot_general(lhs, rhs, (((1,), (1,)), ((), ())), preferred_element_type=jnp.float32)
        rounded = lax.optimization_barrier(partial_value.astype(jnp.bfloat16))
        total = total + rounded.astype(jnp.float32)
    return total

def slopes_of(upstream, preact, weights):
    incoming = jnp.dot(upstream, weights[1], preferred_element_type=jnp.float32)
    sigma = jax.nn.sigmoid(preact)
    return (incoming * sigma * (1.0 + preact * (1.0 - sigma))).astype(jnp.bfloat16)

def weight_terms(normed_low, slopes, upstream, active):
    first = lax.dot_general(normed_low, slopes, (((0,), (0,)), ((), ())), preferred_element_type=jnp.float32)
    second = lax.dot_general(upstream, active, (((0,), (0,)), ((), ())), preferred_element_type=jnp.float32)
    return jnp.stack([first, second])

def selection(targets):
    count = targets.shape[-1]
    shared = targets[..., :, None] == targets[..., None, :]
    before = jnp.arange(count)[:, None] > jnp.arange(count)[None, :]
    rank = lax.optimization_barrier(jnp.sum((shared & before).astype(jnp.int32), axis=-1))
    target_slot = targets * SLOT + rank
    slot_ids = jnp.arange(N_BA * SLOT, dtype=jnp.int32)
    return (slot_ids[:, None] == target_slot[..., None, :]).astype(jnp.float32)

def reference(docs, cot, route, doc_len, wt1, mom1, wt2, mom2):
    per = docs.shape[0] // (N_AA * N_BA)
    inside = jnp.arange(BLOCK, dtype=jnp.int32)[None, :] < doc_len[:, None]
    masked = jnp.where(inside[:, :, None], cot, jnp.zeros_like(cot))
    source = docs.reshape(N_AA, N_BA, per, BLOCK, D)
    masked = masked.reshape(N_AA, N_BA, per, BLOCK, D)
    selector = selection(route[:, 0].reshape(N_AA, N_BA, per))
    weights_two = wt2.astype(jnp.bfloat16)
    summed_two = jnp.zeros(wt2.shape, jnp.float32)
    level_terms = []

    def path_step(items):
        weights, inputs, target = items
        rows_in = inputs.reshape(-1, D)
        upstream = target.reshape(-1, D)
        floated, factor, normed, normed_low = normalize(rows_in)
        preact = jnp.dot(normed_low, weights[0], preferred_element_type=jnp.float32)
        active = jax.nn.silu(preact).astype(jnp.bfloat16)
        slopes = slopes_of(upstream, preact, weights)
        terms = weight_terms(normed_low, slopes, upstream, active).astype(jnp.bfloat16)
        dnorm = split_sum(slopes, weights[0])
        back = upstream.astype(jnp.float32) + factor * (dnorm - normed * lax.optimization_barrier(jnp.mean(dnorm * normed, axis=-1, keepdims=True)))
        return (terms, back.astype(jnp.bfloat16).reshape(N_BA, SLOT, BLOCK, D))
    for level in range(N_AA):
        weights_one = wt1[level].astype(jnp.bfloat16)
        rows_in = source[level].reshape(-1, D)
        floated, factor, normed, normed_low = normalize(rows_in)
        preact = jnp.dot(normed_low, weights_one[0], preferred_element_type=jnp.float32)
        active = jax.nn.silu(preact).astype(jnp.bfloat16)
        output = (floated + split_sum(active, weights_one[1])).astype(jnp.bfloat16)
        output = output.reshape(N_BA, per, BLOCK, D)
        chosen = selector[level]
        packed = jnp.einsum('bsp,bptc->bstc', chosen, output.astype(jnp.float32)).astype(jnp.bfloat16)
        packed = packed.reshape(N_BA, N_BA, SLOT, BLOCK, D).transpose(1, 0, 2, 3, 4)
        carried = jnp.einsum('bsp,bptc->bstc', chosen, masked[level].astype(jnp.float32)).astype(jnp.bfloat16)
        carried = carried.reshape(N_BA, N_BA, SLOT, BLOCK, D).transpose(1, 0, 2, 3, 4)
        terms, backs = lax.map(path_step, (weights_two, packed, carried))
        terms = lax.optimization_barrier(terms)
        summed_two = summed_two + terms.astype(jnp.float32)
        returned = backs.transpose(1, 0, 2, 3, 4).reshape(N_BA, N_BA * SLOT, BLOCK, D)
        upstream = jnp.einsum('bsp,bstc->bptc', chosen, returned.astype(jnp.float32)).astype(jnp.bfloat16)
        upstream = upstream.reshape(-1, D)
        slopes = slopes_of(upstream, preact, weights_one)
        level_terms.append(weight_terms(normed_low, slopes, upstream, active))
    delta_one = jnp.stack(level_terms) / N_BA
    delta_two = summed_two / N_AA
    new_mom1 = MOMENTUM * mom1 + delta_one
    new_wt1 = wt1 - OUTER_RATE * (delta_one + MOMENTUM * new_mom1)
    new_mom2 = MOMENTUM * mom2 + delta_two
    new_wt2 = wt2 - OUTER_RATE * (delta_two + MOMENTUM * new_mom2)
    return (new_wt1, new_mom1, new_wt2, new_mom2)
```

```python
import jax
import jax.numpy as jnp
from jax import lax
from jax.experimental import pallas as pl
from jax.experimental.pallas import tpu as pltpu
from jax.sharding import PartitionSpec as P

SLOT = 2
EPS = 1e-05
MOMENTUM = 0.9
OUTER_RATE = 0.7

MESH = pl.DeviceIdType.MESH
BF16 = jnp.bfloat16
F32 = jnp.float32
RING = 4
VMEM_LIMIT = 60 * 1024 * 1024


def dot(left, right, contract=(1, 0)):
    return lax.dot_general(
        left,
        right,
        (((contract[0],), (contract[1],)), ((), ())),
        preferred_element_type=F32,
    )


def wrap(index, size=RING):
    return lax.rem(index + size, size)


class Gather:
    def __init__(self, own, land, rank, device, send, recv):
        up, down = wrap(rank + 1), wrap(rank - 1)

        def copy(number, source, target, to):
            return pltpu.make_async_remote_copy(
                src_ref=source,
                dst_ref=target,
                send_sem=send.at[number],
                recv_sem=recv.at[number],
                device_id=device(to),
                device_id_type=MESH,
            )

        self.direct = [
            copy(0, own(0), land(rank, 0), up),
            copy(1, own(1), land(rank, 1), down),
            copy(2, own(1), land(rank, 1), up),
            copy(3, own(0), land(rank, 0), down),
        ]
        self.passed = [
            copy(4, land(down, 0), land(down, 0), up),
            copy(5, land(up, 1), land(up, 1), down),
        ]

    def start(self):
        for copy in self.direct:
            copy.start()

    def forward(self):
        for near, far in zip(self.direct[:2], self.passed):
            near.wait_recv()
            far.start()

    def near(self):
        for copy in self.direct[2:]:
            copy.wait_recv()

    def far(self):
        for copy in self.passed:
            copy.wait_recv()

    def drain(self):
        for copy in self.direct + self.passed:
            copy.wait_send()


class Scatter:
    def __init__(self, own, summed, bufs, rank, device, send, recv):
        up, down, far = wrap(rank + 1), wrap(rank - 1), wrap(rank + 2)
        through, landed = bufs

        def copy(number, source, target, to):
            return pltpu.make_async_remote_copy(
                src_ref=source,
                dst_ref=target,
                send_sem=send.at[number],
                recv_sem=recv.at[number],
                device_id=device(to),
                device_id_type=MESH,
            )

        self.first = [
            copy(0, own(far, 0), through.at[0], up),
            copy(1, own(far, 1), through.at[1], down),
            copy(2, own(up, 1), landed.at[1], up),
            copy(3, own(down, 0), landed.at[2], down),
        ]
        self.second = [
            copy(4, summed.at[0], landed.at[0], up),
            copy(5, summed.at[1], landed.at[3], down),
        ]
        self.through, self.summed, self.landed = through, summed, landed

    def start(self):
        for copy in self.first:
            copy.start()

    def forward(self, mine):
        for which in range(2):
            self.first[which].wait_recv()
            total = mine(which).astype(F32) + self.through[which].astype(F32)
            self.summed[which] = total.astype(BF16)
            self.second[which].start()

    def finish(self):
        for copy in self.first[2:] + self.second:
            copy.wait_recv()

    def total(self, half, mine):
        return mine.astype(F32) + (
            self.landed[half].astype(F32) + self.landed[2 + half].astype(F32)
        )

    def drain(self):
        for copy in self.first + self.second:
            copy.wait_send()


class Exchange:
    def __init__(self, packed, halves, place, send, recv, pair_send, pair_recv):
        level, base, core = place
        self.place, self.groups = place, packed.shape[0]
        self.packed, self.halves, self.send, self.recv = packed, halves, send, recv
        self.pair = pltpu.make_async_remote_copy(
            src_ref=halves.at[core],
            dst_ref=halves.at[core],
            send_sem=pair_send,
            recv_sem=pair_recv,
            device_id=(level, base, 1 - core),
            device_id_type=MESH,
        )

    def copy(self, step):
        level, base, core = self.place
        target = lax.rem(base + step, self.groups)
        return pltpu.make_async_remote_copy(
            src_ref=self.packed.at[target],
            dst_ref=self.halves.at[core, base],
            send_sem=self.send.at[step],
            recv_sem=self.recv.at[step],
            device_id=(level, target, core),
            device_id_type=MESH,
        )

    def start(self):
        level, base, core = self.place

        def step(number, carry):
            self.copy(number).start()
            return carry

        lax.fori_loop(1, self.groups, step, 0)
        self.halves[core, base] = self.packed[base]

    def turn(self):
        def step(number, carry):
            self.copy(number).wait_recv()
            return carry

        lax.fori_loop(1, self.groups, step, 0)
        self.pair.start()

    def finish(self):
        self.pair.wait_recv()

    def drain(self):
        def step(number, carry):
            self.copy(number).wait_send()
            return carry

        lax.fori_loop(1, self.groups, step, 0)
        self.pair.wait_send()


def greet(devices):
    barrier = pltpu.get_barrier_semaphore()
    for device in devices:
        pl.semaphore_signal(barrier, inc=1, device_id=device, device_id_type=MESH)
    pl.semaphore_wait(barrier, len(devices))


def here():
    level, base, core = lax.axis_index("aa"), lax.axis_index("ba"), lax.axis_index("ma")
    return level, base, core, base // RING, lax.rem(base, RING)


def rms(floated):
    width = floated.shape[-1]
    return lax.rsqrt(jnp.sum(floated * floated, axis=-1, keepdims=True) / width + EPS)


def forward_kernel(
    docs, masked, pick, own1, own2,
    down1, act_out, gate_out, terms_out, back_out,
    weights1, weights2, cot_send, cot, row_send, rows, back_send, back,
    normed1, act1, gate1, part1, part1_in,
    normed2, incoming2, act2, slopes2, dn, dn_in, terms2,
    ring_send, ring_recv, swap_send, swap_recv, pair_send, pair_recv, dn_send, dn_recv, local_sem,
):
    level, base, core, row, col = here()
    width, hidden = weights1.shape[2] * 16, weights1.shape[3]
    half, tile = width // 2, hidden // 4
    groups = cot_send.shape[0]
    deep, block = weights2.shape[2], weights1.shape[2]
    sibling = (level, base, 1 - core)
    greet(
        [sibling, (wrap(level + 1), base, core), (wrap(level - 1), base, core)]
        + [(level, lax.rem(base + step, groups), core) for step in range(1, groups)]
    )

    def at(matrix, along, other):
        return other * RING + along if matrix == 0 else along * RING + other

    def gather1(matrix, phase, shift, number):
        along, other = (col, row) if matrix == 0 else (row, col)
        h = block // 2
        if phase == 0:
            spot = lambda pos: at(matrix, pos, other)
            rank = along
        else:
            fixed = wrap(along + shift)
            spot = lambda pos: at(matrix, fixed, pos)
            rank = other
        land = lambda pos, part: weights1.at[matrix, spot(pos), pl.ds(part * h, h)]
        if phase == 0 or shift == 0:
            own = lambda part: own1.at[matrix, pl.ds(part * h, h)]
        else:
            own = lambda part: land(rank, part)
        device = lambda pos: (level, spot(pos) if phase == 0 else at(matrix, along, pos), core)
        return Gather(own, land, rank, device, ring_send.at[number], ring_recv.at[number])

    first = [gather1(m, 0, 0, m) for m in range(2)]
    second = [[gather1(m, 1, s, 2 + 4 * m + k) for k, s in enumerate((0, -1, 1, 2))] for m in range(2)]

    def gather2(matrix):
        h = deep // 2
        return Gather(
            lambda part: own2.at[matrix, pl.ds(part * h, h)],
            lambda pos, part: weights2.at[matrix, pos, pl.ds(part * h, h)],
            level,
            lambda pos: (pos, base, core),
            ring_send.at[10 + matrix],
            ring_recv.at[10 + matrix],
        )

    column = [gather2(m) for m in range(2)]
    for m in range(2):
        first[m].start()
    for m in (1, 0):
        column[m].start()
    for m in range(2):
        second[m][0].start()
    mine = [
        pltpu.make_async_copy(own1, weights1.at[:, base], local_sem.at[0]),
        pltpu.make_async_copy(own2, weights2.at[:, level], local_sem.at[1]),
    ]
    for copy in mine:
        copy.start()

    place = (level, base, core)
    left = pl.ds(pl.multiple_of(core * half, half), half)
    swaps = [
        Exchange(a, b, place, swap_send.at[k], swap_recv.at[k], pair_send.at[k], pair_recv.at[k])
        for k, (a, b) in enumerate(((cot_send, cot), (row_send, rows), (back_send, back)))
    ]
    cot_send[...] = dot(pick[...], masked[:, left]).astype(BF16).reshape(cot_send.shape)
    swaps[0].start()

    floated = docs[...].astype(F32)
    normed1[...] = (floated * rms(floated)).astype(BF16)

    for m in range(2):
        first[m].forward()
    for m in range(2):
        first[m].near()
        second[m][1].start()
        second[m][2].start()
    for m in range(2):
        first[m].far()
        second[m][3].start()
    for m in range(2):
        second[m][0].forward()
    column[1].forward()
    for k in (1, 2):
        for m in range(2):
            second[m][k].forward()
    swaps[0].turn()
    for m in range(2):
        second[m][3].forward()
    column[0].forward()
    for m in range(2):
        for k in range(4):
            second[m][k].near()
            second[m][k].far()
    mine[0].wait()

    keep_down = pltpu.make_async_copy(weights1.at[1], down1, local_sem.at[2])
    keep_down.start()

    def up_tile(number, carry):
        columns = pl.ds(pl.multiple_of(number * tile, tile), tile)
        pre = dot(normed1[...], weights1[0, :, :, columns].reshape(width, tile))
        sigma = jax.nn.sigmoid(pre)
        act1[:, columns] = (pre * sigma).astype(BF16)
        gate1[:, columns] = (sigma * (1.0 + pre * (1.0 - sigma))).astype(BF16)
        return carry

    lax.fori_loop(0, 4, up_tile, 0)
    keep = [
        pltpu.make_async_copy(act1, act_out, local_sem.at[3]),
        pltpu.make_async_copy(gate1, gate_out, local_sem.at[4]),
    ]
    for copy in keep:
        copy.start()

    def down_tile(number, carry):
        piece = weights1[1, pl.ds(number * 4, 4)].reshape(4 * block, hidden)
        part1[number] = dot(act1[...], piece, (1, 1)).astype(BF16)
        return carry

    lax.fori_loop(0, 4, down_tile, 0)
    give = pltpu.make_async_remote_copy(
        src_ref=part1.at[pl.ds(2 * (1 - core), 2)],
        dst_ref=part1_in,
        send_sem=dn_send.at[4],
        recv_sem=dn_recv.at[4],
        device_id=sibling,
        device_id_type=MESH,
    )
    give.start()
    give.wait_recv()
    quarter = half // 2
    for k in range(2):
        columns = pl.ds(pl.multiple_of(core * half + k * quarter, quarter), quarter)
        total = part1[2 * core + k].astype(F32) + part1_in[k].astype(F32)
        output = (docs[:, columns].astype(F32) + total).astype(BF16)
        row_send[:, :, k * quarter:(k + 1) * quarter] = (
            dot(pick[...], output).astype(BF16).reshape(groups, -1, quarter)
        )
    swaps[1].start()
    swaps[0].finish()

    count = cot.shape[1] * cot.shape[2]
    side = lambda ref, h: ref[h].reshape(count, half)

    def piece2(matrix, h, columns):
        return weights2[matrix, 2 * h:2 * h + 2, :, columns].reshape(half, tile)

    mine[1].wait()
    column[1].near()
    column[1].far()

    def incoming_tile(number, carry):
        columns = pl.ds(pl.multiple_of(number * tile, tile), tile)
        incoming2[:, columns] = dot(side(cot, 0), piece2(1, 0, columns)) + dot(
            side(cot, 1), piece2(1, 1, columns)
        )
        return carry

    lax.fori_loop(0, 4, incoming_tile, 0)
    swaps[1].turn()
    swaps[1].finish()
    floats = [side(rows, h).astype(F32) for h in range(2)]
    square = sum(jnp.sum(f * f, axis=-1, keepdims=True) for f in floats)
    factor = lax.rsqrt(square / width + EPS)
    for h in range(2):
        normed2[h] = (side(rows, h).astype(F32) * factor).astype(BF16)
    column[0].near()
    column[0].far()

    def slope_tile(number, carry):
        columns = pl.ds(pl.multiple_of(number * tile, tile), tile)
        pre = dot(normed2[0], piece2(0, 0, columns)) + dot(normed2[1], piece2(0, 1, columns))
        sigma = jax.nn.sigmoid(pre)
        act2[:, columns] = (pre * sigma).astype(BF16)
        slopes2[:, columns] = (
            incoming2[:, columns] * sigma * (1.0 + pre * (1.0 - sigma))
        ).astype(BF16)
        return carry

    lax.fori_loop(0, 4, slope_tile, 0)

    def dn_copy(number):
        return pltpu.make_async_remote_copy(
            src_ref=dn.at[number],
            dst_ref=dn_in.at[number],
            send_sem=dn_send.at[number],
            recv_sem=dn_recv.at[number],
            device_id=sibling,
            device_id_type=MESH,
        )

    def dn_tile(number, carry):
        dn[number] = dot(slopes2[...], weights2[0, number], (1, 1)).astype(BF16)
        dn_copy(number).start()
        return carry

    lax.fori_loop(0, 4, dn_tile, 0)

    def term_tile(matrix, lefts, right):
        def step(number, carry):
            columns = pl.ds(pl.multiple_of(number * tile, tile), tile)
            for h in range(2):
                terms2[matrix, h * half:(h + 1) * half, columns] = dot(
                    lefts(h), right[:, columns], (0, 0)
                ).astype(BF16)
            return carry

        lax.fori_loop(0, 4, step, 0)
        copy = pltpu.make_async_copy(
            terms2.at[matrix], terms_out.at[matrix], local_sem.at[5 + matrix]
        )
        copy.start()
        return copy

    keep.append(term_tile(1, lambda h: side(cot, h), act2))
    for number in range(4):
        dn_copy(number).wait_recv()

    def dn_of(number):
        return dn[number].astype(F32) + dn_in[number].astype(F32)

    mean = jnp.zeros((count, 1), F32)
    for number in range(4):
        columns = slice((number % 2) * quarter, (number % 2 + 1) * quarter)
        normed = rows[number // 2, :, :, columns].reshape(count, quarter).astype(F32) * factor
        mean = mean + jnp.sum(dn_of(number) * normed, axis=-1, keepdims=True)
    mean = mean / width
    for k in range(2):
        columns = slice(k * quarter, (k + 1) * quarter)
        normed = rows[core, :, :, columns].reshape(count, quarter).astype(F32) * factor
        value = cot[core, :, :, columns].reshape(count, quarter).astype(F32) + factor * (
            dn_of(2 * core + k) - normed * mean
        )
        back_send[:, :, columns] = value.astype(BF16).reshape(groups, -1, quarter)
    swaps[2].start()
    keep.append(term_tile(0, lambda h: normed2[h], slopes2))
    swaps[2].turn()
    swaps[2].finish()
    keep.append(pltpu.make_async_copy(back, back_out, local_sem.at[7]))
    keep[-1].start()

    for gather in first + second[0] + second[1] + column:
        gather.drain()
    for swap in swaps:
        swap.drain()
    give.wait_send()
    for number in range(4):
        dn_copy(number).wait_send()
    keep_down.wait()
    for copy in keep:
        copy.wait()


def backward_kernel(
    docs, pick, down1, act1, gate1, terms2, back,
    sum1, sum2,
    weights1, normed1, upstream, slopes, terms1, own2,
    through, summed, landed, mid, through_b, summed_b, landed_b,
    send, recv, local_sem,
):
    level, base, core, row, col = here()
    width, hidden = docs.shape[1], act1.shape[1]
    half, tile = width // 2, hidden // 4
    block = width // 16
    neighbours = [(wrap(level + s), base, core) for s in (1, -1)]
    neighbours += [(level, wrap(row + s) * RING + col, core) for s in (1, -1)]
    neighbours += [(level, row * RING + wrap(col + s), core) for s in (1, -1)]
    load = pltpu.make_async_copy(down1, weights1, local_sem.at[0])
    load.start()
    h2 = width // 8

    def part2(matrix, pos, part):
        return terms2.at[matrix, pos, pl.ds(part * 2, 2)]

    loads = []
    for m in range(2):
        loads.append(
            [
                pltpu.make_async_copy(part2(m, wrap(level + 1), 0), summed.at[m, 0], local_sem.at[1 + 3 * m]),
                pltpu.make_async_copy(part2(m, wrap(level - 1), 1), summed.at[m, 1], local_sem.at[2 + 3 * m]),
                pltpu.make_async_copy(terms2.at[m, level], own2.at[m], local_sem.at[3 + 3 * m]),
            ]
        )
        for copy in loads[m]:
            copy.start()
    greet(neighbours)

    def scatter2(matrix):
        return Scatter(
            lambda pos, part: part2(matrix, pos, part),
            summed.at[matrix],
            (through.at[matrix], landed.at[matrix]),
            level,
            lambda pos: (pos, base, core),
            send.at[matrix],
            recv.at[matrix],
        )

    column = [scatter2(m) for m in range(2)]
    for scatter in column:
        scatter.start()

    count = back.shape[1] * back.shape[2]
    for h in range(2):
        upstream[h] = dot(pick[...], back[h].reshape(count, half), (0, 0)).astype(BF16)
    floated = docs[...].astype(F32)
    normed1[...] = (floated * rms(floated)).astype(BF16)

    def term_tile(matrix, left, right):
        def step(number, carry):
            columns = pl.ds(pl.multiple_of(number * tile, tile), tile)
            for h in range(2):
                value = dot(left(h), right[:, columns], (0, 0)).astype(BF16)
                terms1[matrix, 2 * h:2 * h + 2, :, :, columns] = value.reshape(2, RING, block, tile)
            return carry

        lax.fori_loop(0, 4, step, 0)

    def part1(matrix, pos, part):
        if matrix == 0:
            return terms1.at[0, pos, pl.ds(part * 2, 2)]
        return terms1.at[1, pl.ds(part * 2, 2), pos]

    def scatter1(matrix):
        if matrix == 0:
            rank, device = row, lambda pos: (level, pos * RING + col, core)
        else:
            rank, device = col, lambda pos: (level, row * RING + pos, core)
        return Scatter(
            lambda pos, part: part1(matrix, pos, part),
            summed.at[2 + matrix],
            (through.at[2 + matrix], landed.at[2 + matrix]),
            rank,
            device,
            send.at[2 + matrix],
            recv.at[2 + matrix],
        )

    plane = [scatter1(m) for m in range(2)]
    term_tile(1, lambda h: upstream[h], act1)
    plane[1].start()
    load.wait()

    def slope_tile(number, carry):
        columns = pl.ds(pl.multiple_of(number * tile, tile), tile)
        incoming = dot(upstream[0], weights1[0:8, :, columns].reshape(half, tile)) + dot(
            upstream[1], weights1[8:16, :, columns].reshape(half, tile)
        )
        slopes[:, columns] = (incoming * gate1[:, columns].astype(F32)).astype(BF16)
        return carry

    lax.fori_loop(0, 4, slope_tile, 0)
    term_tile(0, lambda h: normed1[:, h * half:(h + 1) * half], slopes)
    plane[0].start()

    for m in range(2):
        for copy in loads[m]:
            copy.wait()
    column[0].forward(lambda which: summed[0, which])
    ranks = (row, col)

    def mine1(matrix, pos, part):
        return part1(matrix, pos, part)[...]

    for m in (1, 0):
        plane[m].forward(
            lambda which, m=m: mine1(m, wrap(ranks[m] + 1 - 2 * which), which)
        )
    column[1].forward(lambda which: summed[1, which])

    def scatter_b(matrix):
        if matrix == 0:
            rank, device = col, lambda pos: (level, row * RING + pos, core)
        else:
            rank, device = row, lambda pos: (level, pos * RING + col, core)
        hb = block // 2
        return Scatter(
            lambda pos, part: mid.at[matrix, pos, pl.ds(part * hb, hb)],
            summed_b.at[matrix],
            (through_b.at[matrix], landed_b.at[matrix]),
            rank,
            device,
            send.at[4 + matrix],
            recv.at[4 + matrix],
        )

    last = [scatter_b(m) for m in range(2)]
    for m in (1, 0):
        plane[m].finish()
        for part in range(2):
            mid[m, 2 * part:2 * part + 2] = plane[m].total(part, mine1(m, ranks[m], part)).astype(BF16)
        last[m].start()
    other = (col, row)
    hb = block // 2
    for m in (1, 0):
        last[m].forward(
            lambda which, m=m: mid[m, wrap(other[m] + 1 - 2 * which), pl.ds(which * hb, hb)]
        )
    for m in (1, 0):
        last[m].finish()
        for part in range(2):
            mine = mid[m, other[m], pl.ds(part * hb, hb)]
            sum1[m, part * hb:(part + 1) * hb] = last[m].total(part, mine).astype(BF16)
    for m in range(2):
        column[m].finish()
        for part in range(2):
            mine = own2[m, 2 * part:2 * part + 2]
            sum2[m, 2 * part:2 * part + 2] = column[m].total(part, mine).astype(BF16)
    for scatter in column + plane + last:
        scatter.drain()


def outer_step(weights, moment, delta):
    new_moment = MOMENTUM * moment + delta[None]
    return (weights - OUTER_RATE * (delta[None] + MOMENTUM * new_moment), new_moment)


def local(docs, cot, route, doc_len, wt1, mom1, wt2, mom2):
    blocks, block, width = docs.shape
    groups = lax.axis_size("ba")
    levels = lax.axis_size("aa")
    slots = groups * SLOT
    count, lanes = slots * block, blocks * block
    hidden = wt1.shape[-1]
    inside = lax.broadcasted_iota(jnp.int32, (blocks, block), 1) < doc_len[:, None]
    masked = jnp.where(inside[:, :, None], cot, jnp.zeros_like(cot)).reshape(lanes, width)
    targets = route[:, 0]
    shared = targets[:, None] == targets[None, :]
    before = lax.broadcasted_iota(jnp.int32, (blocks, blocks), 0) > lax.broadcasted_iota(
        jnp.int32, (blocks, blocks), 1
    )
    rank = jnp.sum((shared & before).astype(jnp.int32), axis=1)
    target_row = (targets * SLOT + rank)[:, None] * block + jnp.arange(block, dtype=jnp.int32)[None]
    pick = (
        lax.broadcasted_iota(jnp.int32, (count, lanes), 0) == target_row.reshape(1, lanes)
    ).astype(BF16)
    rows = docs.reshape(lanes, width)

    def shape(*sizes, kind=BF16):
        return jax.ShapeDtypeStruct(sizes, kind)

    whole = pl.BlockSpec(memory_space=pltpu.VMEM)
    anywhere = pl.BlockSpec(memory_space=pl.ANY)
    half, quarter = width // 2, width // 4
    per = count // groups
    swap = [pltpu.VMEM((groups, per, half), BF16), pltpu.VMEM((2, groups, per, half), BF16)]
    down1, act1, gate1, terms2, back = pl.pallas_call(
        forward_kernel,
        out_shape=(
            shape(16, width // 16, hidden),
            shape(lanes, hidden),
            shape(lanes, hidden),
            shape(2, width, hidden),
            shape(2, groups, per, half),
        ),
        in_specs=[whole, whole, whole, anywhere, anywhere],
        out_specs=[anywhere] * 5,
        scratch_shapes=[
            pltpu.VMEM((2, 16, width // 16, hidden), BF16),
            pltpu.VMEM((2, RING, width // 4, hidden), BF16),
        ]
        + swap * 3
        + [
            pltpu.VMEM((lanes, width), BF16),
            pltpu.VMEM((lanes, hidden), BF16),
            pltpu.VMEM((lanes, hidden), BF16),
            pltpu.VMEM((RING, lanes, quarter), BF16),
            pltpu.VMEM((2, lanes, quarter), BF16),
            pltpu.VMEM((2, count, half), BF16),
            pltpu.VMEM((count, hidden), F32),
            pltpu.VMEM((count, hidden), BF16),
            pltpu.VMEM((count, hidden), BF16),
            pltpu.VMEM((RING, count, quarter), BF16),
            pltpu.VMEM((RING, count, quarter), BF16),
            pltpu.VMEM((2, width, hidden), BF16),
            pltpu.SemaphoreType.DMA((12, 6)),
            pltpu.SemaphoreType.DMA((12, 6)),
            pltpu.SemaphoreType.DMA((3, groups)),
            pltpu.SemaphoreType.DMA((3, groups)),
            pltpu.SemaphoreType.DMA((3,)),
            pltpu.SemaphoreType.DMA((3,)),
            pltpu.SemaphoreType.DMA((5,)),
            pltpu.SemaphoreType.DMA((5,)),
            pltpu.SemaphoreType.DMA((8,)),
        ],
        compiler_params=pltpu.CompilerParams(
            collective_id=0, has_side_effects=True, vmem_limit_bytes=VMEM_LIMIT
        ),
        name="forward",
    )(rows, masked, pick, wt1[0].astype(BF16), wt2[0].astype(BF16))

    group = width // 4
    unit = group // 4
    sum1, sum2 = pl.pallas_call(
        backward_kernel,
        out_shape=(shape(2, width // 16, hidden), shape(2, 4, unit, hidden)),
        in_specs=[whole, whole, anywhere, whole, whole, anywhere, whole],
        out_specs=[whole, whole],
        scratch_shapes=[
            pltpu.VMEM((16, width // 16, hidden), BF16),
            pltpu.VMEM((lanes, width), BF16),
            pltpu.VMEM((2, lanes, half), BF16),
            pltpu.VMEM((lanes, hidden), BF16),
            pltpu.VMEM((2, RING, RING, width // 16, hidden), BF16),
            pltpu.VMEM((2, 4, unit, hidden), BF16),
            pltpu.VMEM((4, 2, 2, unit, hidden), BF16),
            pltpu.VMEM((4, 2, 2, unit, hidden), BF16),
            pltpu.VMEM((4, 4, 2, unit, hidden), BF16),
            pltpu.VMEM((2, RING, width // 16, hidden), BF16),
            pltpu.VMEM((2, 2, width // 32, hidden), BF16),
            pltpu.VMEM((2, 2, width // 32, hidden), BF16),
            pltpu.VMEM((2, 4, width // 32, hidden), BF16),
            pltpu.SemaphoreType.DMA((6, 6)),
            pltpu.SemaphoreType.DMA((6, 6)),
            pltpu.SemaphoreType.DMA((7,)),
        ],
        compiler_params=pltpu.CompilerParams(
            collective_id=1, has_side_effects=True, vmem_limit_bytes=VMEM_LIMIT
        ),
        name="backward",
    )(rows, pick, down1, act1, gate1, terms2.reshape(2, RING, 4, unit, hidden), back)
    delta1 = sum1.astype(F32) / groups
    delta2 = sum2.reshape(2, group, hidden).astype(F32) / levels
    new_wt1, new_mom1 = outer_step(wt1, mom1, delta1)
    new_wt2, new_mom2 = outer_step(wt2, mom2, delta2)
    return (new_wt1, new_mom1, new_wt2, new_mom2)


def solution(mesh):
    return jax.shard_map(
        local,
        mesh=mesh,
        in_specs=(
            P(("aa", "ba"), None, None),
            P(("aa", "ba"), None, None),
            P(("aa", "ba"), None),
            P(("aa", "ba")),
            P("aa", None, "ba", "ma"),
            P("aa", None, "ba", "ma"),
            P("ba", None, "aa", "ma"),
            P("ba", None, "aa", "ma"),
        ),
        out_specs=(
            P("aa", None, "ba", "ma"),
            P("aa", None, "ba", "ma"),
            P("ba", None, "aa", "ma"),
            P("ba", None, "aa", "ma"),
        ),
        check_vma=False,
    )
```

```python
import jax
import jax.numpy as jnp
from jax import lax
from jax.experimental import pallas as pl
from jax.experimental.pallas import tpu as pltpu
from jax.sharding import PartitionSpec as P

SLOT = 2
EPS = 1e-05
MOMENTUM = 0.9
OUTER_RATE = 0.7

MESH = pl.DeviceIdType.MESH
BF16 = jnp.bfloat16
F32 = jnp.float32
RING = 4
VMEM_LIMIT = 57 * 1024 * 1024


def dot(left, right, contract=(1, 0)):
    return lax.dot_general(
        left,
        right,
        (((contract[0],), (contract[1],)), ((), ())),
        preferred_element_type=F32,
    )


def wrap(index, size=RING):
    return lax.rem(index + size, size)


def remote(source, target, send, recv, device):
    return pltpu.make_async_remote_copy(
        src_ref=source,
        dst_ref=target,
        send_sem=send,
        recv_sem=recv,
        device_id=device,
        device_id_type=MESH,
    )


def each(first, last, step):
    def body(number, carry):
        step(number)
        return carry

    lax.fori_loop(first, last, body, 0)


class Gather:
    def __init__(self, own, land, rank, device, send, recv):
        up, down = wrap(rank + 1), wrap(rank - 1)

        def copy(number, source, target, to):
            return remote(source, target, send.at[number], recv.at[number], device(to))

        self.direct = [
            copy(0, own(0), land(rank, 0), up),
            copy(1, own(1), land(rank, 1), down),
            copy(2, own(1), land(rank, 1), up),
            copy(3, own(0), land(rank, 0), down),
        ]
        self.passed = [
            copy(4, land(down, 0), land(down, 0), up),
            copy(5, land(up, 1), land(up, 1), down),
        ]

    def start(self):
        for copy in self.direct:
            copy.start()

    def forward(self):
        for near, far in zip(self.direct[:2], self.passed):
            near.wait_recv()
            far.start()

    def near(self):
        for copy in self.direct[2:]:
            copy.wait_recv()

    def far(self):
        for copy in self.passed:
            copy.wait_recv()

    def drain(self):
        for copy in self.direct + self.passed:
            copy.wait_send()


class Scatter:
    def __init__(self, own, bufs, rank, device, send, recv):
        up, down, far = wrap(rank + 1), wrap(rank - 1), wrap(rank + 2)
        through, summed, landed = bufs

        def copy(number, source, target, to):
            return remote(source, target, send.at[number], recv.at[number], device(to))

        self.first = [
            copy(0, own(far, 0), through.at[0], up),
            copy(1, own(far, 1), through.at[1], down),
            copy(2, own(up, 1), landed.at[1], up),
            copy(3, own(down, 0), landed.at[2], down),
        ]
        self.second = [
            copy(4, summed.at[0], landed.at[0], up),
            copy(5, summed.at[1], landed.at[3], down),
        ]
        self.through, self.summed, self.landed = through, summed, landed
        self.own, self.rank = own, rank

    def start(self):
        for copy in self.first:
            copy.start()

    def forward(self):
        for which in range(2):
            self.first[which].wait_recv()
            mine = self.own(wrap(self.rank + 1 - 2 * which), which)[...]
            total = mine.astype(F32) + self.through[which].astype(F32)
            self.summed[which] = total.astype(BF16)
            self.second[which].start()

    def finish(self):
        for copy in self.first[2:] + self.second:
            copy.wait_recv()

    def total(self, half):
        return self.own(self.rank, half)[...].astype(F32) + (
            self.landed[half].astype(F32) + self.landed[2 + half].astype(F32)
        )

    def drain(self):
        for copy in self.first + self.second:
            copy.wait_send()


class Exchange:
    def __init__(self, packed, land, place, send, recv):
        self.place, self.groups = place, packed.shape[0]
        self.packed, self.land, self.send, self.recv = packed, land, send, recv

    def copy(self, step):
        level, base, core = self.place
        target = lax.rem(base + step, self.groups)
        return remote(
            self.packed.at[target],
            self.land.at[base],
            self.send.at[step],
            self.recv.at[step],
            (level, target, core),
        )

    def start(self):
        each(1, self.groups, lambda step: self.copy(step).start())
        base = self.place[1]
        self.land[base] = self.packed[base]

    def wait(self, step):
        self.copy(step).wait_recv()

    def drain(self):
        each(1, self.groups, lambda step: self.copy(step).wait_send())


class Share:
    def __init__(self, exchange, rows, place, partner, sibling, send, recv, last_send, last_recv):
        core = place[2]
        self.exchange, self.groups = exchange, exchange.groups

        def copy(path, step):
            source = wrap(place[1] - step, self.groups)
            mine = rows.at[0, core, source]
            if path == 0:
                return remote(mine, mine, send.at[0, step], recv.at[0, step], sibling)
            return remote(mine, rows.at[1, core, source], send.at[1, step], recv.at[1, step], partner)

        self.copy = copy
        self.last = remote(rows.at[1, core], rows.at[1, core], last_send, last_recv, sibling)

    def turn(self):
        def step(number):
            self.copy(1, number).start()
            self.copy(0, number).start()

        def arrived(number):
            self.exchange.wait(number)
            step(number)

        step(0)
        each(1, self.groups, arrived)

    def own(self):
        each(0, self.groups, lambda step: self.copy(0, step).wait_recv())

    def partner(self):
        each(0, self.groups, lambda step: self.copy(1, step).wait_recv())
        self.last.start()

    def finish(self):
        self.last.wait_recv()

    def drain(self):
        def step(number):
            self.copy(0, number).wait_send()
            self.copy(1, number).wait_send()

        each(0, self.groups, step)
        self.last.wait_send()


def greet(devices):
    barrier = pltpu.get_barrier_semaphore()
    for device in devices:
        pl.semaphore_signal(barrier, inc=1, device_id=device, device_id_type=MESH)
    pl.semaphore_wait(barrier, len(devices))


def rms_of(square, width):
    return lax.rsqrt(square / width + EPS)


def kernel(
    docs, masked, pick, wt1, wt2,
    sum1, sum2,
    stage1, stage2, own1, own2, weights1, weights2,
    normed1, act1, gate1, part1, joined1, through1, summed1, landed1, out1,
    packed, cot, rows, back,
    normed2, act2, slopes2, dn_sum, dn_far, mean_out, mean_in,
    terms2, near2, via2, far2,
    upstream, terms1, through_x, summed_x, landed_x, mid, final1,
    ring_send, ring_recv, swap_send, swap_recv, share_send, share_recv, pair_send, pair_recv,
    col_send, col_recv, local_sem,
):
    level, base, core = lax.axis_index("aa"), lax.axis_index("ba"), lax.axis_index("ma")
    row, col = base // RING, lax.rem(base, RING)
    lanes, width = docs.shape
    groups = packed.shape[0]
    count = groups * packed.shape[1]
    half, quarter = width // 2, width // 4
    block, deep = weights1.shape[2], weights2.shape[2]
    hidden1, hidden2 = weights1.shape[3], weights2.shape[3]
    tile = hidden2 // 2
    mate, partner = level + 1 - 2 * lax.rem(level, 2), RING - 1 - level
    across = RING - 1 - mate
    side = level // 2
    place = (level, base, core)
    sibling = (level, base, 1 - core)
    mate_chip, partner_chip = (mate, base, core), (partner, base, core)

    loads = [
        pltpu.make_async_copy(wt1, stage1, local_sem.at[0]),
    ] + [
        pltpu.make_async_copy(
            wt2.at[m, :, pl.ds(h * hidden2, hidden2)], stage2.at[h, m], local_sem.at[1 + 2 * m + h]
        )
        for m in range(2)
        for h in range(2)
    ]
    for load in loads:
        load.start()
    greet(
        [sibling, mate_chip, partner_chip]
        + [(level, lax.rem(base + step, groups), core) for step in range(1, groups)]
    )

    loads[0].wait()
    for q in range(RING):
        for m in range(2):
            own1[q, m] = stage1[m, :, q * hidden1:(q + 1) * hidden1].astype(BF16)
    weights1[base] = own1[col]

    def along(step):
        other = wrap(col + step)
        return remote(
            own1.at[other],
            weights1.at[base],
            col_send.at[step],
            col_recv.at[step],
            (level, row * RING + other, core),
        )

    def gather_x(step, number):
        fixed = wrap(col + step)
        land = lambda pos, m: weights1.at[pos * RING + fixed, m]
        own = (lambda m: own1.at[col, m]) if step == 0 else (lambda m: land(row, m))
        device = lambda pos: (level, pos * RING + col, core)
        return Gather(own, land, row, device, ring_send.at[number], ring_recv.at[number])

    spread = [along(step) for step in (1, 3, 2)]
    gathers = [gather_x(step, k) for k, step in enumerate((0, 3, 1, 2))]
    for copy in spread:
        copy.start()
    gathers[0].start()

    rows_half = lanes // 2
    rows_part = rows_half // 2
    on_y = lambda pos: (level, row * RING + pos, core)

    def doc_part(pos, part):
        return normed1.at[pos, pl.ds(pl.multiple_of(core * rows_half + part * rows_part, rows_part), rows_part)]

    documents = Gather(
        lambda part: docs.at[pl.ds(pl.multiple_of(core * rows_half + part * rows_part, rows_part), rows_part)],
        doc_part,
        col,
        on_y,
        ring_send.at[4],
        ring_recv.at[4],
    )
    documents.start()

    def doc_pair(step):
        where = normed1.at[wrap(col + step), pl.ds(pl.multiple_of(core * rows_half, rows_half), rows_half)]
        return remote(where, where, pair_send.at[step], pair_recv.at[step], sibling)

    def down_z(m):
        return [
            remote(own2.at[1 - side, m], weights2.at[level, m], col_send.at[4 + m], col_recv.at[4 + m], partner_chip),
            remote(own2.at[side, m], weights2.at[level, m], col_send.at[6 + m], col_recv.at[6 + m], mate_chip),
            remote(weights2.at[partner, m], weights2.at[partner, m], col_send.at[8 + m], col_recv.at[8 + m], mate_chip),
        ]

    column = [down_z(m) for m in range(2)]
    for m in (1, 0):
        for h in range(2):
            loads[1 + 2 * m + h].wait()
            own2[h, m] = stage2[h, m].astype(BF16)
        column[m][0].start()
        column[m][1].start()
        weights2[level, m] = own2[side, m]

    left = pl.ds(pl.multiple_of(core * half, half), half)
    swaps = [
        Exchange(packed, land, place, swap_send.at[k], swap_recv.at[k])
        for k, land in enumerate((cot.at[0, core], rows.at[0, core], back))
    ]
    shares = [
        Share(
            swaps[k], buf, place, partner_chip, sibling,
            share_send.at[k], share_recv.at[k], pair_send.at[4 + k], pair_recv.at[4 + k],
        )
        for k, buf in enumerate((cot, rows))
    ]
    packed[...] = dot(pick[...], masked[:, left]).astype(BF16).reshape(packed.shape)
    swaps[0].start()

    for k, copy in enumerate((spread[0], spread[1], spread[2])):
        copy.wait_recv()
        gathers[1 + k].start()
    documents.forward()
    gathers[0].forward()
    documents.near()
    doc_pair(3).start()
    doc_pair(1).start()
    gathers[1].forward()
    gathers[2].forward()
    column[1][0].wait_recv()
    column[1][2].start()
    documents.far()
    doc_pair(2).start()
    gathers[3].forward()
    normed1[col] = docs[...]
    documents.drain()
    for step in (1, 2, 3):
        doc_pair(step).wait()

    def normalize_one(number):
        floated = normed1[number].astype(F32)
        square = jnp.sum(floated * floated, axis=-1, keepdims=True)
        normed1[number] = (floated * rms_of(square, width)).astype(BF16)

    each(0, RING, normalize_one)
    for gather in gathers:
        gather.near()
        gather.far()

    def matrix1(m):
        return weights1[:, m].reshape(width, hidden1)

    def give1(pos):
        return remote(
            part1.at[pos, 1 - core], joined1.at[pos], share_send.at[2, 0, pos], share_recv.at[2, 0, pos], sibling
        )

    def level_one(number):
        pos = lax.rem(col + 2 + 3 * number, RING)
        pre = dot(normed1[pos], matrix1(0))
        sigma = jax.nn.sigmoid(pre)
        active = (pre * sigma).astype(BF16)
        act1[pos] = active
        gate1[pos] = (sigma * (1.0 + pre * (1.0 - sigma))).astype(BF16)
        for h in range(2):
            piece = weights1[8 * h:8 * h + 8, 1].reshape(half, hidden1)
            part1[pos, h] = dot(active, piece, (1, 1)).astype(BF16)
        give1(pos).start()

    each(0, RING, level_one)

    def join_one(number):
        pos = lax.rem(col + 2 + 3 * number, RING)
        give1(pos).wait_recv()
        joined1[pos] = (part1[pos, core].astype(F32) + joined1[pos].astype(F32)).astype(BF16)

    each(0, RING, join_one)
    hold = lanes // 2
    reduce1 = Scatter(
        lambda pos, part: joined1.at[pos, pl.ds(part * hold, hold)],
        (through1, summed1, landed1),
        col,
        on_y,
        ring_send.at[5],
        ring_recv.at[5],
    )
    reduce1.start()
    column[0][0].wait_recv()
    column[0][2].start()
    reduce1.forward()
    shares[0].turn()
    reduce1.finish()
    for part in range(2):
        where = slice(part * hold, (part + 1) * hold)
        out1[where] = (docs[where, left].astype(F32) + reduce1.total(part)).astype(BF16)
    swaps[0].drain()
    packed[...] = dot(pick[...], out1[...]).astype(BF16).reshape(packed.shape)
    swaps[1].start()
    shares[0].own()
    shares[0].partner()

    def flat(ref, path, h):
        return ref[path, h].reshape(count, half)

    def piece2(m, h, columns):
        return weights2[2 * h:2 * h + 2, m, :, columns].reshape(half, tile)

    def columns_of(number):
        return pl.ds(pl.multiple_of(number * tile, tile), tile)

    column[1][1].wait_recv()
    column[1][2].wait_recv()
    shares[0].finish()

    def incoming_tile(number):
        path, columns = number // 2, columns_of(lax.rem(number, 2))
        value = dot(flat(cot, path, 0), piece2(1, 0, columns)) + dot(
            flat(cot, path, 1), piece2(1, 1, columns)
        )
        stage2[path, :, :, columns] = value.reshape(2, deep, tile)

    each(0, 4, incoming_tile)
    reduce1.drain()
    each(0, RING, lambda pos: give1(pos).wait_send())
    shares[1].turn()
    shares[1].own()

    def normalize_two(path):
        square = sum(
            jnp.sum(jnp.square(flat(rows, path, h).astype(F32)), axis=-1, keepdims=True) for h in range(2)
        )
        factor = rms_of(square, width)
        for h in range(2):
            normed2[path, h] = (flat(rows, path, h).astype(F32) * factor).astype(BF16)
        return factor

    def slope_tile(path):
        def step(number):
            columns = columns_of(number)
            pre = dot(normed2[path, 0], piece2(0, 0, columns)) + dot(normed2[path, 1], piece2(0, 1, columns))
            sigma = jax.nn.sigmoid(pre)
            incoming = stage2[path, :, :, columns].reshape(count, tile)
            act2[path, :, columns] = (pre * sigma).astype(BF16)
            slopes2[path, :, columns] = (incoming * sigma * (1.0 + pre * (1.0 - sigma))).astype(BF16)

        return step

    factor = normalize_two(0)
    column[0][1].wait_recv()
    column[0][2].wait_recv()
    each(0, 2, slope_tile(0))
    shares[1].partner()
    shares[1].finish()
    normalize_two(1)
    each(0, 2, slope_tile(1))

    def give2(path):
        where = pl.ds(2 * path, 2)
        return remote(
            part1.at[where, 1 - core], joined1.at[where], pair_send.at[6 + path], pair_recv.at[6 + path], sibling
        )

    def dn_tiles(path):
        def step(number):
            h = lax.rem(1 - core + number, 2)
            piece = weights2[pl.ds(2 * h, 2), 0].reshape(half, hidden2)
            value = dot(slopes2[path], piece, (1, 1)).astype(BF16)
            part1[2 * path:2 * path + 2, h] = value.reshape(2, lanes, half)

        each(0, 1, step)
        give2(path).start()
        each(1, 2, step)

    def dn_of(path):
        where = slice(2 * path, 2 * path + 2)
        return (part1[where, core].astype(F32) + joined1[where].astype(F32)).reshape(count, half)

    to_partner = remote(dn_sum, dn_far, pair_send.at[8], pair_recv.at[8], partner_chip)
    dn_tiles(1)
    give2(1).wait_recv()
    dn_sum[...] = dn_of(1).astype(BF16)
    to_partner.start()
    dn_tiles(0)

    def term_tiles(m, lefts, right):
        def step(number):
            columns = columns_of(number)
            for h in range(2):
                value = dot(lefts(0, h), right[0, :, columns], (0, 0)) + dot(
                    lefts(1, h), right[1, :, columns], (0, 0)
                )
                terms2[2 * h:2 * h + 2, m, :, columns] = value.astype(BF16).reshape(2, deep, tile)

        each(0, 2, step)

    def sums_z(m):
        return [
            remote(terms2.at[across, m], via2.at[m], col_send.at[10 + m], col_recv.at[10 + m], mate_chip),
            remote(terms2.at[mate, m], near2.at[m], col_send.at[12 + m], col_recv.at[12 + m], mate_chip),
            remote(via2.at[m], far2.at[m], col_send.at[14 + m], col_recv.at[14 + m], partner_chip),
        ]

    sums = [sums_z(m) for m in range(2)]
    term_tiles(1, lambda path, h: flat(cot, path, h), act2)
    sums[1][0].start()
    sums[1][1].start()

    give2(0).wait_recv()
    to_partner.wait_recv()

    def pieces():
        return flat(rows, 0, core).astype(F32) * factor, dn_of(0) + dn_far[...].astype(F32)

    normed, value = pieces()
    mean = jnp.sum(value * normed, axis=-1, keepdims=True)
    mean_out[...] = jnp.broadcast_to(mean, mean_out.shape)
    swap_mean = remote(mean_out, mean_in, pair_send.at[9], pair_recv.at[9], sibling)
    swap_mean.start()
    swap_mean.wait_recv()
    mean = (mean + mean_in[:, 0:1]) / width
    normed, value = pieces()
    result = flat(cot, 0, core).astype(F32) + factor * (value - normed * mean)
    swaps[1].drain()
    packed[...] = result.astype(BF16).reshape(packed.shape)
    swaps[2].start()
    term_tiles(0, lambda path, h: normed2[path, h], slopes2)
    sums[0][0].start()
    sums[0][1].start()
    sums[1][0].wait_recv()
    via2[1] = (terms2[partner, 1].astype(F32) + via2[1].astype(F32)).astype(BF16)
    sums[1][2].start()

    each(1, groups, swaps[2].wait)
    upstream[col, core] = dot(pick[...], back[...].reshape(count, half), (0, 0)).astype(BF16)
    lifts = Gather(
        lambda part: upstream.at[col, core, pl.ds(part * hold, hold)],
        lambda pos, part: upstream.at[pos, core, pl.ds(part * hold, hold)],
        col,
        on_y,
        ring_send.at[6],
        ring_recv.at[6],
    )
    lifts.start()

    def lift_pair(step):
        where = upstream.at[wrap(col + step), core]
        return remote(where, where, pair_send.at[10 + step], pair_recv.at[10 + step], sibling)

    lift_pair(0).start()
    lifts.forward()
    lifts.near()
    lift_pair(3).start()
    lift_pair(1).start()

    def slope_one(step):
        pos = wrap(col + step)
        lift_pair(step).wait_recv()
        incoming = dot(upstream[pos, 0], weights1[0:8, 1].reshape(half, hidden1)) + dot(
            upstream[pos, 1], weights1[8:16, 1].reshape(half, hidden1)
        )
        joined1[pos] = (incoming * gate1[pos].astype(F32)).astype(BF16)

    slope_one(0)
    lifts.far()
    lift_pair(2).start()
    slope_one(3)
    slope_one(1)
    slope_one(2)

    def term_one(m, lefts, right):
        for h in range(2):
            value = dot(lefts(h).reshape(RING * lanes, half), right[...].reshape(RING * lanes, hidden1), (0, 0))
            terms1[2 * h:2 * h + 2, m] = value.astype(BF16).reshape(2, RING, block, hidden1)

    def scatter_x(m):
        return Scatter(
            lambda pos, part: terms1.at[pos, m, pl.ds(2 * part, 2)],
            (through_x.at[m], summed_x.at[m], landed_x.at[m]),
            row,
            lambda pos: (level, pos * RING + col, core),
            ring_send.at[7 + m],
            ring_recv.at[7 + m],
        )

    plane = [scatter_x(m) for m in range(2)]
    term_one(1, lambda h: upstream[:, h], act1)
    plane[1].start()
    term_one(0, lambda h: normed1[:, :, h * half:(h + 1) * half], joined1)
    plane[0].start()
    plane[1].forward()
    sums[0][0].wait_recv()
    via2[0] = (terms2[partner, 0].astype(F32) + via2[0].astype(F32)).astype(BF16)
    sums[0][2].start()
    plane[0].forward()

    def along_back(step):
        other = wrap(col + step)
        return remote(
            mid.at[other], final1.at[col], col_send.at[16 + step], col_recv.at[16 + step],
            (level, row * RING + other, core),
        )

    for m in (1, 0):
        plane[m].finish()
        for part in range(2):
            mid[2 * part:2 * part + 2, m] = plane[m].total(part).astype(BF16)
    for step in (2, 1, 3):
        along_back(step).start()
    final1[col] = mid[col]
    own_side = pl.ds(pl.multiple_of(side * hidden2, hidden2), hidden2)
    other_side = pl.ds(pl.multiple_of((1 - side) * hidden2, hidden2), hidden2)
    for m in (1, 0):
        sums[m][1].wait_recv()
        sum2[m, :, own_side] = (terms2[level, m].astype(F32) + near2[m].astype(F32)).astype(BF16)
        sums[m][2].wait_recv()
        sum2[m, :, other_side] = far2[m]
    for step in (1, 3, 2):
        along_back(step).wait_recv()
    for q in range(RING):
        sum1[:, :, q * hidden1:(q + 1) * hidden1] = final1[q]

    for copy in spread + column[0] + column[1] + sums[0] + sums[1]:
        copy.wait_send()
    for ring in gathers + [lifts] + plane + [swaps[2]] + shares:
        ring.drain()
    for step in range(RING):
        lift_pair(step).wait_send()
    for step in (1, 2, 3):
        along_back(step).wait_send()
    give2(0).wait_send()
    give2(1).wait_send()
    to_partner.wait_send()
    swap_mean.wait_send()


def outer_step(weights, moment, delta):
    new_moment = MOMENTUM * moment + delta[None]
    return (weights - OUTER_RATE * (delta[None] + MOMENTUM * new_moment), new_moment)


def local(docs, cot, route, doc_len, wt1, mom1, wt2, mom2):
    blocks, block, width = docs.shape
    groups = lax.axis_size("ba")
    levels = lax.axis_size("aa")
    slots = groups * SLOT
    count, lanes = slots * block, blocks * block
    hidden = wt1.shape[-1]
    inside = lax.broadcasted_iota(jnp.int32, (blocks, block), 1) < doc_len[:, None]
    masked = jnp.where(inside[:, :, None], cot, jnp.zeros_like(cot)).reshape(lanes, width)
    targets = route[:, 0]
    shared = targets[:, None] == targets[None, :]
    before = lax.broadcasted_iota(jnp.int32, (blocks, blocks), 0) > lax.broadcasted_iota(
        jnp.int32, (blocks, blocks), 1
    )
    rank = jnp.sum((shared & before).astype(jnp.int32), axis=1)
    target_row = (targets * SLOT + rank)[:, None] * block + jnp.arange(block, dtype=jnp.int32)[None]
    pick = (
        lax.broadcasted_iota(jnp.int32, (count, lanes), 0) == target_row.reshape(1, lanes)
    ).astype(BF16)
    rows = docs.reshape(lanes, width)

    whole = pl.BlockSpec(memory_space=pltpu.VMEM)
    anywhere = pl.BlockSpec(memory_space=pl.ANY)
    half, quarter = width // 2, width // 4
    per = count // groups
    small = width // 16
    hidden1, hidden2 = hidden // RING, hidden // 2

    def vmem(*sizes, kind=BF16):
        return pltpu.VMEM(sizes, kind)

    def dma(*sizes):
        return pltpu.SemaphoreType.DMA(sizes)

    hold = lanes // 2
    sum1, sum2 = pl.pallas_call(
        kernel,
        out_shape=(
            jax.ShapeDtypeStruct((2, small, hidden), BF16),
            jax.ShapeDtypeStruct((2, quarter, hidden), BF16),
        ),
        in_specs=[whole, whole, whole, anywhere, anywhere],
        out_specs=[whole, whole],
        scratch_shapes=[
            vmem(2, small, hidden, kind=F32),
            vmem(2, 2, quarter, hidden2, kind=F32),
            vmem(RING, 2, small, hidden1),
            vmem(2, 2, quarter, hidden2),
            vmem(16, 2, small, hidden1),
            vmem(RING, 2, quarter, hidden2),
            vmem(RING, lanes, width),
            vmem(RING, lanes, hidden1),
            vmem(RING, lanes, hidden1),
            vmem(RING, 2, lanes, half),
            vmem(RING, lanes, half),
            vmem(2, hold, half),
            vmem(2, hold, half),
            vmem(4, hold, half),
            vmem(lanes, half),
            vmem(groups, per, half),
            vmem(2, 2, groups, per, half),
            vmem(2, 2, groups, per, half),
            vmem(groups, per, half),
            vmem(2, 2, count, half),
            vmem(2, count, hidden2),
            vmem(2, count, hidden2),
            vmem(count, half),
            vmem(count, half),
            vmem(count, 128, kind=F32),
            vmem(count, 128, kind=F32),
            vmem(RING, 2, quarter, hidden2),
            vmem(2, quarter, hidden2),
            vmem(2, quarter, hidden2),
            vmem(2, quarter, hidden2),
            vmem(RING, 2, lanes, half),
            vmem(RING, 2, RING, small, hidden1),
            vmem(2, 2, 2, small, hidden1),
            vmem(2, 2, 2, small, hidden1),
            vmem(2, 4, 2, small, hidden1),
            vmem(RING, 2, small, hidden1),
            vmem(RING, 2, small, hidden1),
            dma(9, 6),
            dma(9, 6),
            dma(3, groups),
            dma(3, groups),
            dma(3, 2, groups),
            dma(3, 2, groups),
            dma(14),
            dma(14),
            dma(20),
            dma(20),
            dma(5),
        ],
        compiler_params=pltpu.CompilerParams(
            collective_id=0, has_side_effects=True, vmem_limit_bytes=VMEM_LIMIT
        ),
        name="window",
    )(rows, masked, pick, wt1[0], wt2[0])

    delta1 = sum1.astype(F32) / groups
    delta2 = sum2.astype(F32) / levels
    new_wt1, new_mom1 = outer_step(wt1, mom1, delta1)
    new_wt2, new_mom2 = outer_step(wt2, mom2, delta2)
    return (new_wt1, new_mom1, new_wt2, new_mom2)


def solution(mesh):
    return jax.shard_map(
        local,
        mesh=mesh,
        in_specs=(
            P(("aa", "ba"), None, None),
            P(("aa", "ba"), None, None),
            P(("aa", "ba"), None),
            P(("aa", "ba")),
            P("aa", None, "ba", "ma"),
            P("aa", None, "ba", "ma"),
            P("ba", None, "aa", "ma"),
            P("ba", None, "aa", "ma"),
        ),
        out_specs=(
            P("aa", None, "ba", "ma"),
            P("aa", None, "ba", "ma"),
            P("ba", None, "aa", "ma"),
            P("ba", None, "aa", "ma"),
        ),
        check_vma=False,
    )
```

```python
import jax
import jax.numpy as jnp
from jax import lax
from jax.experimental import pallas as pl
from jax.experimental.pallas import tpu as pltpu
from jax.sharding import PartitionSpec as P

SLOT = 2
EPS = 1e-05
MOMENTUM = 0.9
OUTER_RATE = 0.7

MESH = pl.DeviceIdType.MESH
BF16 = jnp.bfloat16
F32 = jnp.float32
RING = 4
VMEM_LIMIT = 57 * 1024 * 1024


def dot(left, right, contract=(1, 0)):
    return lax.dot_general(
        left,
        right,
        (((contract[0],), (contract[1],)), ((), ())),
        preferred_element_type=F32,
    )


def wrap(index, size=RING):
    return lax.rem(index + size, size)


def remote(source, target, send, recv, device):
    return pltpu.make_async_remote_copy(
        src_ref=source,
        dst_ref=target,
        send_sem=send,
        recv_sem=recv,
        device_id=device,
        device_id_type=MESH,
    )


def each(first, last, step):
    def body(number, carry):
        step(number)
        return carry

    lax.fori_loop(first, last, body, 0)


class Gather:
    def __init__(self, own, land, rank, device, send, recv):
        up, down = wrap(rank + 1), wrap(rank - 1)

        def copy(number, source, target, to):
            return remote(source, target, send.at[number], recv.at[number], device(to))

        self.direct = [
            copy(0, own(0), land(rank, 0), up),
            copy(1, own(1), land(rank, 1), down),
            copy(2, own(1), land(rank, 1), up),
            copy(3, own(0), land(rank, 0), down),
        ]
        self.passed = [
            copy(4, land(down, 0), land(down, 0), up),
            copy(5, land(up, 1), land(up, 1), down),
        ]

    def start(self):
        for copy in self.direct:
            copy.start()

    def forward(self):
        for near, far in zip(self.direct[:2], self.passed):
            near.wait_recv()
            far.start()

    def near(self):
        for copy in self.direct[2:]:
            copy.wait_recv()

    def far(self):
        for copy in self.passed:
            copy.wait_recv()

    def drain(self):
        for copy in self.direct + self.passed:
            copy.wait_send()


class Scatter:
    def __init__(self, own, bufs, rank, device, send, recv):
        up, down, far = wrap(rank + 1), wrap(rank - 1), wrap(rank + 2)
        through, summed, landed = bufs

        def copy(number, source, target, to):
            return remote(source, target, send.at[number], recv.at[number], device(to))

        self.first = [
            copy(0, own(far, 0), through.at[0], up),
            copy(1, own(far, 1), through.at[1], down),
            copy(2, own(up, 1), landed.at[1], up),
            copy(3, own(down, 0), landed.at[2], down),
        ]
        self.second = [
            copy(4, summed.at[0], landed.at[0], up),
            copy(5, summed.at[1], landed.at[3], down),
        ]
        self.through, self.summed, self.landed = through, summed, landed
        self.own, self.rank = own, rank

    def start(self):
        for copy in self.first:
            copy.start()

    def forward(self):
        for which in range(2):
            self.first[which].wait_recv()
            mine = self.own(wrap(self.rank + 1 - 2 * which), which)[...]
            total = mine.astype(F32) + self.through[which].astype(F32)
            self.summed[which] = total.astype(BF16)
            self.second[which].start()

    def finish(self):
        for copy in self.first[2:] + self.second:
            copy.wait_recv()

    def total(self, half):
        return self.own(self.rank, half)[...].astype(F32) + (
            self.landed[half].astype(F32) + self.landed[2 + half].astype(F32)
        )

    def drain(self):
        for copy in self.first + self.second:
            copy.wait_send()


class Exchange:
    def __init__(self, packed, land, place, send, recv):
        self.place, self.groups = place, packed.shape[0]
        self.packed, self.land, self.send, self.recv = packed, land, send, recv

    def copy(self, step):
        level, base, core = self.place
        target = lax.rem(base + step, self.groups)
        return remote(
            self.packed.at[target],
            self.land.at[base],
            self.send.at[step],
            self.recv.at[step],
            (level, target, core),
        )

    def start(self):
        each(1, self.groups, lambda step: self.copy(step).start())
        base = self.place[1]
        self.land[base] = self.packed[base]

    def wait(self, step):
        self.copy(step).wait_recv()

    def drain(self):
        each(1, self.groups, lambda step: self.copy(step).wait_send())


class Share:
    def __init__(self, exchange, rows, place, partner, sibling, send, recv, last_send, last_recv):
        core = place[2]
        self.exchange, self.groups = exchange, exchange.groups

        def copy(path, step):
            source = wrap(place[1] - step, self.groups)
            mine = rows.at[0, core, source]
            if path == 0:
                return remote(mine, mine, send.at[0, step], recv.at[0, step], sibling)
            return remote(mine, rows.at[1, core, source], send.at[1, step], recv.at[1, step], partner)

        self.copy = copy
        self.last = remote(rows.at[1, core], rows.at[1, core], last_send, last_recv, sibling)

    def turn(self):
        def step(number):
            self.copy(1, number).start()
            self.copy(0, number).start()

        def arrived(number):
            self.exchange.wait(number)
            step(number)

        step(0)
        each(1, self.groups, arrived)

    def own(self):
        each(0, self.groups, lambda step: self.copy(0, step).wait_recv())

    def partner(self):
        each(0, self.groups, lambda step: self.copy(1, step).wait_recv())
        self.last.start()

    def finish(self):
        self.last.wait_recv()

    def drain(self):
        def step(number):
            self.copy(0, number).wait_send()
            self.copy(1, number).wait_send()

        each(0, self.groups, step)
        self.last.wait_send()


def greet(devices):
    barrier = pltpu.get_barrier_semaphore()
    for device in devices:
        pl.semaphore_signal(barrier, inc=1, device_id=device, device_id_type=MESH)
    pl.semaphore_wait(barrier, len(devices))


def doc_of_row(lanes, docs):
    row = lax.broadcasted_iota(jnp.int32, (lanes, docs), 0) // (lanes // docs)
    return (row == lax.broadcasted_iota(jnp.int32, (lanes, docs), 1)).astype(F32)


def slot_matrix(route, pick):
    count, lanes = pick.shape
    docs = route.shape[0]
    block = lanes // docs
    target = route[...].astype(F32)
    spread = jnp.broadcast_to(target, (docs, 128))
    by_row = dot(spread, doc_of_row(lanes, docs), (0, 1))[0:docs]
    own = lax.broadcasted_iota(jnp.int32, (docs, lanes), 1)
    earlier = lax.broadcasted_iota(jnp.int32, (docs, lanes), 0) < own // block
    rank = jnp.sum(jnp.where((by_row == target) & earlier, 1.0, 0.0), axis=0, keepdims=True)
    place = (by_row[0:1] * SLOT + rank) * block + lax.rem(own[0:1], block).astype(F32)
    slots = lax.broadcasted_iota(jnp.int32, (count, lanes), 0).astype(F32)
    pick[...] = jnp.where(slots == place, 1.0, 0.0).astype(BF16)


def live_rows(doc_len, lanes):
    docs = doc_len.shape[1]
    lengths = jnp.broadcast_to(doc_len[...].astype(F32), (128, docs))
    lengths = dot(doc_of_row(lanes, docs), lengths, (1, 1))[:, 0:1]
    position = lax.rem(lax.broadcasted_iota(jnp.int32, (lanes, 1), 0), lanes // docs)
    return position.astype(F32) < lengths


def rms_of(square, width):
    return lax.rsqrt(square / width + EPS)


def kernel(
    docs, cot_docs, route, doc_len, wt1, wt2,
    sum1, sum2,
    pick,
    stage1, stage2, own1, own2, weights1, weights2,
    normed1, act1, gate1, part1, joined1, through1, summed1, landed1, out1,
    packed, cot, rows, back,
    normed2, act2, slopes2, dn_sum, dn_far, mean_out, mean_in,
    terms2, near2, via2, far2,
    upstream, terms1, through_x, summed_x, landed_x, mid, final1,
    ring_send, ring_recv, swap_send, swap_recv, share_send, share_recv, pair_send, pair_recv,
    col_send, col_recv, local_sem,
):
    level, base, core = lax.axis_index("aa"), lax.axis_index("ba"), lax.axis_index("ma")
    row, col = base // RING, lax.rem(base, RING)
    lanes, width = docs.shape
    groups = packed.shape[0]
    count = groups * packed.shape[1]
    half, quarter = width // 2, width // 4
    block, deep = weights1.shape[2], weights2.shape[2]
    hidden1, hidden2 = weights1.shape[3], weights2.shape[3]
    tile = hidden2 // 2
    mate, partner = level + 1 - 2 * lax.rem(level, 2), RING - 1 - level
    across = RING - 1 - mate
    side = level // 2
    place = (level, base, core)
    sibling = (level, base, 1 - core)
    mate_chip, partner_chip = (mate, base, core), (partner, base, core)

    loads = [
        pltpu.make_async_copy(wt1, stage1, local_sem.at[0]),
    ] + [
        pltpu.make_async_copy(
            wt2.at[m, :, pl.ds(h * hidden2, hidden2)], stage2.at[h, m], local_sem.at[1 + 2 * m + h]
        )
        for m in range(2)
        for h in range(2)
    ]
    for load in loads:
        load.start()
    greet(
        [sibling, mate_chip, partner_chip]
        + [(level, lax.rem(base + step, groups), core) for step in range(1, groups)]
    )

    loads[0].wait()
    for q in range(RING):
        for m in range(2):
            own1[q, m] = stage1[m, :, q * hidden1:(q + 1) * hidden1].astype(BF16)
    weights1[base] = own1[col]

    def along(step):
        other = wrap(col + step)
        return remote(
            own1.at[other],
            weights1.at[base],
            col_send.at[step],
            col_recv.at[step],
            (level, row * RING + other, core),
        )

    def gather_x(step, number):
        fixed = wrap(col + step)
        land = lambda pos, m: weights1.at[pos * RING + fixed, m]
        own = (lambda m: own1.at[col, m]) if step == 0 else (lambda m: land(row, m))
        device = lambda pos: (level, pos * RING + col, core)
        return Gather(own, land, row, device, ring_send.at[number], ring_recv.at[number])

    spread = [along(step) for step in (1, 3, 2)]
    gathers = [gather_x(step, k) for k, step in enumerate((0, 3, 1, 2))]
    for copy in spread:
        copy.start()
    gathers[0].start()

    rows_half = lanes // 2
    rows_part = rows_half // 2
    on_y = lambda pos: (level, row * RING + pos, core)

    def doc_part(pos, part):
        return normed1.at[pos, pl.ds(pl.multiple_of(core * rows_half + part * rows_part, rows_part), rows_part)]

    documents = Gather(
        lambda part: docs.at[pl.ds(pl.multiple_of(core * rows_half + part * rows_part, rows_part), rows_part)],
        doc_part,
        col,
        on_y,
        ring_send.at[4],
        ring_recv.at[4],
    )
    def doc_pair(step):
        where = normed1.at[wrap(col + step), pl.ds(pl.multiple_of(core * rows_half, rows_half), rows_half)]
        return remote(where, where, pair_send.at[step], pair_recv.at[step], sibling)

    def down_z(m):
        return [
            remote(own2.at[1 - side, m], weights2.at[level, m], col_send.at[4 + m], col_recv.at[4 + m], partner_chip),
            remote(own2.at[side, m], weights2.at[level, m], col_send.at[6 + m], col_recv.at[6 + m], mate_chip),
            remote(weights2.at[partner, m], weights2.at[partner, m], col_send.at[8 + m], col_recv.at[8 + m], mate_chip),
        ]

    column = [down_z(m) for m in range(2)]
    for m in (1, 0):
        for h in range(2):
            loads[1 + 2 * m + h].wait()
            own2[h, m] = stage2[h, m].astype(BF16)
        column[m][0].start()
        column[m][1].start()
        weights2[level, m] = own2[side, m]

    left = pl.ds(pl.multiple_of(core * half, half), half)
    swaps = [
        Exchange(packed, land, place, swap_send.at[k], swap_recv.at[k])
        for k, land in enumerate((cot.at[0, core], rows.at[0, core], back))
    ]
    shares = [
        Share(
            swaps[k], buf, place, partner_chip, sibling,
            share_send.at[k], share_recv.at[k], pair_send.at[4 + k], pair_recv.at[4 + k],
        )
        for k, buf in enumerate((cot, rows))
    ]
    slot_matrix(route, pick)
    live = live_rows(doc_len, lanes)
    masked = jnp.where(live, cot_docs[:, left], jnp.zeros((lanes, half), BF16))
    packed[...] = dot(pick[...], masked).astype(BF16).reshape(packed.shape)

    for k, copy in enumerate((spread[0], spread[1], spread[2])):
        copy.wait_recv()
        gathers[1 + k].start()
    documents.start()
    for gather in gathers[:3]:
        gather.forward()
    column[1][0].wait_recv()
    column[1][2].start()
    gathers[3].forward()
    documents.forward()
    documents.near()
    doc_pair(3).start()
    doc_pair(1).start()
    documents.far()
    doc_pair(2).start()
    normed1[col] = docs[...]
    documents.drain()
    for step in (1, 2, 3):
        doc_pair(step).wait()

    def normalize_one(number):
        floated = normed1[number].astype(F32)
        square = jnp.sum(floated * floated, axis=-1, keepdims=True)
        normed1[number] = (floated * rms_of(square, width)).astype(BF16)

    each(0, RING, normalize_one)
    for gather in gathers:
        gather.near()
        gather.far()
    swaps[0].start()

    def matrix1(m):
        return weights1[:, m].reshape(width, hidden1)

    def give1(pos):
        return remote(
            part1.at[pos, 1 - core], joined1.at[pos], share_send.at[2, 0, pos], share_recv.at[2, 0, pos], sibling
        )

    def level_one(number):
        pos = lax.rem(col + 2 + 3 * number, RING)
        pre = dot(normed1[pos], matrix1(0))
        sigma = jax.nn.sigmoid(pre)
        active = (pre * sigma).astype(BF16)
        act1[pos] = active
        gate1[pos] = (sigma * (1.0 + pre * (1.0 - sigma))).astype(BF16)
        for h in range(2):
            piece = weights1[8 * h:8 * h + 8, 1].reshape(half, hidden1)
            part1[pos, h] = dot(active, piece, (1, 1)).astype(BF16)
        give1(pos).start()

    each(0, RING, level_one)

    def join_one(number):
        pos = lax.rem(col + 2 + 3 * number, RING)
        give1(pos).wait_recv()
        joined1[pos] = (part1[pos, core].astype(F32) + joined1[pos].astype(F32)).astype(BF16)

    each(0, RING, join_one)
    hold = lanes // 2
    reduce1 = Scatter(
        lambda pos, part: joined1.at[pos, pl.ds(part * hold, hold)],
        (through1, summed1, landed1),
        col,
        on_y,
        ring_send.at[5],
        ring_recv.at[5],
    )
    reduce1.start()
    column[0][0].wait_recv()
    column[0][2].start()
    reduce1.forward()
    shares[0].turn()
    reduce1.finish()
    for part in range(2):
        where = slice(part * hold, (part + 1) * hold)
        out1[where] = (docs[where, left].astype(F32) + reduce1.total(part)).astype(BF16)
    swaps[0].drain()
    packed[...] = dot(pick[...], out1[...]).astype(BF16).reshape(packed.shape)
    swaps[1].start()
    shares[0].own()

    def flat(ref, path, h):
        return ref[path, h].reshape(count, half)

    def piece2(m, h, columns):
        return weights2[2 * h:2 * h + 2, m, :, columns].reshape(half, tile)

    def columns_of(number):
        return pl.ds(pl.multiple_of(number * tile, tile), tile)

    column[1][1].wait_recv()
    column[1][2].wait_recv()

    def incoming_tile(number):
        path, columns = number // 2, columns_of(lax.rem(number, 2))
        value = dot(flat(cot, path, 0), piece2(1, 0, columns)) + dot(
            flat(cot, path, 1), piece2(1, 1, columns)
        )
        stage2[path, :, :, columns] = value.reshape(2, deep, tile)

    each(0, 2, incoming_tile)
    reduce1.drain()
    each(0, RING, lambda pos: give1(pos).wait_send())
    shares[1].turn()
    shares[0].partner()
    shares[1].own()

    def normalize_two(path):
        square = sum(
            jnp.sum(jnp.square(flat(rows, path, h).astype(F32)), axis=-1, keepdims=True) for h in range(2)
        )
        factor = rms_of(square, width)
        for h in range(2):
            normed2[path, h] = (flat(rows, path, h).astype(F32) * factor).astype(BF16)
        return factor

    def slope_tile(path):
        def step(number):
            columns = columns_of(number)
            pre = dot(normed2[path, 0], piece2(0, 0, columns)) + dot(normed2[path, 1], piece2(0, 1, columns))
            sigma = jax.nn.sigmoid(pre)
            incoming = stage2[path, :, :, columns].reshape(count, tile)
            act2[path, :, columns] = (pre * sigma).astype(BF16)
            slopes2[path, :, columns] = (incoming * sigma * (1.0 + pre * (1.0 - sigma))).astype(BF16)

        return step

    factor = normalize_two(0)
    column[0][1].wait_recv()
    column[0][2].wait_recv()
    each(0, 2, slope_tile(0))
    shares[1].partner()
    shares[0].finish()
    each(2, 4, incoming_tile)
    shares[1].finish()
    normalize_two(1)
    each(0, 2, slope_tile(1))

    def give2(path):
        where = pl.ds(2 * path, 2)
        return remote(
            part1.at[where, 1 - core], joined1.at[where], pair_send.at[6 + path], pair_recv.at[6 + path], sibling
        )

    def dn_tiles(path):
        def step(number):
            h = lax.rem(1 - core + number, 2)
            piece = weights2[pl.ds(2 * h, 2), 0].reshape(half, hidden2)
            value = dot(slopes2[path], piece, (1, 1)).astype(BF16)
            part1[2 * path:2 * path + 2, h] = value.reshape(2, lanes, half)

        each(0, 1, step)
        give2(path).start()
        each(1, 2, step)

    def dn_of(path):
        where = slice(2 * path, 2 * path + 2)
        return (part1[where, core].astype(F32) + joined1[where].astype(F32)).reshape(count, half)

    to_partner = remote(dn_sum, dn_far, pair_send.at[8], pair_recv.at[8], partner_chip)
    dn_tiles(1)
    give2(1).wait_recv()
    dn_sum[...] = dn_of(1).astype(BF16)
    to_partner.start()
    dn_tiles(0)

    def term_tiles(m, lefts, right):
        def step(number):
            columns = columns_of(number)
            for h in range(2):
                value = dot(lefts(0, h), right[0, :, columns], (0, 0)) + dot(
                    lefts(1, h), right[1, :, columns], (0, 0)
                )
                terms2[2 * h:2 * h + 2, m, :, columns] = value.astype(BF16).reshape(2, deep, tile)

        each(0, 2, step)

    def sums_z(m):
        return [
            remote(terms2.at[across, m], via2.at[m], col_send.at[10 + m], col_recv.at[10 + m], mate_chip),
            remote(terms2.at[mate, m], near2.at[m], col_send.at[12 + m], col_recv.at[12 + m], mate_chip),
            remote(via2.at[m], far2.at[m], col_send.at[14 + m], col_recv.at[14 + m], partner_chip),
        ]

    sums = [sums_z(m) for m in range(2)]
    term_tiles(1, lambda path, h: flat(cot, path, h), act2)
    sums[1][0].start()
    sums[1][1].start()

    give2(0).wait_recv()
    to_partner.wait_recv()

    def pieces():
        return flat(rows, 0, core).astype(F32) * factor, dn_of(0) + dn_far[...].astype(F32)

    normed, value = pieces()
    mean = jnp.sum(value * normed, axis=-1, keepdims=True)
    mean_out[...] = jnp.broadcast_to(mean, mean_out.shape)
    swap_mean = remote(mean_out, mean_in, pair_send.at[9], pair_recv.at[9], sibling)
    swap_mean.start()
    swap_mean.wait_recv()
    mean = (mean + mean_in[:, 0:1]) / width
    normed, value = pieces()
    result = flat(cot, 0, core).astype(F32) + factor * (value - normed * mean)
    swaps[1].drain()
    packed[...] = result.astype(BF16).reshape(packed.shape)
    swaps[2].start()
    term_tiles(0, lambda path, h: normed2[path, h], slopes2)
    sums[0][0].start()
    sums[0][1].start()
    sums[1][0].wait_recv()
    via2[1] = (terms2[partner, 1].astype(F32) + via2[1].astype(F32)).astype(BF16)
    sums[1][2].start()

    each(1, groups, swaps[2].wait)
    upstream[col, core] = dot(pick[...], back[...].reshape(count, half), (0, 0)).astype(BF16)
    lifts = Gather(
        lambda part: upstream.at[col, core, pl.ds(part * hold, hold)],
        lambda pos, part: upstream.at[pos, core, pl.ds(part * hold, hold)],
        col,
        on_y,
        ring_send.at[6],
        ring_recv.at[6],
    )
    lifts.start()

    def lift_pair(step):
        where = upstream.at[wrap(col + step), core]
        return remote(where, where, pair_send.at[10 + step], pair_recv.at[10 + step], sibling)

    lift_pair(0).start()
    lifts.forward()
    lifts.near()
    lift_pair(3).start()
    lift_pair(1).start()

    def slope_one(step):
        pos = wrap(col + step)
        lift_pair(step).wait_recv()
        incoming = dot(upstream[pos, 0], weights1[0:8, 1].reshape(half, hidden1)) + dot(
            upstream[pos, 1], weights1[8:16, 1].reshape(half, hidden1)
        )
        joined1[pos] = (incoming * gate1[pos].astype(F32)).astype(BF16)

    slope_one(0)
    lifts.far()
    lift_pair(2).start()
    slope_one(3)
    slope_one(1)
    slope_one(2)

    def term_one(m, lefts, right):
        for h in range(2):
            value = dot(lefts(h).reshape(RING * lanes, half), right[...].reshape(RING * lanes, hidden1), (0, 0))
            terms1[2 * h:2 * h + 2, m] = value.astype(BF16).reshape(2, RING, block, hidden1)

    def scatter_x(m):
        return Scatter(
            lambda pos, part: terms1.at[pos, m, pl.ds(2 * part, 2)],
            (through_x.at[m], summed_x.at[m], landed_x.at[m]),
            row,
            lambda pos: (level, pos * RING + col, core),
            ring_send.at[7 + m],
            ring_recv.at[7 + m],
        )

    plane = [scatter_x(m) for m in range(2)]
    term_one(1, lambda h: upstream[:, h], act1)
    plane[1].start()
    term_one(0, lambda h: normed1[:, :, h * half:(h + 1) * half], joined1)
    plane[0].start()
    plane[1].forward()
    sums[0][0].wait_recv()
    via2[0] = (terms2[partner, 0].astype(F32) + via2[0].astype(F32)).astype(BF16)
    sums[0][2].start()
    plane[0].forward()

    def along_back(step, m):
        other = wrap(col + step)
        number = 16 + 4 * m + step
        return remote(
            mid.at[m, other], final1.at[m, col], col_send.at[number], col_recv.at[number],
            (level, row * RING + other, core),
        )

    for m in (1, 0):
        plane[m].finish()
        for part in range(2):
            mid[m, 2 * part:2 * part + 2] = plane[m].total(part).astype(BF16)
        for step in (2, 1, 3):
            along_back(step, m).start()
        final1[m, col] = mid[m, col]
    own_side = pl.ds(pl.multiple_of(side * hidden2, hidden2), hidden2)
    other_side = pl.ds(pl.multiple_of((1 - side) * hidden2, hidden2), hidden2)
    for m in (1, 0):
        sums[m][1].wait_recv()
        sum2[m, :, own_side] = (terms2[level, m].astype(F32) + near2[m].astype(F32)).astype(BF16)
        sums[m][2].wait_recv()
        sum2[m, :, other_side] = far2[m]
    for m in (1, 0):
        for step in (1, 3, 2):
            along_back(step, m).wait_recv()
        for q in range(RING):
            sum1[m, :, q * hidden1:(q + 1) * hidden1] = final1[m, q]

    for copy in spread + column[0] + column[1] + sums[0] + sums[1]:
        copy.wait_send()
    for ring in gathers + [lifts] + plane + [swaps[2]] + shares:
        ring.drain()
    for step in range(RING):
        lift_pair(step).wait_send()
    for step in (1, 2, 3):
        along_back(step, 0).wait_send()
        along_back(step, 1).wait_send()
    give2(0).wait_send()
    give2(1).wait_send()
    to_partner.wait_send()
    swap_mean.wait_send()


def outer_step(weights, moment, delta):
    new_moment = MOMENTUM * moment + delta[None]
    return (weights - OUTER_RATE * (delta[None] + MOMENTUM * new_moment), new_moment)


def local(docs, cot, route, doc_len, wt1, mom1, wt2, mom2):
    blocks, block, width = docs.shape
    groups = lax.axis_size("ba")
    levels = lax.axis_size("aa")
    slots = groups * SLOT
    count, lanes = slots * block, blocks * block
    hidden = wt1.shape[-1]
    whole = pl.BlockSpec(memory_space=pltpu.VMEM)
    anywhere = pl.BlockSpec(memory_space=pl.ANY)
    half, quarter = width // 2, width // 4
    per = count // groups
    small = width // 16
    hidden1, hidden2 = hidden // RING, hidden // 2

    def vmem(*sizes, kind=BF16):
        return pltpu.VMEM(sizes, kind)

    def dma(*sizes):
        return pltpu.SemaphoreType.DMA(sizes)

    hold = lanes // 2
    sum1, sum2 = pl.pallas_call(
        kernel,
        out_shape=(
            jax.ShapeDtypeStruct((2, small, hidden), BF16),
            jax.ShapeDtypeStruct((2, quarter, hidden), BF16),
        ),
        in_specs=[whole, whole, whole, whole, anywhere, anywhere],
        out_specs=[whole, whole],
        scratch_shapes=[
            vmem(count, lanes),
            vmem(2, small, hidden, kind=F32),
            vmem(2, 2, quarter, hidden2, kind=F32),
            vmem(RING, 2, small, hidden1),
            vmem(2, 2, quarter, hidden2),
            vmem(16, 2, small, hidden1),
            vmem(RING, 2, quarter, hidden2),
            vmem(RING, lanes, width),
            vmem(RING, lanes, hidden1),
            vmem(RING, lanes, hidden1),
            vmem(RING, 2, lanes, half),
            vmem(RING, lanes, half),
            vmem(2, hold, half),
            vmem(2, hold, half),
            vmem(4, hold, half),
            vmem(lanes, half),
            vmem(groups, per, half),
            vmem(2, 2, groups, per, half),
            vmem(2, 2, groups, per, half),
            vmem(groups, per, half),
            vmem(2, 2, count, half),
            vmem(2, count, hidden2),
            vmem(2, count, hidden2),
            vmem(count, half),
            vmem(count, half),
            vmem(count, 128, kind=F32),
            vmem(count, 128, kind=F32),
            vmem(RING, 2, quarter, hidden2),
            vmem(2, quarter, hidden2),
            vmem(2, quarter, hidden2),
            vmem(2, quarter, hidden2),
            vmem(RING, 2, lanes, half),
            vmem(RING, 2, RING, small, hidden1),
            vmem(2, 2, 2, small, hidden1),
            vmem(2, 2, 2, small, hidden1),
            vmem(2, 4, 2, small, hidden1),
            vmem(2, RING, small, hidden1),
            vmem(2, RING, small, hidden1),
            dma(9, 6),
            dma(9, 6),
            dma(3, groups),
            dma(3, groups),
            dma(3, 2, groups),
            dma(3, 2, groups),
            dma(14),
            dma(14),
            dma(24),
            dma(24),
            dma(5),
        ],
        compiler_params=pltpu.CompilerParams(
            collective_id=0, has_side_effects=True, vmem_limit_bytes=VMEM_LIMIT
        ),
        name="window",
    )(docs.reshape(lanes, width), cot.reshape(lanes, width), route, doc_len[None], wt1[0], wt2[0])

    delta1 = sum1.astype(F32) / groups
    delta2 = sum2.astype(F32) / levels
    new_wt1, new_mom1 = outer_step(wt1, mom1, delta1)
    new_wt2, new_mom2 = outer_step(wt2, mom2, delta2)
    return (new_wt1, new_mom1, new_wt2, new_mom2)


def solution(mesh):
    return jax.shard_map(
        local,
        mesh=mesh,
        in_specs=(
            P(("aa", "ba"), None, None),
            P(("aa", "ba"), None, None),
            P(("aa", "ba"), None),
            P(("aa", "ba")),
            P("aa", None, "ba", "ma"),
            P("aa", None, "ba", "ma"),
            P("ba", None, "aa", "ma"),
            P("ba", None, "aa", "ma"),
        ),
        out_specs=(
            P("aa", None, "ba", "ma"),
            P("aa", None, "ba", "ma"),
            P("ba", None, "aa", "ma"),
            P("ba", None, "aa", "ma"),
        ),
        check_vma=False,
    )
```

```python
import jax
import jax.numpy as jnp
from jax import lax
from jax.experimental import pallas as pl
from jax.experimental.pallas import tpu as pltpu
from jax.sharding import PartitionSpec as P

SLOT = 2
EPS = 1e-05
MOMENTUM = 0.9
OUTER_RATE = 0.7

MESH = pl.DeviceIdType.MESH
BF16 = jnp.bfloat16
F32 = jnp.float32
RING = 4
VMEM_LIMIT = 50 * 1024 * 1024


def dot(left, right, contract=(1, 0)):
    return lax.dot_general(
        left,
        right,
        (((contract[0],), (contract[1],)), ((), ())),
        preferred_element_type=F32,
    )


def wrap(index, size=RING):
    return lax.rem(index + size, size)


def remote(source, target, send, recv, device):
    return pltpu.make_async_remote_copy(
        src_ref=source,
        dst_ref=target,
        send_sem=send,
        recv_sem=recv,
        device_id=device,
        device_id_type=MESH,
    )


def each(first, last, step):
    def body(number, carry):
        step(number)
        return carry

    lax.fori_loop(first, last, body, 0)


class Gather:
    def __init__(self, own, land, rank, device, send, recv):
        up, down = wrap(rank + 1), wrap(rank - 1)

        def copy(number, source, target, to):
            return remote(source, target, send.at[number], recv.at[number], device(to))

        self.direct = [
            copy(0, own(0), land(rank, 0), up),
            copy(1, own(1), land(rank, 1), down),
            copy(2, own(1), land(rank, 1), up),
            copy(3, own(0), land(rank, 0), down),
        ]
        self.passed = [
            copy(4, land(down, 0), land(down, 0), up),
            copy(5, land(up, 1), land(up, 1), down),
        ]

    def start(self):
        for copy in self.direct:
            copy.start()

    def forward(self):
        for near, far in zip(self.direct[:2], self.passed):
            near.wait_recv()
            far.start()

    def near(self):
        for copy in self.direct[2:]:
            copy.wait_recv()

    def far(self):
        for copy in self.passed:
            copy.wait_recv()

    def drain(self):
        for copy in self.direct + self.passed:
            copy.wait_send()


class Scatter:
    def __init__(self, own, bufs, rank, device, send, recv):
        up, down, far = wrap(rank + 1), wrap(rank - 1), wrap(rank + 2)
        through, summed, landed = bufs

        def copy(number, source, target, to):
            return remote(source, target, send.at[number], recv.at[number], device(to))

        self.first = [
            copy(0, own(far, 0), through.at[0], up),
            copy(1, own(far, 1), through.at[1], down),
            copy(2, own(up, 1), landed.at[1], up),
            copy(3, own(down, 0), landed.at[2], down),
        ]
        self.second = [
            copy(4, summed.at[0], landed.at[0], up),
            copy(5, summed.at[1], landed.at[3], down),
        ]
        self.through, self.summed, self.landed = through, summed, landed
        self.own, self.rank = own, rank

    def start(self):
        for copy in self.first:
            copy.start()

    def forward(self):
        for which in range(2):
            self.first[which].wait_recv()
            mine = self.own(wrap(self.rank + 1 - 2 * which), which)[...]
            total = mine.astype(F32) + self.through[which].astype(F32)
            self.summed[which] = total.astype(BF16)
            self.second[which].start()

    def finish(self):
        for copy in self.first[2:] + self.second:
            copy.wait_recv()

    def total(self, half):
        return self.own(self.rank, half)[...].astype(F32) + (
            self.landed[half].astype(F32) + self.landed[2 + half].astype(F32)
        )

    def drain(self):
        for copy in self.first + self.second:
            copy.wait_send()


class Exchange:
    def __init__(self, packed, land, place, send, recv):
        self.place, self.groups = place, packed.shape[0]
        self.packed, self.land, self.send, self.recv = packed, land, send, recv

    def copy(self, step):
        level, base, core = self.place
        target = lax.rem(base + step, self.groups)
        return remote(
            self.packed.at[target],
            self.land.at[base],
            self.send.at[step],
            self.recv.at[step],
            (level, target, core),
        )

    def start(self):
        each(1, self.groups, lambda step: self.copy(step).start())
        base = self.place[1]
        self.land[base] = self.packed[base]

    def wait(self, step):
        self.copy(step).wait_recv()

    def drain(self):
        each(1, self.groups, lambda step: self.copy(step).wait_send())


class Share:
    def __init__(self, exchange, rows, place, partner, sibling, send, recv, last_send, last_recv):
        core = place[2]
        self.exchange, self.groups = exchange, exchange.groups

        def copy(path, step):
            source = wrap(place[1] - step, self.groups)
            mine = rows.at[0, core, source]
            if path == 0:
                return remote(mine, mine, send.at[0, step], recv.at[0, step], sibling)
            return remote(mine, rows.at[1, core, source], send.at[1, step], recv.at[1, step], partner)

        self.copy = copy
        self.last = remote(rows.at[1, core], rows.at[1, core], last_send, last_recv, sibling)

    def turn(self):
        def step(number):
            self.copy(1, number).start()
            self.copy(0, number).start()

        def arrived(number):
            self.exchange.wait(number)
            step(number)

        step(0)
        each(1, self.groups, arrived)

    def own(self):
        each(0, self.groups, lambda step: self.copy(0, step).wait_recv())

    def partner(self):
        each(0, self.groups, lambda step: self.copy(1, step).wait_recv())
        self.last.start()

    def finish(self):
        self.last.wait_recv()

    def drain(self):
        def step(number):
            self.copy(0, number).wait_send()
            self.copy(1, number).wait_send()

        each(0, self.groups, step)
        self.last.wait_send()


def greet(devices):
    barrier = pltpu.get_barrier_semaphore()
    for device in devices:
        pl.semaphore_signal(barrier, inc=1, device_id=device, device_id_type=MESH)
    pl.semaphore_wait(barrier, len(devices))


def doc_of_row(lanes, docs):
    row = lax.broadcasted_iota(jnp.int32, (lanes, docs), 0) // (lanes // docs)
    return (row == lax.broadcasted_iota(jnp.int32, (lanes, docs), 1)).astype(F32)


def slot_matrix(route, pick):
    count, lanes = pick.shape
    docs = route.shape[1]
    block = lanes // docs
    spread = jnp.broadcast_to(route[...].astype(F32), (128, docs))
    by_row = dot(spread, doc_of_row(lanes, docs), (1, 1))[0:docs]
    target = dot(doc_of_row(docs, docs), spread, (1, 1))[:, 0:1]
    own = lax.broadcasted_iota(jnp.int32, (docs, lanes), 1)
    earlier = lax.broadcasted_iota(jnp.int32, (docs, lanes), 0) < own // block
    rank = jnp.sum(jnp.where((by_row == target) & earlier, 1.0, 0.0), axis=0, keepdims=True)
    place = (by_row[0:1] * SLOT + rank) * block + lax.rem(own[0:1], block).astype(F32)
    slots = lax.broadcasted_iota(jnp.int32, (count, lanes), 0).astype(F32)
    pick[...] = jnp.where(slots == place, 1.0, 0.0).astype(BF16)


def live_rows(doc_len, lanes):
    docs = doc_len.shape[1]
    lengths = jnp.broadcast_to(doc_len[...].astype(F32), (128, docs))
    lengths = dot(doc_of_row(lanes, docs), lengths, (1, 1))[:, 0:1]
    position = lax.rem(lax.broadcasted_iota(jnp.int32, (lanes, 1), 0), lanes // docs)
    return position.astype(F32) < lengths


def rms_of(square, width):
    return lax.rsqrt(square / width + EPS)


def kernel(
    docs, cot_docs, route, doc_len, wt1, wt2,
    sum1, sum2_out,
    pick, sum2,
    stage1, stage2, own1, weights1, weights2,
    normed1, act1, gate1, part1, joined1, through1, summed1, landed1, out1,
    packed, cot, rows, back,
    act2, slopes2, dn_sum, dn_far, mean_out, mean_in,
    terms2, near2, via2, far2,
    upstream, terms1, through_x, summed_x, landed_x, mid, final1,
    ring_send, ring_recv, swap_send, swap_recv, share_send, share_recv, pair_send, pair_recv,
    col_send, col_recv, local_sem,
):
    level, base, core = lax.axis_index("aa"), lax.axis_index("ba"), lax.axis_index("ma")
    row, col = base // RING, lax.rem(base, RING)
    lanes, width = docs.shape
    groups = packed.shape[0]
    count = groups * packed.shape[1]
    half, quarter = width // 2, width // 4
    block, deep = weights1.shape[2], weights2.shape[2]
    hidden1, hidden2 = weights1.shape[3], weights2.shape[3]
    tile = hidden2 // 2
    mate, partner = level + 1 - 2 * lax.rem(level, 2), RING - 1 - level
    across = RING - 1 - mate
    side = level // 2
    place = (level, base, core)
    sibling = (level, base, 1 - core)
    mate_chip, partner_chip = (mate, base, core), (partner, base, core)

    loads = [
        pltpu.make_async_copy(wt1, stage1, local_sem.at[0]),
    ] + [
        pltpu.make_async_copy(
            wt2.at[m, :, pl.ds(h * hidden2, hidden2)], stage2.at[h, m], local_sem.at[1 + 2 * m + h]
        )
        for m in range(2)
        for h in range(2)
    ]
    for load in loads:
        load.start()
    greet(
        [sibling, mate_chip, partner_chip]
        + [(level, lax.rem(base + step, groups), core) for step in range(1, groups)]
    )

    loads[0].wait()
    for q in range(RING):
        for m in range(2):
            own1[q, m] = stage1[m, :, q * hidden1:(q + 1) * hidden1].astype(BF16)
    weights1[base] = own1[col]

    def along(m, step):
        other = wrap(col + step)
        number = 4 * m + step
        return remote(
            own1.at[other, m],
            weights1.at[base, m],
            share_send.at[2, 1, number],
            share_recv.at[2, 1, number],
            (level, row * RING + other, core),
        )

    def gather_x(m, step, number):
        fixed = wrap(col + step)
        rows_of = lambda part: pl.ds(part * (block // 2), block // 2)
        land = lambda pos, part: weights1.at[pos * RING + fixed, m, rows_of(part)]
        own = (lambda part: own1.at[col, m, rows_of(part)]) if step == 0 else (lambda part: land(row, part))
        device = lambda pos: (level, pos * RING + col, core)
        return Gather(own, land, row, device, ring_send.at[number], ring_recv.at[number])

    spread = [[along(m, step) for step in (1, 3, 2)] for m in range(2)]
    gathers = [[gather_x(m, step, 4 * m + k) for k, step in enumerate((0, 3, 1, 2))] for m in range(2)]
    for m in range(2):
        for copy in spread[m]:
            copy.start()
        gathers[m][0].start()

    rows_half = lanes // 2
    rows_part = rows_half // 2
    on_y = lambda pos: (level, row * RING + pos, core)

    def doc_part(pos, part):
        return normed1.at[pos, pl.ds(pl.multiple_of(core * rows_half + part * rows_part, rows_part), rows_part)]

    documents = Gather(
        lambda part: docs.at[pl.ds(pl.multiple_of(core * rows_half + part * rows_part, rows_part), rows_part)],
        doc_part,
        col,
        on_y,
        ring_send.at[8],
        ring_recv.at[8],
    )
    def doc_pair(step):
        where = normed1.at[wrap(col + step), pl.ds(pl.multiple_of(core * rows_half, rows_half), rows_half)]
        return remote(where, where, pair_send.at[step], pair_recv.at[step], sibling)

    def down_z(m):
        return [
            remote(act2.at[1 - side, m], weights2.at[level, m], col_send.at[4 + m], col_recv.at[4 + m], partner_chip),
            remote(act2.at[side, m], weights2.at[level, m], col_send.at[6 + m], col_recv.at[6 + m], mate_chip),
            remote(weights2.at[partner, m], weights2.at[partner, m], col_send.at[8 + m], col_recv.at[8 + m], mate_chip),
        ]

    column = [down_z(m) for m in range(2)]
    for m in (1, 0):
        for h in range(2):
            loads[1 + 2 * m + h].wait()
            act2[h, m] = stage2[h, m].astype(BF16)
        column[m][0].start()
        column[m][1].start()
        weights2[level, m] = act2[side, m]

    left = pl.ds(pl.multiple_of(core * half, half), half)
    swaps = [
        Exchange(packed, land, place, swap_send.at[k], swap_recv.at[k])
        for k, land in enumerate((cot.at[0, core], rows.at[0, core], back))
    ]
    shares = [
        Share(
            swaps[k], buf, place, partner_chip, sibling,
            share_send.at[k], share_recv.at[k], pair_send.at[4 + k], pair_recv.at[4 + k],
        )
        for k, buf in enumerate((cot, rows))
    ]
    slot_matrix(route, pick)
    live = live_rows(doc_len, lanes)
    masked = jnp.where(live, cot_docs[:, left], jnp.zeros((lanes, half), BF16))
    packed[...] = dot(pick[...], masked).astype(BF16).reshape(packed.shape)

    for m in range(2):
        for k, copy in enumerate(spread[m]):
            copy.wait_recv()
            gathers[m][1 + k].start()
        if m == 0:
            documents.start()
        for gather in gathers[m][:3]:
            gather.forward()
        if m == 1:
            column[1][0].wait_recv()
            column[1][2].start()
        gathers[m][3].forward()
    documents.forward()
    documents.near()
    doc_pair(3).start()
    doc_pair(1).start()
    documents.far()
    doc_pair(2).start()
    normed1[col] = docs[...]
    documents.drain()
    for step in (1, 2, 3):
        doc_pair(step).wait()

    def normalize_one(number):
        floated = normed1[number].astype(F32)
        square = jnp.sum(floated * floated, axis=-1, keepdims=True)
        normed1[number] = (floated * rms_of(square, width)).astype(BF16)

    each(0, RING, normalize_one)
    for gather in gathers[0]:
        gather.near()
        gather.far()

    def matrix1(m):
        return weights1[:, m].reshape(width, hidden1)

    def give1(step):
        pos = wrap(col + step)
        return remote(
            part1.at[pos, 1 - core], joined1.at[pos], share_send.at[2, 0, step], share_recv.at[2, 0, step], sibling
        )

    def up_one(pos):
        pre = dot(normed1[pos], matrix1(0))
        sigma = jax.nn.sigmoid(pre)
        act1[pos] = (pre * sigma).astype(BF16)
        gate1[pos] = (sigma * (1.0 + pre * (1.0 - sigma))).astype(BF16)

    def down_one(step):
        pos = wrap(col + step)
        for number in range(2):
            h = lax.rem(1 - core + number, 2)
            piece = weights1[pl.ds(8 * h, 8), 1].reshape(half, hidden1)
            part1[pos, h] = dot(act1[pos], piece, (1, 1)).astype(BF16)
            if number == 0:
                give1(step).start()

    def join_one(step):
        pos = wrap(col + step)
        give1(step).wait_recv()
        joined1[pos] = (part1[pos, core].astype(F32) + joined1[pos].astype(F32)).astype(BF16)

    each(0, RING, up_one)
    for gather in gathers[1]:
        gather.near()
        gather.far()
    hold = lanes // 2
    reduce1 = Scatter(
        lambda pos, part: joined1.at[pos, pl.ds(part * hold, hold)],
        (through1, summed1, landed1),
        col,
        on_y,
        ring_send.at[9],
        ring_recv.at[9],
    )
    down_one(2)
    down_one(1)
    join_one(2)
    reduce1.first[0].start()
    reduce1.first[1].start()
    down_one(3)
    join_one(1)
    reduce1.first[2].start()
    down_one(0)
    join_one(3)
    reduce1.first[3].start()
    swaps[0].start()
    column[0][0].wait_recv()
    column[0][2].start()
    reduce1.forward()
    join_one(0)
    shares[0].turn()
    reduce1.finish()
    for part in range(2):
        where = slice(part * hold, (part + 1) * hold)
        out1[where] = (docs[where, left].astype(F32) + reduce1.total(part)).astype(BF16)
    swaps[0].drain()
    packed[...] = dot(pick[...], out1[...]).astype(BF16).reshape(packed.shape)
    swaps[1].start()
    shares[0].own()

    def flat(ref, path, h):
        return ref[path, h].reshape(count, half)

    def piece2(m, h, columns):
        return weights2[2 * h:2 * h + 2, m, :, columns].reshape(half, tile)

    def columns_of(number):
        return pl.ds(pl.multiple_of(number * tile, tile), tile)

    column[1][1].wait_recv()
    column[1][2].wait_recv()

    def incoming_tile(number):
        path, columns = number // 2, columns_of(lax.rem(number, 2))
        value = dot(flat(cot, path, 0), piece2(1, 0, columns)) + dot(
            flat(cot, path, 1), piece2(1, 1, columns)
        )
        stage2[path, :, :, columns] = value.reshape(2, deep, tile)

    each(0, 2, incoming_tile)
    reduce1.drain()
    for step in range(RING):
        give1(step).wait_send()
    shares[1].turn()
    shares[0].partner()
    shares[1].own()

    def normalize_two(path):
        square = sum(
            jnp.sum(jnp.square(flat(rows, path, h).astype(F32)), axis=-1, keepdims=True) for h in range(2)
        )
        factor = rms_of(square, width)
        for h in range(2):
            value = (flat(rows, path, h).astype(F32) * factor).astype(BF16)
            terms1[2 * path:2 * path + 2, h] = value.reshape(2, RING, block, half)
        return factor

    def normed2(path, h):
        return terms1[2 * path:2 * path + 2, h].reshape(count, half)

    def slope_tile(path, first, parts):
        where = slice(first, first + parts)

        def step(number):
            columns = columns_of(number)
            lefts = [
                terms1[2 * path + first:2 * path + first + parts, h].reshape(parts * deep, half) for h in range(2)
            ]
            pre = dot(lefts[0], piece2(0, 0, columns)) + dot(lefts[1], piece2(0, 1, columns))
            sigma = jax.nn.sigmoid(pre)
            incoming = stage2[path, where, :, columns].reshape(parts * deep, tile)
            slope = (incoming * sigma * (1.0 + pre * (1.0 - sigma))).astype(BF16)
            act2[path, where, :, columns] = (pre * sigma).astype(BF16).reshape(parts, deep, tile)
            slopes2[path, where, :, columns] = slope.reshape(parts, deep, tile)

        return step

    factor = normalize_two(0)
    column[0][1].wait_recv()
    column[0][2].wait_recv()
    for m in range(2):
        column[m][0].wait_send()
        column[m][1].wait_send()
    each(0, 2, slope_tile(0, 0, 2))
    shares[1].partner()
    shares[0].finish()
    each(2, 4, incoming_tile)
    shares[1].finish()
    normalize_two(1)

    def give2(spot):
        return remote(
            part1.at[spot, 1 - core], joined1.at[spot], share_send.at[2, 0, 4 + spot], share_recv.at[2, 0, 4 + spot], sibling
        )

    def dn_tiles(path, first, parts):
        for number in range(2):
            h = lax.rem(1 - core + number, 2)
            piece = weights2[pl.ds(2 * h, 2), 0].reshape(half, hidden2)
            left2 = slopes2[path, first:first + parts].reshape(parts * deep, hidden2)
            value = dot(left2, piece, (1, 1)).astype(BF16)
            part1[2 * path + first:2 * path + first + parts, h] = value.reshape(parts, deep, half)
            if number == 0:
                for spot in range(2 * path + first, 2 * path + first + parts):
                    give2(spot).start()

    def dn_of(spot):
        return part1[spot, core].astype(F32) + joined1[spot].astype(F32)

    def to_partner(part):
        return remote(dn_sum.at[part], dn_far.at[part], pair_send.at[6 + part], pair_recv.at[6 + part], partner_chip)

    def dn_out(part):
        give2(2 + part).wait_recv()
        dn_sum[part] = dn_of(2 + part).astype(BF16)
        to_partner(part).start()

    each(0, 2, slope_tile(1, 0, 1))
    dn_tiles(1, 0, 1)
    each(0, 2, slope_tile(1, 1, 1))
    dn_out(0)
    dn_tiles(1, 1, 1)
    dn_out(1)
    dn_tiles(0, 0, 2)

    def term_tiles(m, lefts, right):
        def step(number):
            columns = columns_of(number)
            for h in range(2):
                value = sum(
                    dot(lefts(path, h), right[path, :, :, columns].reshape(count, tile), (0, 0))
                    for path in range(2)
                )
                terms2[2 * h:2 * h + 2, m, :, columns] = value.astype(BF16).reshape(2, deep, tile)

        each(0, 2, step)

    def sums_z(m):
        return [
            remote(terms2.at[across, m], via2.at[m], col_send.at[10 + m], col_recv.at[10 + m], mate_chip),
            remote(terms2.at[mate, m], near2.at[m], col_send.at[12 + m], col_recv.at[12 + m], mate_chip),
            remote(via2.at[m], far2.at[m], col_send.at[14 + m], col_recv.at[14 + m], partner_chip),
        ]

    sums = [sums_z(m) for m in range(2)]
    term_tiles(1, lambda path, h: flat(cot, path, h), act2)
    sums[1][0].start()
    sums[1][1].start()

    for part in range(2):
        give2(part).wait_recv()
        to_partner(part).wait_recv()

    def pieces():
        value = jnp.concatenate([dn_of(part) + dn_far[part].astype(F32) for part in range(2)], axis=0)
        return flat(rows, 0, core).astype(F32) * factor, value

    normed, value = pieces()
    mean = jnp.sum(value * normed, axis=-1, keepdims=True)
    mean_out[...] = jnp.broadcast_to(mean, mean_out.shape)
    swap_mean = remote(mean_out, mean_in, pair_send.at[9], pair_recv.at[9], sibling)
    swap_mean.start()
    swap_mean.wait_recv()
    mean = (mean + mean_in[:, 0:1]) / width
    normed, value = pieces()
    result = flat(cot, 0, core).astype(F32) + factor * (value - normed * mean)
    swaps[1].drain()
    packed[...] = result.astype(BF16).reshape(packed.shape)
    swaps[2].start()
    term_tiles(0, normed2, slopes2)
    sums[0][0].start()
    sums[0][1].start()
    sums[1][0].wait_recv()
    via2[1] = (terms2[partner, 1].astype(F32) + via2[1].astype(F32)).astype(BF16)
    sums[1][2].start()

    each(1, groups, swaps[2].wait)
    upstream[col, core] = dot(pick[...], back[...].reshape(count, half), (0, 0)).astype(BF16)
    lifts = Gather(
        lambda part: upstream.at[col, core, pl.ds(part * hold, hold)],
        lambda pos, part: upstream.at[pos, core, pl.ds(part * hold, hold)],
        col,
        on_y,
        ring_send.at[10],
        ring_recv.at[10],
    )
    lifts.start()

    def lift_pair(step):
        where = upstream.at[wrap(col + step), core]
        return remote(where, where, pair_send.at[10 + step], pair_recv.at[10 + step], sibling)

    lift_pair(0).start()
    lifts.forward()
    lifts.near()
    lift_pair(3).start()
    lift_pair(1).start()

    def slope_one(pos):
        incoming = dot(upstream[pos, 0], weights1[0:8, 1].reshape(half, hidden1)) + dot(
            upstream[pos, 1], weights1[8:16, 1].reshape(half, hidden1)
        )
        joined1[pos] = (incoming * gate1[pos].astype(F32)).astype(BF16)

    lifts.far()
    lift_pair(2).start()
    for step in range(RING):
        lift_pair(step).wait_recv()

    def term_one(m, lefts, right):
        for h in range(2):
            value = dot(lefts(h).reshape(RING * lanes, half), right[...].reshape(RING * lanes, hidden1), (0, 0))
            terms1[2 * h:2 * h + 2, m] = value.astype(BF16).reshape(2, RING, block, hidden1)

    def scatter_x(m):
        return Scatter(
            lambda pos, part: terms1.at[pos, m, pl.ds(2 * part, 2)],
            (through_x.at[m], summed_x.at[m], landed_x.at[m]),
            row,
            lambda pos: (level, pos * RING + col, core),
            ring_send.at[11 + m],
            ring_recv.at[11 + m],
        )

    plane = [scatter_x(m) for m in range(2)]
    term_one(1, lambda h: upstream[:, h], act1)
    plane[1].start()
    each(0, RING, slope_one)
    term_one(0, lambda h: normed1[:, :, h * half:(h + 1) * half], joined1)
    plane[0].start()
    plane[1].forward()
    sums[0][0].wait_recv()
    via2[0] = (terms2[partner, 0].astype(F32) + via2[0].astype(F32)).astype(BF16)
    sums[0][2].start()
    plane[0].forward()

    def along_back(step, m):
        other = wrap(col + step)
        number = 16 + 4 * m + step
        return remote(
            mid.at[m, other], final1.at[m, col], col_send.at[number], col_recv.at[number],
            (level, row * RING + other, core),
        )

    for m in (1, 0):
        plane[m].finish()
        for part in range(2):
            mid[m, 2 * part:2 * part + 2] = plane[m].total(part).astype(BF16)
        for step in (2, 1, 3):
            along_back(step, m).start()
        final1[m, col] = mid[m, col]
    own_side = pl.ds(pl.multiple_of(side * hidden2, hidden2), hidden2)
    other_side = pl.ds(pl.multiple_of((1 - side) * hidden2, hidden2), hidden2)
    for m in (1, 0):
        sums[m][1].wait_recv()
        sum2[m, :, own_side] = (terms2[level, m].astype(F32) + near2[m].astype(F32)).astype(BF16)
        sums[m][2].wait_recv()
        sum2[m, :, other_side] = far2[m]
    keep = pltpu.make_async_copy(sum2, sum2_out, local_sem.at[0])
    keep.start()
    for m in (1, 0):
        for step in (1, 3, 2):
            along_back(step, m).wait_recv()
        for q in range(RING):
            sum1[m, :, q * hidden1:(q + 1) * hidden1] = final1[m, q]

    for copy in spread[0] + spread[1] + [column[0][2], column[1][2]] + sums[0] + sums[1]:
        copy.wait_send()
    for ring in gathers[0] + gathers[1] + [lifts] + plane + [swaps[2]] + shares:
        ring.drain()
    for step in range(RING):
        lift_pair(step).wait_send()
    for step in (1, 2, 3):
        along_back(step, 0).wait_send()
        along_back(step, 1).wait_send()
        give2(step).wait_send()
    give2(0).wait_send()
    to_partner(0).wait_send()
    to_partner(1).wait_send()
    swap_mean.wait_send()
    keep.wait()


def outer_step(weights, moment, delta):
    new_moment = MOMENTUM * moment + delta[None]
    return (weights - OUTER_RATE * (delta[None] + MOMENTUM * new_moment), new_moment)


def local(docs, cot, route, doc_len, wt1, mom1, wt2, mom2):
    blocks, block, width = docs.shape
    groups = lax.axis_size("ba")
    levels = lax.axis_size("aa")
    slots = groups * SLOT
    count, lanes = slots * block, blocks * block
    hidden = wt1.shape[-1]
    whole = pl.BlockSpec(memory_space=pltpu.VMEM)
    anywhere = pl.BlockSpec(memory_space=pl.ANY)
    half, quarter = width // 2, width // 4
    per = count // groups
    small = width // 16
    hidden1, hidden2 = hidden // RING, hidden // 2

    def vmem(*sizes, kind=BF16):
        return pltpu.VMEM(sizes, kind)

    def dma(*sizes):
        return pltpu.SemaphoreType.DMA(sizes)

    hold = lanes // 2
    sum1, sum2 = pl.pallas_call(
        kernel,
        out_shape=(
            jax.ShapeDtypeStruct((2, small, hidden), BF16),
            jax.ShapeDtypeStruct((2, quarter, hidden), BF16),
        ),
        in_specs=[whole, whole, whole, whole, anywhere, anywhere],
        out_specs=[whole, anywhere],
        scratch_shapes=[
            vmem(count, lanes),
            vmem(2, quarter, hidden),
            vmem(2, small, hidden, kind=F32),
            vmem(2, 2, quarter, hidden2, kind=F32),
            vmem(RING, 2, small, hidden1),
            vmem(16, 2, small, hidden1),
            vmem(RING, 2, quarter, hidden2),
            vmem(RING, lanes, width),
            vmem(RING, lanes, hidden1),
            vmem(RING, lanes, hidden1),
            vmem(RING, 2, lanes, half),
            vmem(RING, lanes, half),
            vmem(2, hold, half),
            vmem(2, hold, half),
            vmem(4, hold, half),
            vmem(lanes, half),
            vmem(groups, per, half),
            vmem(2, 2, groups, per, half),
            vmem(2, 2, groups, per, half),
            vmem(groups, per, half),
            vmem(2, 2, quarter, hidden2),
            vmem(2, 2, quarter, hidden2),
            vmem(2, quarter, half),
            vmem(2, quarter, half),
            vmem(count, 128, kind=F32),
            vmem(count, 128, kind=F32),
            vmem(RING, 2, quarter, hidden2),
            vmem(2, quarter, hidden2),
            vmem(2, quarter, hidden2),
            vmem(2, quarter, hidden2),
            vmem(RING, 2, lanes, half),
            vmem(RING, 2, RING, small, hidden1),
            vmem(2, 2, 2, small, hidden1),
            vmem(2, 2, 2, small, hidden1),
            vmem(2, 4, 2, small, hidden1),
            vmem(2, RING, small, hidden1),
            vmem(2, RING, small, hidden1),
            dma(13, 6),
            dma(13, 6),
            dma(3, groups),
            dma(3, groups),
            dma(3, 2, groups),
            dma(3, 2, groups),
            dma(14),
            dma(14),
            dma(24),
            dma(24),
            dma(5),
        ],
        compiler_params=pltpu.CompilerParams(
            collective_id=0, has_side_effects=True, vmem_limit_bytes=VMEM_LIMIT
        ),
        name="window",
    )(docs.reshape(lanes, width), cot.reshape(lanes, width), route.T, doc_len[None], wt1[0], wt2[0])

    delta1 = sum1.astype(F32) / groups
    delta2 = sum2.astype(F32) / levels
    new_wt1, new_mom1 = outer_step(wt1, mom1, delta1)
    new_wt2, new_mom2 = outer_step(wt2, mom2, delta2)
    return (new_wt1, new_mom1, new_wt2, new_mom2)


def solution(mesh):
    return jax.shard_map(
        local,
        mesh=mesh,
        in_specs=(
            P(("aa", "ba"), None, None),
            P(("aa", "ba"), None, None),
            P(("aa", "ba"), None),
            P(("aa", "ba")),
            P("aa", None, "ba", "ma"),
            P("aa", None, "ba", "ma"),
            P("ba", None, "aa", "ma"),
            P("ba", None, "aa", "ma"),
        ),
        out_specs=(
            P("aa", None, "ba", "ma"),
            P("aa", None, "ba", "ma"),
            P("ba", None, "aa", "ma"),
            P("ba", None, "aa", "ma"),
        ),
        check_vma=False,
    )
```

```python
import functools

import jax
import jax.numpy as jnp
from jax import lax
from jax.experimental import pallas as pl
from jax.experimental.pallas import tpu as pltpu
from jax.sharding import PartitionSpec as P

SLOT = 2
EPS = 1e-05
MOMENTUM = 0.9
OUTER_RATE = 0.7

MESH = pl.DeviceIdType.MESH
BF16 = jnp.bfloat16
F32 = jnp.float32
RING = 4
VMEM_LIMIT = 57 * 1024 * 1024


def dot(left, right, contract=(1, 0)):
    return lax.dot_general(
        left,
        right,
        (((contract[0],), (contract[1],)), ((), ())),
        preferred_element_type=F32,
    )


def wrap(index, size=RING):
    return lax.rem(index + size, size)


def remote(source, target, send, recv, device):
    return pltpu.make_async_remote_copy(
        src_ref=source,
        dst_ref=target,
        send_sem=send,
        recv_sem=recv,
        device_id=device,
        device_id_type=MESH,
    )


def each(first, last, step):
    def body(number, carry):
        step(number)
        return carry

    lax.fori_loop(first, last, body, 0)


class Gather:
    def __init__(self, own, land, rank, device, send, recv):
        up, down = wrap(rank + 1), wrap(rank - 1)

        def copy(number, source, target, to):
            return remote(source, target, send.at[number], recv.at[number], device(to))

        self.direct = [
            copy(0, own(0), land(rank, 0), up),
            copy(1, own(1), land(rank, 1), down),
            copy(2, own(1), land(rank, 1), up),
            copy(3, own(0), land(rank, 0), down),
        ]
        self.passed = [
            copy(4, land(down, 0), land(down, 0), up),
            copy(5, land(up, 1), land(up, 1), down),
        ]

    def start(self):
        for copy in self.direct:
            copy.start()

    def forward(self):
        for near, far in zip(self.direct[:2], self.passed):
            near.wait_recv()
            far.start()

    def near(self):
        for copy in self.direct[2:]:
            copy.wait_recv()

    def far(self):
        for copy in self.passed:
            copy.wait_recv()

    def drain(self):
        for copy in self.direct + self.passed:
            copy.wait_send()


class Scatter:
    def __init__(self, own, bufs, rank, device, send, recv):
        up, down, far = wrap(rank + 1), wrap(rank - 1), wrap(rank + 2)
        through, summed, landed = bufs

        def copy(number, source, target, to):
            return remote(source, target, send.at[number], recv.at[number], device(to))

        self.first = [
            copy(0, own(far, 0), through.at[0], up),
            copy(1, own(far, 1), through.at[1], down),
            copy(2, own(up, 1), landed.at[1], up),
            copy(3, own(down, 0), landed.at[2], down),
        ]
        self.second = [
            copy(4, summed.at[0], landed.at[0], up),
            copy(5, summed.at[1], landed.at[3], down),
        ]
        self.through, self.summed, self.landed = through, summed, landed
        self.own, self.rank = own, rank

    def start(self):
        for copy in self.first:
            copy.start()

    def forward(self):
        for which in range(2):
            self.first[which].wait_recv()
            mine = self.own(wrap(self.rank + 1 - 2 * which), which)[...]
            total = mine.astype(F32) + self.through[which].astype(F32)
            self.summed[which] = total.astype(BF16)
            self.second[which].start()

    def finish(self):
        for copy in self.first[2:] + self.second:
            copy.wait_recv()

    def total(self, half):
        return self.own(self.rank, half)[...].astype(F32) + (
            self.landed[half].astype(F32) + self.landed[2 + half].astype(F32)
        )

    def drain(self):
        for copy in self.first + self.second:
            copy.wait_send()


class Exchange:
    def __init__(self, packed, land, place, send, recv):
        self.place, self.groups = place, packed.shape[0]
        self.packed, self.land, self.send, self.recv = packed, land, send, recv

    def copy(self, step):
        level, base, core = self.place
        target = lax.rem(base + step, self.groups)
        return remote(
            self.packed.at[target],
            self.land.at[base],
            self.send.at[step],
            self.recv.at[step],
            (level, target, core),
        )

    def start(self):
        each(1, self.groups, lambda step: self.copy(step).start())
        base = self.place[1]
        self.land[base] = self.packed[base]

    def wait(self, step):
        self.copy(step).wait_recv()

    def drain(self):
        each(1, self.groups, lambda step: self.copy(step).wait_send())


class Share:
    def __init__(self, exchange, rows, place, partner, sibling, send, recv, last_send, last_recv):
        core = place[2]
        self.exchange, self.groups = exchange, exchange.groups

        def copy(path, step):
            source = wrap(place[1] - step, self.groups)
            mine = rows.at[0, core, source]
            if path == 0:
                return remote(mine, mine, send.at[0, step], recv.at[0, step], sibling)
            return remote(mine, rows.at[1, core, source], send.at[1, step], recv.at[1, step], partner)

        self.copy = copy
        self.last = remote(rows.at[1, core], rows.at[1, core], last_send, last_recv, sibling)

    def turn(self):
        def step(number):
            self.copy(1, number).start()
            self.copy(0, number).start()

        def arrived(number):
            self.exchange.wait(number)
            step(number)

        step(0)
        each(1, self.groups, arrived)

    def own(self):
        each(0, self.groups, lambda step: self.copy(0, step).wait_recv())

    def partner(self):
        each(0, self.groups, lambda step: self.copy(1, step).wait_recv())
        self.last.start()

    def finish(self):
        self.last.wait_recv()

    def drain(self):
        def step(number):
            self.copy(0, number).wait_send()
            self.copy(1, number).wait_send()

        each(0, self.groups, step)
        self.last.wait_send()


def greet(devices):
    barrier = pltpu.get_barrier_semaphore()
    for device in devices:
        pl.semaphore_signal(barrier, inc=1, device_id=device, device_id_type=MESH)
    pl.semaphore_wait(barrier, len(devices))


def doc_of_row(lanes, docs):
    row = lax.broadcasted_iota(jnp.int32, (lanes, docs), 0) // (lanes // docs)
    return (row == lax.broadcasted_iota(jnp.int32, (lanes, docs), 1)).astype(F32)


def slot_matrix(route, pick):
    count, lanes = pick.shape
    docs = route.shape[1]
    block = lanes // docs
    spread = jnp.broadcast_to(route[...].astype(F32), (128, docs))
    by_row = dot(spread, doc_of_row(lanes, docs), (1, 1))[0:docs]
    target = dot(doc_of_row(docs, docs), spread, (1, 1))[:, 0:1]
    own = lax.broadcasted_iota(jnp.int32, (docs, lanes), 1)
    earlier = lax.broadcasted_iota(jnp.int32, (docs, lanes), 0) < own // block
    rank = jnp.sum(jnp.where((by_row == target) & earlier, 1.0, 0.0), axis=0, keepdims=True)
    place = (by_row[0:1] * SLOT + rank) * block + lax.rem(own[0:1], block).astype(F32)
    slots = lax.broadcasted_iota(jnp.int32, (count, lanes), 0).astype(F32)
    pick[...] = jnp.where(slots == place, 1.0, 0.0).astype(BF16)


def live_rows(doc_len, lanes):
    docs = doc_len.shape[1]
    lengths = jnp.broadcast_to(doc_len[...].astype(F32), (128, docs))
    lengths = dot(doc_of_row(lanes, docs), lengths, (1, 1))[:, 0:1]
    position = lax.rem(lax.broadcasted_iota(jnp.int32, (lanes, 1), 0), lanes // docs)
    return position.astype(F32) < lengths


def rms_of(square, width):
    return lax.rsqrt(square / width + EPS)


def kernel(
    docs, cot_docs, route, doc_len, wt1, wt2,
    sum1, sum2_out,
    pick, sum2,
    stage1, stage2, own1, weights1, weights2,
    normed1, act1, gate1, part1, joined1, through1, summed1, landed1, out1,
    packed, cot, rows, back,
    act2, slopes2, dn_sum, dn_far, mean_out, mean_in,
    terms2, near2, via2, far2,
    upstream, terms1, through_x, summed_x, landed_x, mid, final1,
    ring_send, ring_recv, swap_send, swap_recv, share_send, share_recv, pair_send, pair_recv,
    col_send, col_recv, local_sem,
):
    level, base, core = lax.axis_index("aa"), lax.axis_index("ba"), lax.axis_index("ma")
    row, col = base // RING, lax.rem(base, RING)
    lanes, width = docs.shape
    groups = packed.shape[0]
    count = groups * packed.shape[1]
    half, quarter = width // 2, width // 4
    block, deep = weights1.shape[2], weights2.shape[2]
    hidden1, hidden2 = weights1.shape[3], weights2.shape[3]
    tile = hidden2 // 2
    mate, partner = level + 1 - 2 * lax.rem(level, 2), RING - 1 - level
    across = RING - 1 - mate
    side = level // 2
    place = (level, base, core)
    sibling = (level, base, 1 - core)
    mate_chip, partner_chip = (mate, base, core), (partner, base, core)

    loads = [
        pltpu.make_async_copy(wt1, stage1, local_sem.at[0]),
    ] + [
        pltpu.make_async_copy(
            wt2.at[m, :, pl.ds(h * hidden2, hidden2)], stage2.at[h, m], local_sem.at[1 + 2 * m + h]
        )
        for m in range(2)
        for h in range(2)
    ]
    for load in loads:
        load.start()
    greet(
        [sibling, mate_chip, partner_chip]
        + [(level, lax.rem(base + step, groups), core) for step in range(1, groups)]
    )

    loads[0].wait()
    for q in range(RING):
        for m in range(2):
            own1[q, m] = stage1[m, :, q * hidden1:(q + 1) * hidden1].astype(BF16)
    weights1[base] = own1[col]

    def along(m, step):
        other = wrap(col + step)
        number = 4 * m + step
        return remote(
            own1.at[other, m],
            weights1.at[base, m],
            share_send.at[2, 1, number],
            share_recv.at[2, 1, number],
            (level, row * RING + other, core),
        )

    def gather_x(m, step, number):
        fixed = wrap(col + step)
        rows_of = lambda part: pl.ds(part * (block // 2), block // 2)
        land = lambda pos, part: weights1.at[pos * RING + fixed, m, rows_of(part)]
        own = (lambda part: own1.at[col, m, rows_of(part)]) if step == 0 else (lambda part: land(row, part))
        device = lambda pos: (level, pos * RING + col, core)
        return Gather(own, land, row, device, ring_send.at[number], ring_recv.at[number])

    spread = [[along(m, step) for step in (1, 3, 2)] for m in range(2)]
    gathers = [[gather_x(m, step, 4 * m + k) for k, step in enumerate((0, 3, 1, 2))] for m in range(2)]
    for m in range(2):
        for copy in spread[m]:
            copy.start()
        gathers[m][0].start()

    rows_half = lanes // 2
    rows_part = rows_half // 2
    on_y = lambda pos: (level, row * RING + pos, core)

    def doc_part(pos, part):
        return normed1.at[pos, pl.ds(pl.multiple_of(core * rows_half + part * rows_part, rows_part), rows_part)]

    documents = Gather(
        lambda part: docs.at[pl.ds(pl.multiple_of(core * rows_half + part * rows_part, rows_part), rows_part)],
        doc_part,
        col,
        on_y,
        ring_send.at[8],
        ring_recv.at[8],
    )
    def doc_pair(step):
        where = normed1.at[wrap(col + step), pl.ds(pl.multiple_of(core * rows_half, rows_half), rows_half)]
        return remote(where, where, pair_send.at[step], pair_recv.at[step], sibling)

    def down_z(m):
        return [
            remote(act2.at[1 - side, m], weights2.at[level, m], col_send.at[4 + m], col_recv.at[4 + m], partner_chip),
            remote(act2.at[side, m], weights2.at[level, m], col_send.at[6 + m], col_recv.at[6 + m], mate_chip),
            remote(weights2.at[partner, m], weights2.at[partner, m], col_send.at[8 + m], col_recv.at[8 + m], mate_chip),
        ]

    column = [down_z(m) for m in range(2)]
    for m in (1, 0):
        for h in range(2):
            loads[1 + 2 * m + h].wait()
            act2[h, m] = stage2[h, m].astype(BF16)
        column[m][0].start()
        column[m][1].start()
        weights2[level, m] = act2[side, m]

    left = pl.ds(pl.multiple_of(core * half, half), half)
    swaps = [
        Exchange(packed, land, place, swap_send.at[k], swap_recv.at[k])
        for k, land in enumerate((cot.at[0, core], rows.at[0, core], back))
    ]
    shares = [
        Share(
            swaps[k], buf, place, partner_chip, sibling,
            share_send.at[k], share_recv.at[k], pair_send.at[4 + k], pair_recv.at[4 + k],
        )
        for k, buf in enumerate((cot, rows))
    ]
    slot_matrix(route, pick)
    live = live_rows(doc_len, lanes)
    masked = jnp.where(live, cot_docs[:, left], jnp.zeros((lanes, half), BF16))
    packed[...] = dot(pick[...], masked).astype(BF16).reshape(packed.shape)

    for m in range(2):
        for k, copy in enumerate(spread[m]):
            copy.wait_recv()
            gathers[m][1 + k].start()
        if m == 0:
            documents.start()
        for gather in gathers[m][:3]:
            gather.forward()
        if m == 1:
            column[1][0].wait_recv()
            column[1][2].start()
        gathers[m][3].forward()
    documents.forward()
    documents.near()
    doc_pair(3).start()
    doc_pair(1).start()
    documents.far()
    doc_pair(2).start()
    swaps[0].start()
    normed1[col] = docs[...]
    documents.drain()
    for step in (1, 2, 3):
        doc_pair(step).wait()

    def normalize_one(number):
        floated = normed1[number].astype(F32)
        square = jnp.sum(floated * floated, axis=-1, keepdims=True)
        normed1[number] = (floated * rms_of(square, width)).astype(BF16)

    each(0, RING, normalize_one)
    for gather in gathers[0]:
        gather.near()
        gather.far()

    def matrix1(m):
        return weights1[:, m].reshape(width, hidden1)

    def give1(step):
        pos = wrap(col + step)
        return remote(
            part1.at[pos, 1 - core], joined1.at[pos], share_send.at[2, 0, step], share_recv.at[2, 0, step], sibling
        )

    def up_one(pos):
        pre = dot(normed1[pos], matrix1(0))
        sigma = jax.nn.sigmoid(pre)
        act1[pos] = (pre * sigma).astype(BF16)
        gate1[pos] = (sigma * (1.0 + pre * (1.0 - sigma))).astype(BF16)

    def down_one(step):
        pos = wrap(col + step)
        for number in range(2):
            h = lax.rem(1 - core + number, 2)
            piece = weights1[pl.ds(8 * h, 8), 1].reshape(half, hidden1)
            part1[pos, h] = dot(act1[pos], piece, (1, 1)).astype(BF16)
            if number == 0:
                give1(step).start()

    def join_one(step):
        pos = wrap(col + step)
        give1(step).wait_recv()
        joined1[pos] = (part1[pos, core].astype(F32) + joined1[pos].astype(F32)).astype(BF16)

    each(0, RING, up_one)
    for gather in gathers[1]:
        gather.near()
        gather.far()
    hold = lanes // 2
    reduce1 = Scatter(
        lambda pos, part: joined1.at[pos, pl.ds(part * hold, hold)],
        (through1, summed1, landed1),
        col,
        on_y,
        ring_send.at[9],
        ring_recv.at[9],
    )
    down_one(2)
    down_one(1)
    join_one(2)
    reduce1.first[0].start()
    reduce1.first[1].start()
    down_one(3)
    join_one(1)
    reduce1.first[2].start()
    down_one(0)
    join_one(3)
    reduce1.first[3].start()
    column[0][0].wait_recv()
    column[0][2].start()
    reduce1.forward()
    join_one(0)
    shares[0].turn()
    reduce1.finish()
    for part in range(2):
        where = slice(part * hold, (part + 1) * hold)
        out1[where] = (docs[where, left].astype(F32) + reduce1.total(part)).astype(BF16)
    swaps[0].drain()
    packed[...] = dot(pick[...], out1[...]).astype(BF16).reshape(packed.shape)
    swaps[1].start()
    shares[0].own()

    def flat(ref, path, h):
        return ref[path, h].reshape(count, half)

    def piece2(m, h, columns):
        return weights2[2 * h:2 * h + 2, m, :, columns].reshape(half, tile)

    def columns_of(number):
        return pl.ds(pl.multiple_of(number * tile, tile), tile)

    column[1][1].wait_recv()
    column[1][2].wait_recv()

    def incoming_tile(number):
        path, columns = number // 2, columns_of(lax.rem(number, 2))
        value = dot(flat(cot, path, 0), piece2(1, 0, columns)) + dot(
            flat(cot, path, 1), piece2(1, 1, columns)
        )
        stage2[path, :, :, columns] = value.reshape(2, deep, tile)

    each(0, 2, incoming_tile)
    reduce1.drain()
    for step in range(RING):
        give1(step).wait_send()
    shares[1].turn()
    shares[0].partner()
    shares[1].own()

    def normalize_two(path):
        square = sum(
            jnp.sum(jnp.square(flat(rows, path, h).astype(F32)), axis=-1, keepdims=True) for h in range(2)
        )
        factor = rms_of(square, width)
        for h in range(2):
            value = (flat(rows, path, h).astype(F32) * factor).astype(BF16)
            terms1[2 * path:2 * path + 2, h] = value.reshape(2, RING, block, half)
        return factor

    def normed2(path, h):
        return terms1[2 * path:2 * path + 2, h].reshape(count, half)

    def slope_tile(path, first, parts):
        where = slice(first, first + parts)

        def step(number):
            columns = columns_of(number)
            lefts = [
                terms1[2 * path + first:2 * path + first + parts, h].reshape(parts * deep, half) for h in range(2)
            ]
            pre = dot(lefts[0], piece2(0, 0, columns)) + dot(lefts[1], piece2(0, 1, columns))
            sigma = jax.nn.sigmoid(pre)
            incoming = stage2[path, where, :, columns].reshape(parts * deep, tile)
            slope = (incoming * sigma * (1.0 + pre * (1.0 - sigma))).astype(BF16)
            act2[path, where, :, columns] = (pre * sigma).astype(BF16).reshape(parts, deep, tile)
            slopes2[path, where, :, columns] = slope.reshape(parts, deep, tile)

        return step

    factor = normalize_two(0)
    column[0][1].wait_recv()
    column[0][2].wait_recv()
    for m in range(2):
        column[m][0].wait_send()
        column[m][1].wait_send()
    each(0, 2, slope_tile(0, 0, 2))
    shares[1].partner()
    shares[0].finish()
    each(2, 4, incoming_tile)
    shares[1].finish()
    normalize_two(1)

    def give2(spot):
        return remote(
            part1.at[spot, 1 - core], joined1.at[spot], share_send.at[2, 0, 4 + spot], share_recv.at[2, 0, 4 + spot], sibling
        )

    def dn_tiles(path, first, parts):
        for number in range(2):
            h = lax.rem(1 - core + number, 2)
            piece = weights2[pl.ds(2 * h, 2), 0].reshape(half, hidden2)
            left2 = slopes2[path, first:first + parts].reshape(parts * deep, hidden2)
            value = dot(left2, piece, (1, 1)).astype(BF16)
            part1[2 * path + first:2 * path + first + parts, h] = value.reshape(parts, deep, half)
            if number == 0:
                for spot in range(2 * path + first, 2 * path + first + parts):
                    give2(spot).start()

    def dn_of(spot):
        return part1[spot, core].astype(F32) + joined1[spot].astype(F32)

    def to_partner(part):
        return remote(dn_sum.at[part], dn_far.at[part], pair_send.at[6 + part], pair_recv.at[6 + part], partner_chip)

    def dn_out(part):
        give2(2 + part).wait_recv()
        dn_sum[part] = dn_of(2 + part).astype(BF16)
        to_partner(part).start()

    each(0, 2, slope_tile(1, 0, 1))
    dn_tiles(1, 0, 1)
    each(0, 2, slope_tile(1, 1, 1))
    dn_out(0)
    dn_tiles(1, 1, 1)
    dn_out(1)
    dn_tiles(0, 0, 2)

    def term_tiles(m, lefts, right):
        def step(number):
            columns = columns_of(number)
            for h in range(2):
                value = sum(
                    dot(lefts(path, h), right[path, :, :, columns].reshape(count, tile), (0, 0))
                    for path in range(2)
                )
                terms2[2 * h:2 * h + 2, m, :, columns] = value.astype(BF16).reshape(2, deep, tile)

        each(0, 2, step)

    def sums_z(m):
        return [
            remote(terms2.at[across, m], via2.at[m], col_send.at[10 + m], col_recv.at[10 + m], mate_chip),
            remote(terms2.at[mate, m], near2.at[m], col_send.at[12 + m], col_recv.at[12 + m], mate_chip),
            remote(via2.at[m], far2.at[m], col_send.at[14 + m], col_recv.at[14 + m], partner_chip),
        ]

    sums = [sums_z(m) for m in range(2)]
    term_tiles(1, lambda path, h: flat(cot, path, h), act2)
    sums[1][0].start()
    sums[1][1].start()

    for part in range(2):
        give2(part).wait_recv()
        to_partner(part).wait_recv()

    def pieces():
        value = jnp.concatenate([dn_of(part) + dn_far[part].astype(F32) for part in range(2)], axis=0)
        return flat(rows, 0, core).astype(F32) * factor, value

    normed, value = pieces()
    mean = jnp.sum(value * normed, axis=-1, keepdims=True)
    mean_out[...] = jnp.broadcast_to(mean, mean_out.shape)
    swap_mean = remote(mean_out, mean_in, pair_send.at[9], pair_recv.at[9], sibling)
    swap_mean.start()
    swap_mean.wait_recv()
    mean = (mean + mean_in[:, 0:1]) / width
    normed, value = pieces()
    result = flat(cot, 0, core).astype(F32) + factor * (value - normed * mean)
    swaps[1].drain()
    packed[...] = result.astype(BF16).reshape(packed.shape)
    swaps[2].start()
    term_tiles(0, normed2, slopes2)
    sums[0][0].start()
    sums[0][1].start()
    sums[1][0].wait_recv()
    via2[1] = (terms2[partner, 1].astype(F32) + via2[1].astype(F32)).astype(BF16)
    sums[1][2].start()

    each(1, groups, swaps[2].wait)
    upstream[col, core] = dot(pick[...], back[...].reshape(count, half), (0, 0)).astype(BF16)
    lifts = Gather(
        lambda part: upstream.at[col, core, pl.ds(part * hold, hold)],
        lambda pos, part: upstream.at[pos, core, pl.ds(part * hold, hold)],
        col,
        on_y,
        ring_send.at[10],
        ring_recv.at[10],
    )
    lifts.start()

    def lift_pair(step):
        where = upstream.at[wrap(col + step), core]
        return remote(where, where, pair_send.at[10 + step], pair_recv.at[10 + step], sibling)

    lift_pair(0).start()
    lifts.forward()
    lifts.near()
    lift_pair(3).start()
    lift_pair(1).start()

    def slope_one(pos):
        incoming = dot(upstream[pos, 0], weights1[0:8, 1].reshape(half, hidden1)) + dot(
            upstream[pos, 1], weights1[8:16, 1].reshape(half, hidden1)
        )
        joined1[pos] = (incoming * gate1[pos].astype(F32)).astype(BF16)

    lifts.far()
    lift_pair(2).start()
    for step in range(RING):
        lift_pair(step).wait_recv()

    def term_one(m, lefts, right):
        for h in range(2):
            value = dot(lefts(h).reshape(RING * lanes, half), right[...].reshape(RING * lanes, hidden1), (0, 0))
            terms1[2 * h:2 * h + 2, m] = value.astype(BF16).reshape(2, RING, block, hidden1)

    def scatter_x(m):
        return Scatter(
            lambda pos, part: terms1.at[pos, m, pl.ds(2 * part, 2)],
            (through_x.at[m], summed_x.at[m], landed_x.at[m]),
            row,
            lambda pos: (level, pos * RING + col, core),
            ring_send.at[11 + m],
            ring_recv.at[11 + m],
        )

    plane = [scatter_x(m) for m in range(2)]
    term_one(1, lambda h: upstream[:, h], act1)
    plane[1].start()
    each(0, RING, slope_one)
    term_one(0, lambda h: normed1[:, :, h * half:(h + 1) * half], joined1)
    plane[0].start()
    plane[1].forward()
    sums[0][0].wait_recv()
    via2[0] = (terms2[partner, 0].astype(F32) + via2[0].astype(F32)).astype(BF16)
    sums[0][2].start()
    plane[0].forward()

    def along_back(step, m):
        other = wrap(col + step)
        number = 16 + 4 * m + step
        return remote(
            mid.at[m, other], final1.at[m, col], col_send.at[number], col_recv.at[number],
            (level, row * RING + other, core),
        )

    for m in (1, 0):
        plane[m].finish()
        for part in range(2):
            mid[m, 2 * part:2 * part + 2] = plane[m].total(part).astype(BF16)
        for step in (2, 1, 3):
            along_back(step, m).start()
        final1[m, col] = mid[m, col]
    own_side = pl.ds(pl.multiple_of(side * hidden2, hidden2), hidden2)
    other_side = pl.ds(pl.multiple_of((1 - side) * hidden2, hidden2), hidden2)
    for m in (1, 0):
        sums[m][1].wait_recv()
        sum2[m, :, own_side] = (terms2[level, m].astype(F32) + near2[m].astype(F32)).astype(BF16)
        sums[m][2].wait_recv()
        sum2[m, :, other_side] = far2[m]
    keep = pltpu.make_async_copy(sum2, sum2_out, local_sem.at[0])
    keep.start()
    for m in (1, 0):
        for step in (1, 3, 2):
            along_back(step, m).wait_recv()
        for q in range(RING):
            sum1[m, :, q * hidden1:(q + 1) * hidden1] = final1[m, q]

    for copy in spread[0] + spread[1] + [column[0][2], column[1][2]] + sums[0] + sums[1]:
        copy.wait_send()
    for ring in gathers[0] + gathers[1] + [lifts] + plane + [swaps[2]] + shares:
        ring.drain()
    for step in range(RING):
        lift_pair(step).wait_send()
    for step in (1, 2, 3):
        along_back(step, 0).wait_send()
        along_back(step, 1).wait_send()
        give2(step).wait_send()
    give2(0).wait_send()
    to_partner(0).wait_send()
    to_partner(1).wait_send()
    swap_mean.wait_send()
    keep.wait()


def outer_step(scales, wt1, mom1, sum1, wt2, mom2, sum2, new_wt1, new_mom1, new_wt2, new_mom2):
    def step(scale, weights, moment, total, new_weights, new_moment):
        delta = total[...].astype(F32) / scale
        moved = MOMENTUM * moment[...] + delta
        new_moment[...] = moved
        new_weights[...] = weights[...] - OUTER_RATE * (delta + MOMENTUM * moved)

    step(scales[1], wt2, mom2, sum2, new_wt2, new_mom2)

    @pl.when(pl.program_id(0) == 0)
    def _():
        step(scales[0], wt1, mom1, sum1, new_wt1, new_mom1)


def local(docs, cot, route, doc_len, wt1, mom1, wt2, mom2):
    blocks, block, width = docs.shape
    groups = lax.axis_size("ba")
    levels = lax.axis_size("aa")
    slots = groups * SLOT
    count, lanes = slots * block, blocks * block
    hidden = wt1.shape[-1]
    whole = pl.BlockSpec(memory_space=pltpu.VMEM)
    anywhere = pl.BlockSpec(memory_space=pl.ANY)
    half, quarter = width // 2, width // 4
    per = count // groups
    small = width // 16
    hidden1, hidden2 = hidden // RING, hidden // 2

    def vmem(*sizes, kind=BF16):
        return pltpu.VMEM(sizes, kind)

    def dma(*sizes):
        return pltpu.SemaphoreType.DMA(sizes)

    hold = lanes // 2
    sum1, sum2 = pl.pallas_call(
        kernel,
        out_shape=(
            jax.ShapeDtypeStruct((2, small, hidden), BF16),
            jax.ShapeDtypeStruct((2, quarter, hidden), BF16),
        ),
        in_specs=[whole, whole, whole, whole, anywhere, anywhere],
        out_specs=[whole, anywhere],
        scratch_shapes=[
            vmem(count, lanes),
            vmem(2, quarter, hidden),
            vmem(2, small, hidden, kind=F32),
            vmem(2, 2, quarter, hidden2, kind=F32),
            vmem(RING, 2, small, hidden1),
            vmem(16, 2, small, hidden1),
            vmem(RING, 2, quarter, hidden2),
            vmem(RING, lanes, width),
            vmem(RING, lanes, hidden1),
            vmem(RING, lanes, hidden1),
            vmem(RING, 2, lanes, half),
            vmem(RING, lanes, half),
            vmem(2, hold, half),
            vmem(2, hold, half),
            vmem(4, hold, half),
            vmem(lanes, half),
            vmem(groups, per, half),
            vmem(2, 2, groups, per, half),
            vmem(2, 2, groups, per, half),
            vmem(groups, per, half),
            vmem(2, 2, quarter, hidden2),
            vmem(2, 2, quarter, hidden2),
            vmem(2, quarter, half),
            vmem(2, quarter, half),
            vmem(count, 128, kind=F32),
            vmem(count, 128, kind=F32),
            vmem(RING, 2, quarter, hidden2),
            vmem(2, quarter, hidden2),
            vmem(2, quarter, hidden2),
            vmem(2, quarter, hidden2),
            vmem(RING, 2, lanes, half),
            vmem(RING, 2, RING, small, hidden1),
            vmem(2, 2, 2, small, hidden1),
            vmem(2, 2, 2, small, hidden1),
            vmem(2, 4, 2, small, hidden1),
            vmem(2, RING, small, hidden1),
            vmem(2, RING, small, hidden1),
            dma(13, 6),
            dma(13, 6),
            dma(3, groups),
            dma(3, groups),
            dma(3, 2, groups),
            dma(3, 2, groups),
            dma(14),
            dma(14),
            dma(24),
            dma(24),
            dma(5),
        ],
        compiler_params=pltpu.CompilerParams(
            collective_id=0, has_side_effects=True, vmem_limit_bytes=VMEM_LIMIT
        ),
        name="window",
    )(docs.reshape(lanes, width), cot.reshape(lanes, width), route.T, doc_len[None], wt1[0], wt2[0])

    flat1, flat2 = (2 * small, hidden), (2 * quarter, hidden)
    steps = 4
    once = pl.BlockSpec(flat1, lambda number: (0, 0))
    part = pl.BlockSpec((flat2[0] // steps, hidden), lambda number: (number, 0))
    results = pl.pallas_call(
        functools.partial(outer_step, (groups, levels)),
        grid=(steps,),
        out_shape=[jax.ShapeDtypeStruct(flat, F32) for flat in (flat1, flat1, flat2, flat2)],
        in_specs=[once] * 3 + [part] * 3,
        out_specs=[once] * 2 + [part] * 2,
        compiler_params=pltpu.CompilerParams(vmem_limit_bytes=VMEM_LIMIT),
        name="outer",
    )(
        wt1.reshape(flat1),
        mom1.reshape(flat1),
        sum1.reshape(flat1),
        wt2.reshape(flat2),
        mom2.reshape(flat2),
        sum2.reshape(flat2),
    )
    return tuple(
        result.reshape(like.shape) for result, like in zip(results, (wt1, mom1, wt2, mom2))
    )


def solution(mesh):
    return jax.shard_map(
        local,
        mesh=mesh,
        in_specs=(
            P(("aa", "ba"), None, None),
            P(("aa", "ba"), None, None),
            P(("aa", "ba"), None),
            P(("aa", "ba")),
            P("aa", None, "ba", "ma"),
            P("aa", None, "ba", "ma"),
            P("ba", None, "aa", "ma"),
            P("ba", None, "aa", "ma"),
        ),
        out_specs=(
            P("aa", None, "ba", "ma"),
            P("aa", None, "ba", "ma"),
            P("ba", None, "aa", "ma"),
            P("ba", None, "aa", "ma"),
        ),
        check_vma=False,
    )
```

```python
import functools

import jax
import jax.numpy as jnp
from jax import lax
from jax.experimental import pallas as pl
from jax.experimental.pallas import tpu as pltpu
from jax.sharding import PartitionSpec as P

SLOT = 2
EPS = 1e-05
MOMENTUM = 0.9
OUTER_RATE = 0.7

MESH = pl.DeviceIdType.MESH
BF16 = jnp.bfloat16
F32 = jnp.float32
RING = 4
VMEM_LIMIT = 54 * 1024 * 1024


def dot(left, right, contract=(1, 0)):
    return lax.dot_general(
        left,
        right,
        (((contract[0],), (contract[1],)), ((), ())),
        preferred_element_type=F32,
    )


def wrap(index, size=RING):
    return lax.rem(index + size, size)


def remote(source, target, send, recv, device):
    return pltpu.make_async_remote_copy(
        src_ref=source,
        dst_ref=target,
        send_sem=send,
        recv_sem=recv,
        device_id=device,
        device_id_type=MESH,
    )


def each(first, last, step):
    def body(number, carry):
        step(number)
        return carry

    lax.fori_loop(first, last, body, 0)


class Gather:
    def __init__(self, own, land, rank, device, send, recv):
        up, down = wrap(rank + 1), wrap(rank - 1)

        def copy(number, source, target, to):
            return remote(source, target, send.at[number], recv.at[number], device(to))

        self.direct = [
            copy(0, own(0), land(rank, 0), up),
            copy(1, own(1), land(rank, 1), down),
            copy(2, own(1), land(rank, 1), up),
            copy(3, own(0), land(rank, 0), down),
        ]
        self.passed = [
            copy(4, land(down, 0), land(down, 0), up),
            copy(5, land(up, 1), land(up, 1), down),
        ]

    def start(self):
        for copy in self.direct:
            copy.start()

    def forward(self):
        for near, far in zip(self.direct[:2], self.passed):
            near.wait_recv()
            far.start()

    def near(self):
        for copy in self.direct[2:]:
            copy.wait_recv()

    def far(self):
        for copy in self.passed:
            copy.wait_recv()

    def drain(self):
        for copy in self.direct + self.passed:
            copy.wait_send()


class Scatter:
    def __init__(self, own, bufs, rank, device, send, recv):
        up, down, far = wrap(rank + 1), wrap(rank - 1), wrap(rank + 2)
        through, summed, landed = bufs

        def copy(number, source, target, to):
            return remote(source, target, send.at[number], recv.at[number], device(to))

        self.first = [
            copy(0, own(far, 0), through.at[0], up),
            copy(1, own(far, 1), through.at[1], down),
            copy(2, own(up, 1), landed.at[1], up),
            copy(3, own(down, 0), landed.at[2], down),
        ]
        self.second = [
            copy(4, summed.at[0], landed.at[0], up),
            copy(5, summed.at[1], landed.at[3], down),
        ]
        self.through, self.summed, self.landed = through, summed, landed
        self.own, self.rank = own, rank

    def start(self):
        for copy in self.first:
            copy.start()

    def forward(self):
        for which in range(2):
            self.first[which].wait_recv()
            mine = self.own(wrap(self.rank + 1 - 2 * which), which)[...]
            total = mine.astype(F32) + self.through[which].astype(F32)
            self.summed[which] = total.astype(BF16)
            self.second[which].start()

    def finish(self):
        for copy in self.first[2:] + self.second:
            copy.wait_recv()

    def total(self, half):
        return self.own(self.rank, half)[...].astype(F32) + (
            self.landed[half].astype(F32) + self.landed[2 + half].astype(F32)
        )

    def drain(self):
        for copy in self.first + self.second:
            copy.wait_send()


class Exchange:
    def __init__(self, packed, land, place, send, recv):
        self.place, self.groups = place, packed.shape[0]
        self.packed, self.land, self.send, self.recv = packed, land, send, recv

    def copy(self, step):
        level, base, core = self.place
        target = lax.rem(base + step, self.groups)
        return remote(
            self.packed.at[target],
            self.land.at[base],
            self.send.at[step],
            self.recv.at[step],
            (level, target, core),
        )

    def start(self):
        each(1, self.groups, lambda step: self.copy(step).start())
        base = self.place[1]
        self.land[base] = self.packed[base]

    def wait(self, step):
        self.copy(step).wait_recv()

    def drain(self):
        each(1, self.groups, lambda step: self.copy(step).wait_send())


class Share:
    def __init__(self, exchange, rows, place, partner, sibling, send, recv, last_send, last_recv):
        core = place[2]
        self.exchange, self.groups = exchange, exchange.groups

        def copy(path, step):
            source = wrap(place[1] - step, self.groups)
            mine = rows.at[0, core, source]
            if path == 0:
                return remote(mine, mine, send.at[0, step], recv.at[0, step], sibling)
            return remote(mine, rows.at[1, core, source], send.at[1, step], recv.at[1, step], partner)

        self.copy = copy
        self.last = remote(rows.at[1, core], rows.at[1, core], last_send, last_recv, sibling)

    def turn(self):
        def step(number):
            self.copy(1, number).start()
            self.copy(0, number).start()

        def arrived(number):
            self.exchange.wait(number)
            step(number)

        step(0)
        each(1, self.groups, arrived)

    def own(self):
        each(0, self.groups, lambda step: self.copy(0, step).wait_recv())

    def partner(self):
        each(0, self.groups, lambda step: self.copy(1, step).wait_recv())
        self.last.start()

    def finish(self):
        self.last.wait_recv()

    def drain(self):
        def step(number):
            self.copy(0, number).wait_send()
            self.copy(1, number).wait_send()

        each(0, self.groups, step)
        self.last.wait_send()


def greet(devices):
    barrier = pltpu.get_barrier_semaphore()
    for device in devices:
        pl.semaphore_signal(barrier, inc=1, device_id=device, device_id_type=MESH)
    pl.semaphore_wait(barrier, len(devices))


def doc_of_row(lanes, docs):
    row = lax.broadcasted_iota(jnp.int32, (lanes, docs), 0) // (lanes // docs)
    return (row == lax.broadcasted_iota(jnp.int32, (lanes, docs), 1)).astype(F32)


def slot_matrix(route, pick):
    count, lanes = pick.shape
    docs = route.shape[1]
    block = lanes // docs
    spread = jnp.broadcast_to(route[...].astype(F32), (128, docs))
    by_row = dot(spread, doc_of_row(lanes, docs), (1, 1))[0:docs]
    target = dot(doc_of_row(docs, docs), spread, (1, 1))[:, 0:1]
    own = lax.broadcasted_iota(jnp.int32, (docs, lanes), 1)
    earlier = lax.broadcasted_iota(jnp.int32, (docs, lanes), 0) < own // block
    rank = jnp.sum(jnp.where((by_row == target) & earlier, 1.0, 0.0), axis=0, keepdims=True)
    place = (by_row[0:1] * SLOT + rank) * block + lax.rem(own[0:1], block).astype(F32)
    slots = lax.broadcasted_iota(jnp.int32, (count, lanes), 0).astype(F32)
    pick[...] = jnp.where(slots == place, 1.0, 0.0).astype(BF16)


def live_rows(doc_len, lanes):
    docs = doc_len.shape[1]
    lengths = jnp.broadcast_to(doc_len[...].astype(F32), (128, docs))
    lengths = dot(doc_of_row(lanes, docs), lengths, (1, 1))[:, 0:1]
    position = lax.rem(lax.broadcasted_iota(jnp.int32, (lanes, 1), 0), lanes // docs)
    return position.astype(F32) < lengths


def rms_of(square, width):
    return lax.rsqrt(square / width + EPS)


def kernel(
    docs, cot_docs, route, doc_len, wt1, wt2,
    sum1, sum2_out,
    pick, sum2,
    stage1, stage2, own1, weights1, weights2,
    normed1, act1, gate1, part1, joined1, through1, summed1, landed1, out1,
    packed, cot, rows, back,
    act2, slopes2, dn_sum, dn_far, mean_out, mean_in,
    terms2, near2, via2, far2,
    upstream, terms1, through_x, summed_x, landed_x, mid, final1,
    ring_send, ring_recv, swap_send, swap_recv, share_send, share_recv, pair_send, pair_recv,
    col_send, col_recv, local_sem,
):
    level, base, core = lax.axis_index("aa"), lax.axis_index("ba"), lax.axis_index("ma")
    row, col = base // RING, lax.rem(base, RING)
    lanes, width = docs.shape
    groups = packed.shape[0]
    count = groups * packed.shape[1]
    half, quarter = width // 2, width // 4
    block, deep = weights1.shape[2], weights2.shape[2]
    hidden1, hidden2 = weights1.shape[3], weights2.shape[3]
    tile = hidden2 // 2
    mate, partner = level + 1 - 2 * lax.rem(level, 2), RING - 1 - level
    across = RING - 1 - mate
    side = level // 2
    place = (level, base, core)
    sibling = (level, base, 1 - core)
    mate_chip, partner_chip = (mate, base, core), (partner, base, core)

    loads = [
        pltpu.make_async_copy(wt1, stage1, local_sem.at[0]),
    ] + [
        pltpu.make_async_copy(
            wt2.at[m, :, pl.ds(h * hidden2, hidden2)], stage2.at[h, m], local_sem.at[1 + 2 * m + h]
        )
        for m in range(2)
        for h in range(2)
    ]
    for load in loads:
        load.start()
    greet(
        [sibling, mate_chip, partner_chip]
        + [(level, lax.rem(base + step, groups), core) for step in range(1, groups)]
    )

    loads[0].wait()
    for q in range(RING):
        for m in range(2):
            own1[q, m] = stage1[m, :, q * hidden1:(q + 1) * hidden1].astype(BF16)
    weights1[base] = own1[col]

    def along(m, step):
        other = wrap(col + step)
        number = 4 * m + step
        return remote(
            own1.at[other, m],
            weights1.at[base, m],
            share_send.at[2, 1, number],
            share_recv.at[2, 1, number],
            (level, row * RING + other, core),
        )

    def gather_x(m, step, number):
        fixed = wrap(col + step)
        rows_of = lambda part: pl.ds(part * (block // 2), block // 2)
        land = lambda pos, part: weights1.at[pos * RING + fixed, m, rows_of(part)]
        own = (lambda part: own1.at[col, m, rows_of(part)]) if step == 0 else (lambda part: land(row, part))
        device = lambda pos: (level, pos * RING + col, core)
        return Gather(own, land, row, device, ring_send.at[number], ring_recv.at[number])

    spread = [[along(m, step) for step in (1, 3, 2)] for m in range(2)]
    gathers = [[gather_x(m, step, 4 * m + k) for k, step in enumerate((0, 3, 1, 2))] for m in range(2)]
    for m in range(2):
        for copy in spread[m]:
            copy.start()
        gathers[m][0].start()

    rows_half = lanes // 2
    rows_part = rows_half // 2
    on_y = lambda pos: (level, row * RING + pos, core)

    def doc_part(pos, part):
        return normed1.at[pos, pl.ds(pl.multiple_of(core * rows_half + part * rows_part, rows_part), rows_part)]

    documents = Gather(
        lambda part: docs.at[pl.ds(pl.multiple_of(core * rows_half + part * rows_part, rows_part), rows_part)],
        doc_part,
        col,
        on_y,
        ring_send.at[8],
        ring_recv.at[8],
    )
    def doc_pair(step):
        where = normed1.at[wrap(col + step), pl.ds(pl.multiple_of(core * rows_half, rows_half), rows_half)]
        return remote(where, where, pair_send.at[step], pair_recv.at[step], sibling)

    def down_z(m):
        return [
            remote(act2.at[1 - side, m], weights2.at[level, m], col_send.at[4 + m], col_recv.at[4 + m], partner_chip),
            remote(act2.at[side, m], weights2.at[level, m], col_send.at[6 + m], col_recv.at[6 + m], mate_chip),
            remote(weights2.at[partner, m], weights2.at[partner, m], col_send.at[8 + m], col_recv.at[8 + m], mate_chip),
        ]

    column = [down_z(m) for m in range(2)]
    for m in (1, 0):
        for h in range(2):
            loads[1 + 2 * m + h].wait()
            act2[h, m] = stage2[h, m].astype(BF16)
        column[m][0].start()
        column[m][1].start()
        weights2[level, m] = act2[side, m]

    left = pl.ds(pl.multiple_of(core * half, half), half)
    swaps = [
        Exchange(packed, land, place, swap_send.at[k], swap_recv.at[k])
        for k, land in enumerate((cot.at[0, core], rows.at[0, core], back))
    ]
    shares = [
        Share(
            swaps[k], buf, place, partner_chip, sibling,
            share_send.at[k], share_recv.at[k], pair_send.at[4 + k], pair_recv.at[4 + k],
        )
        for k, buf in enumerate((cot, rows))
    ]
    slot_matrix(route, pick)
    live = live_rows(doc_len, lanes)
    masked = jnp.where(live, cot_docs[:, left], jnp.zeros((lanes, half), BF16))
    packed[...] = dot(pick[...], masked).astype(BF16).reshape(packed.shape)

    for m in range(2):
        for k, copy in enumerate(spread[m]):
            copy.wait_recv()
            gathers[m][1 + k].start()
        if m == 0:
            documents.start()
        for gather in gathers[m][:3]:
            gather.forward()
        if m == 1:
            column[1][0].wait_recv()
            column[1][2].start()
        gathers[m][3].forward()
    swaps[0].start()
    documents.forward()
    documents.near()
    doc_pair(3).start()
    doc_pair(1).start()
    documents.far()
    doc_pair(2).start()
    normed1[col] = docs[...]
    documents.drain()
    for step in (1, 2, 3):
        doc_pair(step).wait()

    def normalize_one(number):
        floated = normed1[number].astype(F32)
        square = jnp.sum(floated * floated, axis=-1, keepdims=True)
        normed1[number] = (floated * rms_of(square, width)).astype(BF16)

    each(0, RING, normalize_one)
    for gather in gathers[0]:
        gather.near()
        gather.far()

    def matrix1(m):
        return weights1[:, m].reshape(width, hidden1)

    def give1(step):
        pos = wrap(col + step)
        return remote(
            part1.at[pos, 1 - core], joined1.at[pos], share_send.at[2, 0, step], share_recv.at[2, 0, step], sibling
        )

    def up_one(pos):
        pre = dot(normed1[pos], matrix1(0))
        sigma = jax.nn.sigmoid(pre)
        act1[pos] = (pre * sigma).astype(BF16)
        gate1[pos] = (sigma * (1.0 + pre * (1.0 - sigma))).astype(BF16)

    def down_one(step):
        pos = wrap(col + step)
        for number in range(2):
            h = lax.rem(1 - core + number, 2)
            piece = weights1[pl.ds(8 * h, 8), 1].reshape(half, hidden1)
            part1[pos, h] = dot(act1[pos], piece, (1, 1)).astype(BF16)
            if number == 0:
                give1(step).start()

    def join_one(step):
        pos = wrap(col + step)
        give1(step).wait_recv()
        joined1[pos] = (part1[pos, core].astype(F32) + joined1[pos].astype(F32)).astype(BF16)

    each(0, RING, up_one)
    shares[0].turn()
    for gather in gathers[1]:
        gather.near()
        gather.far()
    hold = lanes // 2
    reduce1 = Scatter(
        lambda pos, part: joined1.at[pos, pl.ds(part * hold, hold)],
        (through1, summed1, landed1),
        col,
        on_y,
        ring_send.at[9],
        ring_recv.at[9],
    )
    down_one(2)
    down_one(1)
    join_one(2)
    reduce1.first[0].start()
    reduce1.first[1].start()
    down_one(3)
    join_one(1)
    reduce1.first[2].start()
    down_one(0)
    join_one(3)
    reduce1.first[3].start()
    column[0][0].wait_recv()
    column[0][2].start()
    reduce1.forward()
    join_one(0)
    reduce1.finish()
    for part in range(2):
        where = slice(part * hold, (part + 1) * hold)
        out1[where] = (docs[where, left].astype(F32) + reduce1.total(part)).astype(BF16)
    swaps[0].drain()
    packed[...] = dot(pick[...], out1[...]).astype(BF16).reshape(packed.shape)
    swaps[1].start()
    shares[0].own()

    def flat(ref, path, h):
        return ref[path, h].reshape(count, half)

    def piece2(m, h, columns):
        return weights2[2 * h:2 * h + 2, m, :, columns].reshape(half, tile)

    def columns_of(number):
        return pl.ds(pl.multiple_of(number * tile, tile), tile)

    column[1][1].wait_recv()
    column[1][2].wait_recv()

    def incoming_tile(number):
        path, columns = number // 2, columns_of(lax.rem(number, 2))
        value = dot(flat(cot, path, 0), piece2(1, 0, columns)) + dot(
            flat(cot, path, 1), piece2(1, 1, columns)
        )
        stage2[path, :, :, columns] = value.reshape(2, deep, tile)

    each(0, 2, incoming_tile)
    reduce1.drain()
    for step in range(RING):
        give1(step).wait_send()
    shares[1].turn()
    shares[0].partner()
    shares[1].own()

    def normalize_two(path):
        square = sum(
            jnp.sum(jnp.square(flat(rows, path, h).astype(F32)), axis=-1, keepdims=True) for h in range(2)
        )
        factor = rms_of(square, width)
        for h in range(2):
            value = (flat(rows, path, h).astype(F32) * factor).astype(BF16)
            terms1[2 * path:2 * path + 2, h] = value.reshape(2, RING, block, half)
        return factor

    def normed2(path, h):
        return terms1[2 * path:2 * path + 2, h].reshape(count, half)

    def slope_tile(path, first, parts):
        where = slice(first, first + parts)

        def step(number):
            columns = columns_of(number)
            lefts = [
                terms1[2 * path + first:2 * path + first + parts, h].reshape(parts * deep, half) for h in range(2)
            ]
            pre = dot(lefts[0], piece2(0, 0, columns)) + dot(lefts[1], piece2(0, 1, columns))
            sigma = jax.nn.sigmoid(pre)
            incoming = stage2[path, where, :, columns].reshape(parts * deep, tile)
            slope = (incoming * sigma * (1.0 + pre * (1.0 - sigma))).astype(BF16)
            act2[path, where, :, columns] = (pre * sigma).astype(BF16).reshape(parts, deep, tile)
            slopes2[path, where, :, columns] = slope.reshape(parts, deep, tile)

        return step

    factor = normalize_two(0)
    column[0][1].wait_recv()
    column[0][2].wait_recv()
    for m in range(2):
        column[m][0].wait_send()
        column[m][1].wait_send()
    each(0, 2, slope_tile(0, 0, 2))
    shares[1].partner()
    shares[0].finish()
    each(2, 4, incoming_tile)
    shares[1].finish()
    normalize_two(1)

    def give2(spot):
        return remote(
            part1.at[spot, 1 - core], joined1.at[spot], share_send.at[2, 0, 4 + spot], share_recv.at[2, 0, 4 + spot], sibling
        )

    def dn_tiles(path, first, parts):
        for number in range(2):
            h = lax.rem(1 - core + number, 2)
            piece = weights2[pl.ds(2 * h, 2), 0].reshape(half, hidden2)
            left2 = slopes2[path, first:first + parts].reshape(parts * deep, hidden2)
            value = dot(left2, piece, (1, 1)).astype(BF16)
            part1[2 * path + first:2 * path + first + parts, h] = value.reshape(parts, deep, half)
            if number == 0:
                for spot in range(2 * path + first, 2 * path + first + parts):
                    give2(spot).start()

    def dn_of(spot):
        return part1[spot, core].astype(F32) + joined1[spot].astype(F32)

    def to_partner(part):
        return remote(dn_sum.at[part], dn_far.at[part], pair_send.at[6 + part], pair_recv.at[6 + part], partner_chip)

    def dn_out(part):
        give2(2 + part).wait_recv()
        dn_sum[part] = dn_of(2 + part).astype(BF16)
        to_partner(part).start()

    each(0, 2, slope_tile(1, 0, 1))
    dn_tiles(1, 0, 1)
    each(0, 2, slope_tile(1, 1, 1))
    dn_out(0)
    dn_tiles(1, 1, 1)
    dn_out(1)
    dn_tiles(0, 0, 2)

    def term_tiles(m, lefts, right):
        def step(number):
            columns = columns_of(number)
            for h in range(2):
                value = sum(
                    dot(lefts(path, h), right[path, :, :, columns].reshape(count, tile), (0, 0))
                    for path in range(2)
                )
                terms2[2 * h:2 * h + 2, m, :, columns] = value.astype(BF16).reshape(2, deep, tile)

        each(0, 2, step)

    def sums_z(m):
        return [
            remote(terms2.at[across, m], via2.at[m], col_send.at[10 + m], col_recv.at[10 + m], mate_chip),
            remote(terms2.at[mate, m], near2.at[m], col_send.at[12 + m], col_recv.at[12 + m], mate_chip),
            remote(via2.at[m], far2.at[m], col_send.at[14 + m], col_recv.at[14 + m], partner_chip),
        ]

    sums = [sums_z(m) for m in range(2)]
    term_tiles(1, lambda path, h: flat(cot, path, h), act2)
    sums[1][0].start()
    sums[1][1].start()

    for part in range(2):
        give2(part).wait_recv()
        to_partner(part).wait_recv()

    def pieces():
        value = jnp.concatenate([dn_of(part) + dn_far[part].astype(F32) for part in range(2)], axis=0)
        return flat(rows, 0, core).astype(F32) * factor, value

    normed, value = pieces()
    mean = jnp.sum(value * normed, axis=-1, keepdims=True)
    mean_out[...] = jnp.broadcast_to(mean, mean_out.shape)
    swap_mean = remote(mean_out, mean_in, pair_send.at[9], pair_recv.at[9], sibling)
    swap_mean.start()
    swap_mean.wait_recv()
    mean = (mean + mean_in[:, 0:1]) / width
    normed, value = pieces()
    result = flat(cot, 0, core).astype(F32) + factor * (value - normed * mean)
    swaps[1].drain()
    packed[...] = result.astype(BF16).reshape(packed.shape)
    swaps[2].start()
    term_tiles(0, normed2, slopes2)
    sums[0][0].start()
    sums[0][1].start()
    sums[1][0].wait_recv()
    via2[1] = (terms2[partner, 1].astype(F32) + via2[1].astype(F32)).astype(BF16)
    sums[1][2].start()

    each(1, groups, swaps[2].wait)
    upstream[col, core] = dot(pick[...], back[...].reshape(count, half), (0, 0)).astype(BF16)
    lifts = Gather(
        lambda part: upstream.at[col, core, pl.ds(part * hold, hold)],
        lambda pos, part: upstream.at[pos, core, pl.ds(part * hold, hold)],
        col,
        on_y,
        ring_send.at[10],
        ring_recv.at[10],
    )
    lifts.start()

    def lift_pair(step):
        where = upstream.at[wrap(col + step), core]
        return remote(where, where, pair_send.at[10 + step], pair_recv.at[10 + step], sibling)

    lift_pair(0).start()
    lifts.forward()
    lifts.near()
    lift_pair(3).start()
    lift_pair(1).start()

    def slope_one(pos):
        incoming = dot(upstream[pos, 0], weights1[0:8, 1].reshape(half, hidden1)) + dot(
            upstream[pos, 1], weights1[8:16, 1].reshape(half, hidden1)
        )
        joined1[pos] = (incoming * gate1[pos].astype(F32)).astype(BF16)

    lifts.far()
    lift_pair(2).start()
    for step in range(RING):
        lift_pair(step).wait_recv()

    def term_one(m, lefts, right):
        for h in range(2):
            value = dot(lefts(h).reshape(RING * lanes, half), right[...].reshape(RING * lanes, hidden1), (0, 0))
            terms1[2 * h:2 * h + 2, m] = value.astype(BF16).reshape(2, RING, block, hidden1)

    def scatter_x(m):
        return Scatter(
            lambda pos, part: terms1.at[pos, m, pl.ds(2 * part, 2)],
            (through_x.at[m], summed_x.at[m], landed_x.at[m]),
            row,
            lambda pos: (level, pos * RING + col, core),
            ring_send.at[11 + m],
            ring_recv.at[11 + m],
        )

    plane = [scatter_x(m) for m in range(2)]
    term_one(1, lambda h: upstream[:, h], act1)
    plane[1].start()
    each(0, RING, slope_one)
    term_one(0, lambda h: normed1[:, :, h * half:(h + 1) * half], joined1)
    plane[0].start()
    plane[1].forward()
    sums[0][0].wait_recv()
    via2[0] = (terms2[partner, 0].astype(F32) + via2[0].astype(F32)).astype(BF16)
    sums[0][2].start()
    plane[0].forward()

    def along_back(step, m):
        other = wrap(col + step)
        number = 16 + 4 * m + step
        return remote(
            mid.at[m, other], final1.at[m, col], col_send.at[number], col_recv.at[number],
            (level, row * RING + other, core),
        )

    for m in (1, 0):
        plane[m].finish()
        for part in range(2):
            mid[m, 2 * part:2 * part + 2] = plane[m].total(part).astype(BF16)
        for step in (2, 1, 3):
            along_back(step, m).start()
        final1[m, col] = mid[m, col]
    own_side = pl.ds(pl.multiple_of(side * hidden2, hidden2), hidden2)
    other_side = pl.ds(pl.multiple_of((1 - side) * hidden2, hidden2), hidden2)
    for m in (1, 0):
        sums[m][1].wait_recv()
        sum2[m, :, own_side] = (terms2[level, m].astype(F32) + near2[m].astype(F32)).astype(BF16)
        sums[m][2].wait_recv()
        sum2[m, :, other_side] = far2[m]
    keep = pltpu.make_async_copy(sum2, sum2_out, local_sem.at[0])
    keep.start()
    for m in (1, 0):
        for step in (1, 3, 2):
            along_back(step, m).wait_recv()
        for q in range(RING):
            sum1[m, :, q * hidden1:(q + 1) * hidden1] = final1[m, q]

    for copy in spread[0] + spread[1] + [column[0][2], column[1][2]] + sums[0] + sums[1]:
        copy.wait_send()
    for ring in gathers[0] + gathers[1] + [lifts] + plane + [swaps[2]] + shares:
        ring.drain()
    for step in range(RING):
        lift_pair(step).wait_send()
    for step in (1, 2, 3):
        along_back(step, 0).wait_send()
        along_back(step, 1).wait_send()
        give2(step).wait_send()
    give2(0).wait_send()
    to_partner(0).wait_send()
    to_partner(1).wait_send()
    swap_mean.wait_send()
    keep.wait()


def outer_step(scales, wt1, mom1, sum1, wt2, mom2, sum2, new_wt1, new_mom1, new_wt2, new_mom2):
    def step(scale, weights, moment, total, new_weights, new_moment):
        delta = total[...].astype(F32) / scale
        moved = MOMENTUM * moment[...] + delta
        new_moment[...] = moved
        new_weights[...] = weights[...] - OUTER_RATE * (delta + MOMENTUM * moved)

    step(scales[1], wt2, mom2, sum2, new_wt2, new_mom2)

    @pl.when(pl.program_id(0) == 0)
    def _():
        step(scales[0], wt1, mom1, sum1, new_wt1, new_mom1)


def local(docs, cot, route, doc_len, wt1, mom1, wt2, mom2):
    blocks, block, width = docs.shape
    groups = lax.axis_size("ba")
    levels = lax.axis_size("aa")
    slots = groups * SLOT
    count, lanes = slots * block, blocks * block
    hidden = wt1.shape[-1]
    whole = pl.BlockSpec(memory_space=pltpu.VMEM)
    anywhere = pl.BlockSpec(memory_space=pl.ANY)
    half, quarter = width // 2, width // 4
    per = count // groups
    small = width // 16
    hidden1, hidden2 = hidden // RING, hidden // 2

    def vmem(*sizes, kind=BF16):
        return pltpu.VMEM(sizes, kind)

    def dma(*sizes):
        return pltpu.SemaphoreType.DMA(sizes)

    hold = lanes // 2
    sum1, sum2 = pl.pallas_call(
        kernel,
        out_shape=(
            jax.ShapeDtypeStruct((2, small, hidden), BF16),
            jax.ShapeDtypeStruct((2, quarter, hidden), BF16),
        ),
        in_specs=[whole, whole, whole, whole, anywhere, anywhere],
        out_specs=[whole, anywhere],
        scratch_shapes=[
            vmem(count, lanes),
            vmem(2, quarter, hidden),
            vmem(2, small, hidden, kind=F32),
            vmem(2, 2, quarter, hidden2, kind=F32),
            vmem(RING, 2, small, hidden1),
            vmem(16, 2, small, hidden1),
            vmem(RING, 2, quarter, hidden2),
            vmem(RING, lanes, width),
            vmem(RING, lanes, hidden1),
            vmem(RING, lanes, hidden1),
            vmem(RING, 2, lanes, half),
            vmem(RING, lanes, half),
            vmem(2, hold, half),
            vmem(2, hold, half),
            vmem(4, hold, half),
            vmem(lanes, half),
            vmem(groups, per, half),
            vmem(2, 2, groups, per, half),
            vmem(2, 2, groups, per, half),
            vmem(groups, per, half),
            vmem(2, 2, quarter, hidden2),
            vmem(2, 2, quarter, hidden2),
            vmem(2, quarter, half),
            vmem(2, quarter, half),
            vmem(count, 128, kind=F32),
            vmem(count, 128, kind=F32),
            vmem(RING, 2, quarter, hidden2),
            vmem(2, quarter, hidden2),
            vmem(2, quarter, hidden2),
            vmem(2, quarter, hidden2),
            vmem(RING, 2, lanes, half),
            vmem(RING, 2, RING, small, hidden1),
            vmem(2, 2, 2, small, hidden1),
            vmem(2, 2, 2, small, hidden1),
            vmem(2, 4, 2, small, hidden1),
            vmem(2, RING, small, hidden1),
            vmem(2, RING, small, hidden1),
            dma(13, 6),
            dma(13, 6),
            dma(3, groups),
            dma(3, groups),
            dma(3, 2, groups),
            dma(3, 2, groups),
            dma(14),
            dma(14),
            dma(24),
            dma(24),
            dma(5),
        ],
        compiler_params=pltpu.CompilerParams(
            collective_id=0, has_side_effects=True, vmem_limit_bytes=VMEM_LIMIT
        ),
        cost_estimate=pl.CostEstimate(flops=100_000_000_000, bytes_accessed=40_000_000, transcendentals=2_000_000),
        name="window",
    )(docs.reshape(lanes, width), cot.reshape(lanes, width), route.T, doc_len[None], wt1[0], wt2[0])

    flat1, flat2 = (2 * small, hidden), (2 * quarter, hidden)
    steps = 4
    once = pl.BlockSpec(flat1, lambda number: (0, 0))
    part = pl.BlockSpec((flat2[0] // steps, hidden), lambda number: (number, 0))
    results = pl.pallas_call(
        functools.partial(outer_step, (groups, levels)),
        grid=(steps,),
        out_shape=[jax.ShapeDtypeStruct(flat, F32) for flat in (flat1, flat1, flat2, flat2)],
        in_specs=[once] * 3 + [part] * 3,
        out_specs=[once] * 2 + [part] * 2,
        compiler_params=pltpu.CompilerParams(vmem_limit_bytes=24 * 1024 * 1024),
        name="outer",
    )(
        wt1.reshape(flat1),
        mom1.reshape(flat1),
        sum1.reshape(flat1),
        wt2.reshape(flat2),
        mom2.reshape(flat2),
        sum2.reshape(flat2),
    )
    return tuple(
        result.reshape(like.shape) for result, like in zip(results, (wt1, mom1, wt2, mom2))
    )


def solution(mesh):
    return jax.shard_map(
        local,
        mesh=mesh,
        in_specs=(
            P(("aa", "ba"), None, None),
            P(("aa", "ba"), None, None),
            P(("aa", "ba"), None),
            P(("aa", "ba")),
            P("aa", None, "ba", "ma"),
            P("aa", None, "ba", "ma"),
            P("ba", None, "aa", "ma"),
            P("ba", None, "aa", "ma"),
        ),
        out_specs=(
            P("aa", None, "ba", "ma"),
            P("aa", None, "ba", "ma"),
            P("ba", None, "aa", "ma"),
            P("ba", None, "aa", "ma"),
        ),
        check_vma=False,
    )
```

```python
import functools

import jax
import jax.numpy as jnp
from jax import lax
from jax.experimental import pallas as pl
from jax.experimental.pallas import tpu as pltpu
from jax.sharding import PartitionSpec as P

SLOT = 2
EPS = 1e-05
MOMENTUM = 0.9
OUTER_RATE = 0.7

MESH = pl.DeviceIdType.MESH
BF16 = jnp.bfloat16
F32 = jnp.float32
RING = 4
VMEM_LIMIT = 56517632


def dot(left, right, contract=(1, 0)):
    return lax.dot_general(
        left,
        right,
        (((contract[0],), (contract[1],)), ((), ())),
        preferred_element_type=F32,
    )


def wrap(index, size=RING):
    return lax.rem(index + size, size)


def remote(source, target, send, recv, device):
    return pltpu.make_async_remote_copy(
        src_ref=source,
        dst_ref=target,
        send_sem=send,
        recv_sem=recv,
        device_id=device,
        device_id_type=MESH,
    )


def each(first, last, step):
    def body(number, carry):
        step(number)
        return carry

    lax.fori_loop(first, last, body, 0)


class Gather:
    def __init__(self, own, land, rank, device, send, recv):
        up, down = wrap(rank + 1), wrap(rank - 1)

        def copy(number, source, target, to):
            return remote(source, target, send.at[number], recv.at[number], device(to))

        self.direct = [
            copy(0, own(0), land(rank, 0), up),
            copy(1, own(1), land(rank, 1), down),
            copy(2, own(1), land(rank, 1), up),
            copy(3, own(0), land(rank, 0), down),
        ]
        self.passed = [
            copy(4, land(down, 0), land(down, 0), up),
            copy(5, land(up, 1), land(up, 1), down),
        ]

    def start(self):
        for copy in self.direct:
            copy.start()

    def forward(self):
        for near, far in zip(self.direct[:2], self.passed):
            near.wait_recv()
            far.start()

    def near(self):
        for copy in self.direct[2:]:
            copy.wait_recv()

    def far(self):
        for copy in self.passed:
            copy.wait_recv()

    def drain(self):
        for copy in self.direct + self.passed:
            copy.wait_send()


class Scatter:
    def __init__(self, own, bufs, rank, device, send, recv):
        up, down, far = wrap(rank + 1), wrap(rank - 1), wrap(rank + 2)
        through, summed, landed = bufs

        def copy(number, source, target, to):
            return remote(source, target, send.at[number], recv.at[number], device(to))

        self.first = [
            copy(0, own(far, 0), through.at[0], up),
            copy(1, own(far, 1), through.at[1], down),
            copy(2, own(up, 1), landed.at[1], up),
            copy(3, own(down, 0), landed.at[2], down),
        ]
        self.second = [
            copy(4, summed.at[0], landed.at[0], up),
            copy(5, summed.at[1], landed.at[3], down),
        ]
        self.through, self.summed, self.landed = through, summed, landed
        self.own, self.rank = own, rank

    def start(self):
        for copy in self.first:
            copy.start()

    def forward(self):
        for which in range(2):
            self.first[which].wait_recv()
            mine = self.own(wrap(self.rank + 1 - 2 * which), which)[...]
            total = mine.astype(F32) + self.through[which].astype(F32)
            self.summed[which] = total.astype(BF16)
            self.second[which].start()

    def finish(self):
        for copy in self.first[2:] + self.second:
            copy.wait_recv()

    def total(self, half):
        return self.own(self.rank, half)[...].astype(F32) + (
            self.landed[half].astype(F32) + self.landed[2 + half].astype(F32)
        )

    def drain(self):
        for copy in self.first + self.second:
            copy.wait_send()


class Exchange:
    def __init__(self, packed, land, place, send, recv):
        self.place, self.groups = place, packed.shape[0]
        self.packed, self.land, self.send, self.recv = packed, land, send, recv

    def copy(self, step):
        level, base, core = self.place
        target = lax.rem(base + step, self.groups)
        return remote(
            self.packed.at[target],
            self.land.at[base],
            self.send.at[step],
            self.recv.at[step],
            (level, target, core),
        )

    def start(self):
        each(1, self.groups, lambda step: self.copy(step).start())
        base = self.place[1]
        self.land[base] = self.packed[base]

    def wait(self, step):
        self.copy(step).wait_recv()

    def drain(self):
        each(1, self.groups, lambda step: self.copy(step).wait_send())


class Share:
    def __init__(self, exchange, rows, place, partner, sibling, send, recv, last_send, last_recv):
        core = place[2]
        self.exchange, self.groups = exchange, exchange.groups

        def copy(path, step):
            source = wrap(place[1] - step, self.groups)
            mine = rows.at[0, core, source]
            if path == 0:
                return remote(mine, mine, send.at[0, step], recv.at[0, step], sibling)
            return remote(mine, rows.at[1, core, source], send.at[1, step], recv.at[1, step], partner)

        self.copy = copy
        self.last = remote(rows.at[1, core], rows.at[1, core], last_send, last_recv, sibling)

    def turn(self):
        def step(number):
            self.copy(1, number).start()
            self.copy(0, number).start()

        def arrived(number):
            self.exchange.wait(number)
            step(number)

        step(0)
        each(1, self.groups, arrived)

    def own(self):
        each(0, self.groups, lambda step: self.copy(0, step).wait_recv())

    def partner(self):
        each(0, self.groups, lambda step: self.copy(1, step).wait_recv())
        self.last.start()

    def finish(self):
        self.last.wait_recv()

    def drain(self):
        def step(number):
            self.copy(0, number).wait_send()
            self.copy(1, number).wait_send()

        each(0, self.groups, step)
        self.last.wait_send()


def greet(devices):
    barrier = pltpu.get_barrier_semaphore()
    for device in devices:
        pl.semaphore_signal(barrier, inc=1, device_id=device, device_id_type=MESH)
    pl.semaphore_wait(barrier, len(devices))


def doc_of_row(lanes, docs):
    row = lax.broadcasted_iota(jnp.int32, (lanes, docs), 0) // (lanes // docs)
    return (row == lax.broadcasted_iota(jnp.int32, (lanes, docs), 1)).astype(F32)


def slot_matrix(route, pick):
    count, lanes = pick.shape
    docs = route.shape[1]
    block = lanes // docs
    spread = jnp.broadcast_to(route[...].astype(F32), (128, docs))
    by_row = dot(spread, doc_of_row(lanes, docs), (1, 1))[0:docs]
    target = dot(doc_of_row(docs, docs), spread, (1, 1))[:, 0:1]
    own = lax.broadcasted_iota(jnp.int32, (docs, lanes), 1)
    earlier = lax.broadcasted_iota(jnp.int32, (docs, lanes), 0) < own // block
    rank = jnp.sum(jnp.where((by_row == target) & earlier, 1.0, 0.0), axis=0, keepdims=True)
    place = (by_row[0:1] * SLOT + rank) * block + lax.rem(own[0:1], block).astype(F32)
    slots = lax.broadcasted_iota(jnp.int32, (count, lanes), 0).astype(F32)
    pick[...] = jnp.where(slots == place, 1.0, 0.0).astype(BF16)


def live_rows(doc_len, lanes):
    docs = doc_len.shape[1]
    lengths = jnp.broadcast_to(doc_len[...].astype(F32), (128, docs))
    lengths = dot(doc_of_row(lanes, docs), lengths, (1, 1))[:, 0:1]
    position = lax.rem(lax.broadcasted_iota(jnp.int32, (lanes, 1), 0), lanes // docs)
    return position.astype(F32) < lengths


def rms_of(square, width):
    return lax.rsqrt(square / width + EPS)


def kernel(
    docs, cot_docs, route, doc_len, wt1, wt2,
    sums_out,
    pick, sum_all,
    stage1, stage2, own1, weights1, weights2,
    normed1, act1, gate1, part1, joined1, through1, summed1, landed1, out1,
    packed, cot, rows, back,
    act2, slopes2, dn_sum, dn_far, mean_out, mean_in,
    terms2, near2, via2, far2,
    upstream, terms1, through_x, summed_x, landed_x, mid, final1,
    ring_send, ring_recv, swap_send, swap_recv, share_send, share_recv, pair_send, pair_recv,
    col_send, col_recv, local_sem,
):
    level, base, core = lax.axis_index("aa"), lax.axis_index("ba"), lax.axis_index("ma")
    row, col = base // RING, lax.rem(base, RING)
    lanes, width = docs.shape
    groups = packed.shape[0]
    count = groups * packed.shape[1]
    half, quarter = width // 2, width // 4
    block, deep = weights1.shape[2], weights2.shape[2]
    hidden1, hidden2 = weights1.shape[3], weights2.shape[3]
    tile = hidden2 // 2
    mate, partner = level + 1 - 2 * lax.rem(level, 2), RING - 1 - level
    across = RING - 1 - mate
    side = level // 2
    place = (level, base, core)
    sibling = (level, base, 1 - core)
    mate_chip, partner_chip = (mate, base, core), (partner, base, core)

    loads = [
        pltpu.make_async_copy(wt1, stage1, local_sem.at[0]),
    ] + [
        pltpu.make_async_copy(
            wt2.at[m, :, pl.ds(h * hidden2, hidden2)], stage2.at[h, m], local_sem.at[1 + 2 * m + h]
        )
        for m in range(2)
        for h in range(2)
    ]
    for load in loads:
        load.start()
    greet(
        [sibling, mate_chip, partner_chip]
        + [(level, lax.rem(base + step, groups), core) for step in range(1, groups)]
    )

    loads[0].wait()
    for q in range(RING):
        for m in range(2):
            own1[q, m] = stage1[m, :, q * hidden1:(q + 1) * hidden1].astype(BF16)
    weights1[base] = own1[col]

    def along(m, step):
        other = wrap(col + step)
        number = 4 * m + step
        return remote(
            own1.at[other, m],
            weights1.at[base, m],
            share_send.at[2, 1, number],
            share_recv.at[2, 1, number],
            (level, row * RING + other, core),
        )

    def gather_x(m, step, number):
        fixed = wrap(col + step)
        rows_of = lambda part: pl.ds(part * (block // 2), block // 2)
        land = lambda pos, part: weights1.at[pos * RING + fixed, m, rows_of(part)]
        own = (lambda part: own1.at[col, m, rows_of(part)]) if step == 0 else (lambda part: land(row, part))
        device = lambda pos: (level, pos * RING + col, core)
        return Gather(own, land, row, device, ring_send.at[number], ring_recv.at[number])

    spread = [[along(m, step) for step in (1, 3, 2)] for m in range(2)]
    gathers = [[gather_x(m, step, 4 * m + k) for k, step in enumerate((0, 3, 1, 2))] for m in range(2)]
    for m in range(2):
        for copy in spread[m]:
            copy.start()
        gathers[m][0].start()

    rows_half = lanes // 2
    rows_part = rows_half // 2
    on_y = lambda pos: (level, row * RING + pos, core)

    def doc_part(pos, part):
        return normed1.at[pos, pl.ds(pl.multiple_of(core * rows_half + part * rows_part, rows_part), rows_part)]

    documents = Gather(
        lambda part: docs.at[pl.ds(pl.multiple_of(core * rows_half + part * rows_part, rows_part), rows_part)],
        doc_part,
        col,
        on_y,
        ring_send.at[8],
        ring_recv.at[8],
    )
    def doc_pair(step):
        where = normed1.at[wrap(col + step), pl.ds(pl.multiple_of(core * rows_half, rows_half), rows_half)]
        return remote(where, where, pair_send.at[step], pair_recv.at[step], sibling)

    def down_z(m):
        return [
            remote(act2.at[1 - side, m], weights2.at[level, m], col_send.at[4 + m], col_recv.at[4 + m], partner_chip),
            remote(act2.at[side, m], weights2.at[level, m], col_send.at[6 + m], col_recv.at[6 + m], mate_chip),
            remote(weights2.at[partner, m], weights2.at[partner, m], col_send.at[8 + m], col_recv.at[8 + m], mate_chip),
        ]

    column = [down_z(m) for m in range(2)]

    def cast_z(m):
        for h in range(2):
            loads[1 + 2 * m + h].wait()
            act2[h, m] = stage2[h, m].astype(BF16)
        column[m][0].start()
        column[m][1].start()
        weights2[level, m] = act2[side, m]

    left = pl.ds(pl.multiple_of(core * half, half), half)
    swaps = [
        Exchange(packed, land, place, swap_send.at[k], swap_recv.at[k])
        for k, land in enumerate((cot.at[0, core], rows.at[0, core], back))
    ]
    shares = [
        Share(
            swaps[k], buf, place, partner_chip, sibling,
            share_send.at[k], share_recv.at[k], pair_send.at[4 + k], pair_recv.at[4 + k],
        )
        for k, buf in enumerate((cot, rows))
    ]

    for m in range(2):
        for k, copy in enumerate(spread[m]):
            copy.wait_recv()
            gathers[m][1 + k].start()
        if m == 0:
            documents.start()
            cast_z(1)
    for gather in gathers[0][:3]:
        gather.forward()
    cast_z(0)
    gathers[0][3].forward()
    slot_matrix(route, pick)
    live = live_rows(doc_len, lanes)
    masked = jnp.where(live, cot_docs[:, left], jnp.zeros((lanes, half), BF16))
    packed[...] = dot(pick[...], masked).astype(BF16).reshape(packed.shape)
    for gather in gathers[1]:
        gather.forward()
    column[1][0].wait_recv()
    column[1][2].start()
    swaps[0].start()
    documents.forward()
    documents.near()
    doc_pair(3).start()
    doc_pair(1).start()
    documents.far()
    doc_pair(2).start()
    normed1[col] = docs[...]
    documents.drain()
    for step in (1, 2, 3):
        doc_pair(step).wait()

    def normalize_one(number):
        floated = normed1[number].astype(F32)
        square = jnp.sum(floated * floated, axis=-1, keepdims=True)
        normed1[number] = (floated * rms_of(square, width)).astype(BF16)

    each(0, RING, normalize_one)
    for gather in gathers[0]:
        gather.near()
        gather.far()

    def matrix1(m):
        return weights1[:, m].reshape(width, hidden1)

    def give1(step):
        pos = wrap(col + step)
        return remote(
            part1.at[pos, 1 - core], joined1.at[pos], share_send.at[2, 0, step], share_recv.at[2, 0, step], sibling
        )

    def up_one(pos):
        pre = dot(normed1[pos], matrix1(0))
        sigma = jax.nn.sigmoid(pre)
        act1[pos] = (pre * sigma).astype(BF16)
        gate1[pos] = (sigma * (1.0 + pre * (1.0 - sigma))).astype(BF16)

    def down_one(step):
        pos = wrap(col + step)
        for number in range(2):
            h = lax.rem(1 - core + number, 2)
            piece = weights1[pl.ds(8 * h, 8), 1].reshape(half, hidden1)
            part1[pos, h] = dot(act1[pos], piece, (1, 1)).astype(BF16)
            if number == 0:
                give1(step).start()

    def join_one(step):
        pos = wrap(col + step)
        give1(step).wait_recv()
        joined1[pos] = (part1[pos, core].astype(F32) + joined1[pos].astype(F32)).astype(BF16)

    each(0, RING, up_one)
    shares[0].turn()
    for gather in gathers[1]:
        gather.near()
        gather.far()
    hold = lanes // 2
    reduce1 = Scatter(
        lambda pos, part: joined1.at[pos, pl.ds(part * hold, hold)],
        (through1, summed1, landed1),
        col,
        on_y,
        ring_send.at[9],
        ring_recv.at[9],
    )
    down_one(2)
    down_one(1)
    join_one(2)
    reduce1.first[0].start()
    reduce1.first[1].start()
    down_one(3)
    join_one(1)
    reduce1.first[2].start()
    down_one(0)
    join_one(3)
    reduce1.first[3].start()
    column[0][0].wait_recv()
    column[0][2].start()
    reduce1.forward()
    join_one(0)
    reduce1.finish()
    for part in range(2):
        where = slice(part * hold, (part + 1) * hold)
        out1[where] = (docs[where, left].astype(F32) + reduce1.total(part)).astype(BF16)
    swaps[0].drain()
    packed[...] = dot(pick[...], out1[...]).astype(BF16).reshape(packed.shape)
    swaps[1].start()
    shares[0].own()

    def flat(ref, path, h):
        return ref[path, h].reshape(count, half)

    def piece2(m, h, columns):
        return weights2[2 * h:2 * h + 2, m, :, columns].reshape(half, tile)

    def columns_of(number):
        return pl.ds(pl.multiple_of(number * tile, tile), tile)

    column[1][1].wait_recv()
    column[1][2].wait_recv()

    def incoming_tile(number):
        path, columns = number // 2, columns_of(lax.rem(number, 2))
        value = dot(flat(cot, path, 0), piece2(1, 0, columns)) + dot(
            flat(cot, path, 1), piece2(1, 1, columns)
        )
        stage2[path, :, :, columns] = value.reshape(2, deep, tile)

    each(0, 2, incoming_tile)
    reduce1.drain()
    for step in range(RING):
        give1(step).wait_send()
    shares[1].turn()
    shares[0].partner()
    shares[1].own()

    def normalize_two(path):
        square = sum(
            jnp.sum(jnp.square(flat(rows, path, h).astype(F32)), axis=-1, keepdims=True) for h in range(2)
        )
        factor = rms_of(square, width)
        for h in range(2):
            value = (flat(rows, path, h).astype(F32) * factor).astype(BF16)
            terms1[2 * path:2 * path + 2, h] = value.reshape(2, RING, block, half)
        return factor

    def normed2(path, h):
        return terms1[2 * path:2 * path + 2, h].reshape(count, half)

    def slope_tile(path, first, parts):
        where = slice(first, first + parts)

        def step(number):
            columns = columns_of(number)
            lefts = [
                terms1[2 * path + first:2 * path + first + parts, h].reshape(parts * deep, half) for h in range(2)
            ]
            pre = dot(lefts[0], piece2(0, 0, columns)) + dot(lefts[1], piece2(0, 1, columns))
            sigma = jax.nn.sigmoid(pre)
            incoming = stage2[path, where, :, columns].reshape(parts * deep, tile)
            slope = (incoming * sigma * (1.0 + pre * (1.0 - sigma))).astype(BF16)
            act2[path, where, :, columns] = (pre * sigma).astype(BF16).reshape(parts, deep, tile)
            slopes2[path, where, :, columns] = slope.reshape(parts, deep, tile)

        return step

    factor = normalize_two(0)
    column[0][1].wait_recv()
    column[0][2].wait_recv()
    for m in range(2):
        column[m][0].wait_send()
        column[m][1].wait_send()
    each(0, 2, slope_tile(0, 0, 2))
    shares[1].partner()
    shares[0].finish()
    each(2, 4, incoming_tile)
    shares[1].finish()
    normalize_two(1)

    def give2(spot):
        return remote(
            part1.at[spot, 1 - core], joined1.at[spot], share_send.at[2, 0, 4 + spot], share_recv.at[2, 0, 4 + spot], sibling
        )

    def dn_tiles(path, first, parts):
        for number in range(2):
            h = lax.rem(1 - core + number, 2)
            piece = weights2[pl.ds(2 * h, 2), 0].reshape(half, hidden2)
            left2 = slopes2[path, first:first + parts].reshape(parts * deep, hidden2)
            value = dot(left2, piece, (1, 1)).astype(BF16)
            part1[2 * path + first:2 * path + first + parts, h] = value.reshape(parts, deep, half)
            if number == 0:
                for spot in range(2 * path + first, 2 * path + first + parts):
                    give2(spot).start()

    def dn_of(spot):
        return part1[spot, core].astype(F32) + joined1[spot].astype(F32)

    def to_partner(part):
        return remote(dn_sum.at[part], dn_far.at[part], pair_send.at[6 + part], pair_recv.at[6 + part], partner_chip)

    def dn_out(part):
        give2(2 + part).wait_recv()
        dn_sum[part] = dn_of(2 + part).astype(BF16)
        to_partner(part).start()

    each(0, 2, slope_tile(1, 0, 1))
    dn_tiles(1, 0, 1)
    each(0, 2, slope_tile(1, 1, 1))
    dn_out(0)
    dn_tiles(1, 1, 1)
    dn_out(1)
    dn_tiles(0, 0, 2)

    def term_tiles(m, lefts, right):
        def step(number):
            columns = columns_of(number)
            for h in range(2):
                value = sum(
                    dot(lefts(path, h), right[path, :, :, columns].reshape(count, tile), (0, 0))
                    for path in range(2)
                )
                terms2[2 * h:2 * h + 2, m, :, columns] = value.astype(BF16).reshape(2, deep, tile)

        each(0, 2, step)

    def sums_z(m):
        return [
            remote(terms2.at[across, m], via2.at[m], col_send.at[10 + m], col_recv.at[10 + m], mate_chip),
            remote(terms2.at[mate, m], near2.at[m], col_send.at[12 + m], col_recv.at[12 + m], mate_chip),
            remote(via2.at[m], far2.at[m], col_send.at[14 + m], col_recv.at[14 + m], partner_chip),
        ]

    sums = [sums_z(m) for m in range(2)]
    term_tiles(1, lambda path, h: flat(cot, path, h), act2)
    sums[1][0].start()
    sums[1][1].start()

    for part in range(2):
        give2(part).wait_recv()
        to_partner(part).wait_recv()

    def pieces():
        value = jnp.concatenate([dn_of(part) + dn_far[part].astype(F32) for part in range(2)], axis=0)
        return flat(rows, 0, core).astype(F32) * factor, value

    normed, value = pieces()
    mean = jnp.sum(value * normed, axis=-1, keepdims=True)
    mean_out[...] = jnp.broadcast_to(mean, mean_out.shape)
    swap_mean = remote(mean_out, mean_in, pair_send.at[9], pair_recv.at[9], sibling)
    swap_mean.start()
    swap_mean.wait_recv()
    mean = (mean + mean_in[:, 0:1]) / width
    normed, value = pieces()
    result = flat(cot, 0, core).astype(F32) + factor * (value - normed * mean)
    swaps[1].drain()
    packed[...] = result.astype(BF16).reshape(packed.shape)
    swaps[2].start()
    term_tiles(0, normed2, slopes2)
    sums[0][0].start()
    sums[0][1].start()
    sums[1][0].wait_recv()
    via2[1] = (terms2[partner, 1].astype(F32) + via2[1].astype(F32)).astype(BF16)
    sums[1][2].start()

    each(1, groups, swaps[2].wait)
    upstream[col, core] = dot(pick[...], back[...].reshape(count, half), (0, 0)).astype(BF16)
    lifts = Gather(
        lambda part: upstream.at[col, core, pl.ds(part * hold, hold)],
        lambda pos, part: upstream.at[pos, core, pl.ds(part * hold, hold)],
        col,
        on_y,
        ring_send.at[10],
        ring_recv.at[10],
    )
    lifts.start()

    def lift_pair(step):
        where = upstream.at[wrap(col + step), core]
        return remote(where, where, pair_send.at[10 + step], pair_recv.at[10 + step], sibling)

    lift_pair(0).start()
    lifts.forward()
    lifts.near()
    lift_pair(3).start()
    lift_pair(1).start()

    def slope_one(pos):
        incoming = dot(upstream[pos, 0], weights1[0:8, 1].reshape(half, hidden1)) + dot(
            upstream[pos, 1], weights1[8:16, 1].reshape(half, hidden1)
        )
        joined1[pos] = (incoming * gate1[pos].astype(F32)).astype(BF16)

    lifts.far()
    lift_pair(2).start()
    for step in range(RING):
        lift_pair(step).wait_recv()

    def term_one(m, lefts, right):
        for h in range(2):
            value = dot(lefts(h).reshape(RING * lanes, half), right[...].reshape(RING * lanes, hidden1), (0, 0))
            terms1[2 * h:2 * h + 2, m] = value.astype(BF16).reshape(2, RING, block, hidden1)

    def scatter_x(m):
        return Scatter(
            lambda pos, part: terms1.at[pos, m, pl.ds(2 * part, 2)],
            (through_x.at[m], summed_x.at[m], landed_x.at[m]),
            row,
            lambda pos: (level, pos * RING + col, core),
            ring_send.at[11 + m],
            ring_recv.at[11 + m],
        )

    plane = [scatter_x(m) for m in range(2)]
    term_one(1, lambda h: upstream[:, h], act1)
    plane[1].start()
    each(0, RING, slope_one)
    term_one(0, lambda h: normed1[:, :, h * half:(h + 1) * half], joined1)
    plane[0].start()
    plane[1].forward()
    sums[0][0].wait_recv()
    via2[0] = (terms2[partner, 0].astype(F32) + via2[0].astype(F32)).astype(BF16)
    sums[0][2].start()
    plane[0].forward()

    def along_back(step, m):
        other = wrap(col + step)
        number = 16 + 4 * m + step
        return remote(
            mid.at[m, other], final1.at[m, col], col_send.at[number], col_recv.at[number],
            (level, row * RING + other, core),
        )

    for m in (1, 0):
        plane[m].finish()
        for part in range(2):
            mid[m, 2 * part:2 * part + 2] = plane[m].total(part).astype(BF16)
        for step in (2, 1, 3):
            along_back(step, m).start()
        final1[m, col] = mid[m, col]
    own_side = pl.ds(pl.multiple_of(side * hidden2, hidden2), hidden2)
    other_side = pl.ds(pl.multiple_of((1 - side) * hidden2, hidden2), hidden2)
    for m in (1, 0):
        sums[m][1].wait_recv()
        sum_all[m, 0:deep, own_side] = (terms2[level, m].astype(F32) + near2[m].astype(F32)).astype(BF16)
        sums[m][2].wait_recv()
        sum_all[m, 0:deep, other_side] = far2[m]
    rows2, rows1 = pl.ds(0, deep), pl.ds(deep, block)
    keeps = [
        pltpu.make_async_copy(sum_all.at[:, part], sums_out.at[:, part], local_sem.at[k])
        for k, part in enumerate((rows2, rows1))
    ]
    keeps[0].start()
    for m in (1, 0):
        for step in (1, 3, 2):
            along_back(step, m).wait_recv()
        for q in range(RING):
            sum_all[m, deep:deep + block, q * hidden1:(q + 1) * hidden1] = final1[m, q]
    keeps[1].start()

    for copy in spread[0] + spread[1] + [column[0][2], column[1][2]] + sums[0] + sums[1]:
        copy.wait_send()
    for ring in gathers[0] + gathers[1] + [lifts] + plane + [swaps[2]] + shares:
        ring.drain()
    for step in range(RING):
        lift_pair(step).wait_send()
    for step in (1, 2, 3):
        along_back(step, 0).wait_send()
        along_back(step, 1).wait_send()
        give2(step).wait_send()
    give2(0).wait_send()
    to_partner(0).wait_send()
    to_partner(1).wait_send()
    swap_mean.wait_send()
    for keep in keeps:
        keep.wait()


def outer_step(scales, wt1, mom1, sum1, wt2, mom2, sum2, new_wt1, new_mom1, new_wt2, new_mom2):
    def step(scale, weights, moment, total, new_weights, new_moment):
        delta = total[...].astype(F32) / scale
        moved = MOMENTUM * moment[...] + delta
        new_moment[...] = moved
        new_weights[...] = weights[...] - OUTER_RATE * (delta + MOMENTUM * moved)

    step(scales[1], wt2, mom2, sum2, new_wt2, new_mom2)

    @pl.when((pl.program_id(0) == 0) & (pl.program_id(1) == 0))
    def _():
        step(scales[0], wt1, mom1, sum1, new_wt1, new_mom1)


def local(docs, cot, route, doc_len, wt1, mom1, wt2, mom2):
    blocks, block, width = docs.shape
    groups = lax.axis_size("ba")
    levels = lax.axis_size("aa")
    slots = groups * SLOT
    count, lanes = slots * block, blocks * block
    hidden = wt1.shape[-1]
    whole = pl.BlockSpec(memory_space=pltpu.VMEM)
    anywhere = pl.BlockSpec(memory_space=pl.ANY)
    half, quarter = width // 2, width // 4
    per = count // groups
    small = width // 16
    hidden1, hidden2 = hidden // RING, hidden // 2

    def vmem(*sizes, kind=BF16):
        return pltpu.VMEM(sizes, kind)

    def dma(*sizes):
        return pltpu.SemaphoreType.DMA(sizes)

    hold = lanes // 2
    sums = pl.pallas_call(
        kernel,
        out_shape=jax.ShapeDtypeStruct((2, quarter + small, hidden), BF16),
        in_specs=[whole, whole, whole, whole, anywhere, anywhere],
        out_specs=anywhere,
        scratch_shapes=[
            vmem(count, lanes),
            vmem(2, quarter + small, hidden),
            vmem(2, small, hidden, kind=F32),
            vmem(2, 2, quarter, hidden2, kind=F32),
            vmem(RING, 2, small, hidden1),
            vmem(16, 2, small, hidden1),
            vmem(RING, 2, quarter, hidden2),
            vmem(RING, lanes, width),
            vmem(RING, lanes, hidden1),
            vmem(RING, lanes, hidden1),
            vmem(RING, 2, lanes, half),
            vmem(RING, lanes, half),
            vmem(2, hold, half),
            vmem(2, hold, half),
            vmem(4, hold, half),
            vmem(lanes, half),
            vmem(groups, per, half),
            vmem(2, 2, groups, per, half),
            vmem(2, 2, groups, per, half),
            vmem(groups, per, half),
            vmem(2, 2, quarter, hidden2),
            vmem(2, 2, quarter, hidden2),
            vmem(2, quarter, half),
            vmem(2, quarter, half),
            vmem(count, 128, kind=F32),
            vmem(count, 128, kind=F32),
            vmem(RING, 2, quarter, hidden2),
            vmem(2, quarter, hidden2),
            vmem(2, quarter, hidden2),
            vmem(2, quarter, hidden2),
            vmem(RING, 2, lanes, half),
            vmem(RING, 2, RING, small, hidden1),
            vmem(2, 2, 2, small, hidden1),
            vmem(2, 2, 2, small, hidden1),
            vmem(2, 4, 2, small, hidden1),
            vmem(2, RING, small, hidden1),
            vmem(2, RING, small, hidden1),
            dma(13, 6),
            dma(13, 6),
            dma(3, groups),
            dma(3, groups),
            dma(3, 2, groups),
            dma(3, 2, groups),
            dma(14),
            dma(14),
            dma(24),
            dma(24),
            dma(5),
        ],
        compiler_params=pltpu.CompilerParams(
            collective_id=0, has_side_effects=True, vmem_limit_bytes=VMEM_LIMIT
        ),
        cost_estimate=pl.CostEstimate(flops=100_000_000_000, bytes_accessed=40_000_000, transcendentals=2_000_000),
        name="window",
    )(docs.reshape(lanes, width), cot.reshape(lanes, width), route.T, doc_len[None], wt1[0], wt2[0])

    steps = 2
    once = pl.BlockSpec((2, small, hidden), lambda m, number: (0, 0, 0))
    part = pl.BlockSpec((1, quarter // steps, hidden), lambda m, number: (m, number, 0))
    last = pl.BlockSpec((2, small, hidden), lambda m, number: (0, quarter // small, 0))
    like1, like2 = (jax.ShapeDtypeStruct((2, rows, hidden), F32) for rows in (small, quarter))
    results = pl.pallas_call(
        functools.partial(outer_step, (groups, levels)),
        grid=(2, steps),
        out_shape=[like1, like1, like2, like2],
        in_specs=[once, once, last, part, part, part],
        out_specs=[once, once, part, part],
        compiler_params=pltpu.CompilerParams(vmem_limit_bytes=24 * 1024 * 1024),
        name="outer",
    )(wt1[0], mom1[0], sums, wt2[0], mom2[0], sums)
    return tuple(result[None] for result in results)


def solution(mesh):
    return jax.shard_map(
        local,
        mesh=mesh,
        in_specs=(
            P(("aa", "ba"), None, None),
            P(("aa", "ba"), None, None),
            P(("aa", "ba"), None),
            P(("aa", "ba")),
            P("aa", None, "ba", "ma"),
            P("aa", None, "ba", "ma"),
            P("ba", None, "aa", "ma"),
            P("ba", None, "aa", "ma"),
        ),
        out_specs=(
            P("aa", None, "ba", "ma"),
            P("aa", None, "ba", "ma"),
            P("ba", None, "aa", "ma"),
            P("ba", None, "aa", "ma"),
        ),
        check_vma=False,
    )
```

```python
import functools

import jax
import jax.numpy as jnp
from jax import lax
from jax.experimental import pallas as pl
from jax.experimental.pallas import tpu as pltpu
from jax.sharding import PartitionSpec as P

SLOT = 2
EPS = 1e-05
MOMENTUM = 0.9
OUTER_RATE = 0.7

MESH = pl.DeviceIdType.MESH
BF16 = jnp.bfloat16
F32 = jnp.float32
RING = 4
VMEM_LIMIT = 54 * 1024 * 1024


def dot(left, right, contract=(1, 0)):
    return lax.dot_general(
        left,
        right,
        (((contract[0],), (contract[1],)), ((), ())),
        preferred_element_type=F32,
    )


def wrap(index, size=RING):
    return lax.rem(index + size, size)


def remote(source, target, send, recv, device):
    return pltpu.make_async_remote_copy(
        src_ref=source,
        dst_ref=target,
        send_sem=send,
        recv_sem=recv,
        device_id=device,
        device_id_type=MESH,
    )


def each(first, last, step):
    def body(number, carry):
        step(number)
        return carry

    lax.fori_loop(first, last, body, 0)


class Gather:
    def __init__(self, own, land, rank, device, send, recv):
        up, down = wrap(rank + 1), wrap(rank - 1)

        def copy(number, source, target, to):
            return remote(source, target, send.at[number], recv.at[number], device(to))

        self.direct = [
            copy(0, own(0), land(rank, 0), up),
            copy(1, own(1), land(rank, 1), down),
            copy(2, own(1), land(rank, 1), up),
            copy(3, own(0), land(rank, 0), down),
        ]
        self.passed = [
            copy(4, land(down, 0), land(down, 0), up),
            copy(5, land(up, 1), land(up, 1), down),
        ]

    def start(self):
        for copy in self.direct:
            copy.start()

    def forward(self):
        for near, far in zip(self.direct[:2], self.passed):
            near.wait_recv()
            far.start()

    def near(self):
        for copy in self.direct[2:]:
            copy.wait_recv()

    def far(self):
        for copy in self.passed:
            copy.wait_recv()

    def drain(self):
        for copy in self.direct + self.passed:
            copy.wait_send()


class Scatter:
    def __init__(self, own, bufs, rank, device, send, recv):
        up, down, far = wrap(rank + 1), wrap(rank - 1), wrap(rank + 2)
        through, summed, landed = bufs

        def copy(number, source, target, to):
            return remote(source, target, send.at[number], recv.at[number], device(to))

        self.first = [
            copy(0, own(far, 0), through.at[0], up),
            copy(1, own(far, 1), through.at[1], down),
            copy(2, own(up, 1), landed.at[1], up),
            copy(3, own(down, 0), landed.at[2], down),
        ]
        self.second = [
            copy(4, summed.at[0], landed.at[0], up),
            copy(5, summed.at[1], landed.at[3], down),
        ]
        self.through, self.summed, self.landed = through, summed, landed
        self.own, self.rank = own, rank

    def start(self):
        for copy in self.first:
            copy.start()

    def forward(self):
        for which in range(2):
            self.first[which].wait_recv()
            mine = self.own(wrap(self.rank + 1 - 2 * which), which)[...]
            total = mine.astype(F32) + self.through[which].astype(F32)
            self.summed[which] = total.astype(BF16)
            self.second[which].start()

    def finish(self):
        for copy in self.first[2:] + self.second:
            copy.wait_recv()

    def total(self, half):
        return self.own(self.rank, half)[...].astype(F32) + (
            self.landed[half].astype(F32) + self.landed[2 + half].astype(F32)
        )

    def drain(self):
        for copy in self.first + self.second:
            copy.wait_send()


class Exchange:
    def __init__(self, packed, land, place, send, recv):
        self.place, self.groups = place, packed.shape[0]
        self.packed, self.land, self.send, self.recv = packed, land, send, recv

    def copy(self, step):
        level, base, core = self.place
        target = lax.rem(base + step, self.groups)
        return remote(
            self.packed.at[target],
            self.land.at[base],
            self.send.at[step],
            self.recv.at[step],
            (level, target, core),
        )

    def start(self):
        each(1, self.groups, lambda step: self.copy(step).start())
        base = self.place[1]
        self.land[base] = self.packed[base]

    def wait(self, step):
        self.copy(step).wait_recv()

    def drain(self):
        each(1, self.groups, lambda step: self.copy(step).wait_send())


class Share:
    def __init__(self, exchange, rows, place, partner, sibling, send, recv, last_send, last_recv):
        core = place[2]
        self.exchange, self.groups = exchange, exchange.groups

        def copy(path, step):
            source = wrap(place[1] - step, self.groups)
            mine = rows.at[0, core, source]
            if path == 0:
                return remote(mine, mine, send.at[0, step], recv.at[0, step], sibling)
            return remote(mine, rows.at[1, core, source], send.at[1, step], recv.at[1, step], partner)

        self.copy = copy
        self.last = remote(rows.at[1, core], rows.at[1, core], last_send, last_recv, sibling)

    def turn(self):
        def step(number):
            self.copy(1, number).start()
            self.copy(0, number).start()

        def arrived(number):
            self.exchange.wait(number)
            step(number)

        step(0)
        each(1, self.groups, arrived)

    def own(self):
        each(0, self.groups, lambda step: self.copy(0, step).wait_recv())

    def partner(self):
        each(0, self.groups, lambda step: self.copy(1, step).wait_recv())
        self.last.start()

    def finish(self):
        self.last.wait_recv()

    def drain(self):
        def step(number):
            self.copy(0, number).wait_send()
            self.copy(1, number).wait_send()

        each(0, self.groups, step)
        self.last.wait_send()


def greet(devices):
    barrier = pltpu.get_barrier_semaphore()
    for device in devices:
        pl.semaphore_signal(barrier, inc=1, device_id=device, device_id_type=MESH)
    pl.semaphore_wait(barrier, len(devices))


def doc_of_row(lanes, docs):
    row = lax.broadcasted_iota(jnp.int32, (lanes, docs), 0) // (lanes // docs)
    return (row == lax.broadcasted_iota(jnp.int32, (lanes, docs), 1)).astype(F32)


def slot_matrix(route, pick):
    count, lanes = pick.shape
    docs = route.shape[1]
    block = lanes // docs
    spread = jnp.broadcast_to(route[...].astype(F32), (128, docs))
    by_row = dot(spread, doc_of_row(lanes, docs), (1, 1))[0:docs]
    target = dot(doc_of_row(docs, docs), spread, (1, 1))[:, 0:1]
    own = lax.broadcasted_iota(jnp.int32, (docs, lanes), 1)
    earlier = lax.broadcasted_iota(jnp.int32, (docs, lanes), 0) < own // block
    rank = jnp.sum(jnp.where((by_row == target) & earlier, 1.0, 0.0), axis=0, keepdims=True)
    place = (by_row[0:1] * SLOT + rank) * block + lax.rem(own[0:1], block).astype(F32)
    slots = lax.broadcasted_iota(jnp.int32, (count, lanes), 0).astype(F32)
    pick[...] = jnp.where(slots == place, 1.0, 0.0).astype(BF16)


def live_rows(doc_len, lanes):
    docs = doc_len.shape[1]
    lengths = jnp.broadcast_to(doc_len[...].astype(F32), (128, docs))
    lengths = dot(doc_of_row(lanes, docs), lengths, (1, 1))[:, 0:1]
    position = lax.rem(lax.broadcasted_iota(jnp.int32, (lanes, 1), 0), lanes // docs)
    return position.astype(F32) < lengths


def rms_of(square, width):
    return lax.rsqrt(square / width + EPS)


def kernel(
    docs, cot_docs, route, doc_len, wt1, wt2,
    sums_out,
    pick, sum_all,
    stage1, stage2, own1, weights1, weights2,
    normed1, act1, gate1, part1, joined1, through1, summed1, landed1, out1,
    packed, cot, rows, back,
    act2, slopes2, dn_sum, dn_far, mean_out, mean_in,
    terms2, near2, via2, far2,
    upstream, terms1, through_x, summed_x, landed_x, mid, final1,
    ring_send, ring_recv, swap_send, swap_recv, share_send, share_recv, pair_send, pair_recv,
    col_send, col_recv, local_sem,
):
    level, base, core = lax.axis_index("aa"), lax.axis_index("ba"), lax.axis_index("ma")
    row, col = base // RING, lax.rem(base, RING)
    lanes, width = docs.shape
    groups = packed.shape[0]
    count = groups * packed.shape[1]
    half, quarter = width // 2, width // 4
    block, deep = weights1.shape[2], weights2.shape[2]
    hidden1, hidden2 = weights1.shape[3], weights2.shape[3]
    tile = hidden2 // 2
    mate, partner = level + 1 - 2 * lax.rem(level, 2), RING - 1 - level
    across = RING - 1 - mate
    side = level // 2
    place = (level, base, core)
    sibling = (level, base, 1 - core)
    mate_chip, partner_chip = (mate, base, core), (partner, base, core)

    loads = [
        pltpu.make_async_copy(wt1, stage1, local_sem.at[0]),
    ] + [
        pltpu.make_async_copy(
            wt2.at[m, :, pl.ds(h * hidden2, hidden2)], stage2.at[h, m], local_sem.at[1 + 2 * m + h]
        )
        for m in range(2)
        for h in range(2)
    ]
    for load in loads:
        load.start()
    greet(
        [sibling, mate_chip, partner_chip]
        + [(level, lax.rem(base + step, groups), core) for step in range(1, groups)]
    )

    loads[0].wait()
    for q in range(RING):
        for m in range(2):
            own1[q, m] = stage1[m, :, q * hidden1:(q + 1) * hidden1].astype(BF16)
    weights1[base] = own1[col]

    def along(m, step):
        other = wrap(col + step)
        number = 4 * m + step
        return remote(
            own1.at[other, m],
            weights1.at[base, m],
            share_send.at[2, 1, number],
            share_recv.at[2, 1, number],
            (level, row * RING + other, core),
        )

    def gather_x(m, step, number):
        fixed = wrap(col + step)
        rows_of = lambda part: pl.ds(part * (block // 2), block // 2)
        land = lambda pos, part: weights1.at[pos * RING + fixed, m, rows_of(part)]
        own = (lambda part: own1.at[col, m, rows_of(part)]) if step == 0 else (lambda part: land(row, part))
        device = lambda pos: (level, pos * RING + col, core)
        return Gather(own, land, row, device, ring_send.at[number], ring_recv.at[number])

    spread = [[along(m, step) for step in (1, 3, 2)] for m in range(2)]
    gathers = [[gather_x(m, step, 4 * m + k) for k, step in enumerate((0, 3, 1, 2))] for m in range(2)]
    for m in range(2):
        for copy in spread[m]:
            copy.start()
        gathers[m][0].start()

    rows_half = lanes // 2
    rows_part = rows_half // 2
    on_y = lambda pos: (level, row * RING + pos, core)

    def doc_part(pos, part):
        return normed1.at[pos, pl.ds(pl.multiple_of(core * rows_half + part * rows_part, rows_part), rows_part)]

    documents = Gather(
        lambda part: docs.at[pl.ds(pl.multiple_of(core * rows_half + part * rows_part, rows_part), rows_part)],
        doc_part,
        col,
        on_y,
        ring_send.at[8],
        ring_recv.at[8],
    )
    def doc_pair(step):
        where = normed1.at[wrap(col + step), pl.ds(pl.multiple_of(core * rows_half, rows_half), rows_half)]
        return remote(where, where, pair_send.at[step], pair_recv.at[step], sibling)

    def down_z(m):
        return [
            remote(act2.at[1 - side, m], weights2.at[level, m], col_send.at[4 + m], col_recv.at[4 + m], partner_chip),
            remote(act2.at[side, m], weights2.at[level, m], col_send.at[6 + m], col_recv.at[6 + m], mate_chip),
            remote(weights2.at[partner, m], weights2.at[partner, m], col_send.at[8 + m], col_recv.at[8 + m], mate_chip),
        ]

    column = [down_z(m) for m in range(2)]
    for m in (1, 0):
        for h in range(2):
            loads[1 + 2 * m + h].wait()
            act2[h, m] = stage2[h, m].astype(BF16)
        column[m][0].start()
        column[m][1].start()
        weights2[level, m] = act2[side, m]

    left = pl.ds(pl.multiple_of(core * half, half), half)
    swaps = [
        Exchange(packed, land, place, swap_send.at[k], swap_recv.at[k])
        for k, land in enumerate((cot.at[0, core], rows.at[0, core], back))
    ]
    shares = [
        Share(
            swaps[k], buf, place, partner_chip, sibling,
            share_send.at[k], share_recv.at[k], pair_send.at[4 + k], pair_recv.at[4 + k],
        )
        for k, buf in enumerate((cot, rows))
    ]
    slot_matrix(route, pick)
    live = live_rows(doc_len, lanes)
    masked = jnp.where(live, cot_docs[:, left], jnp.zeros((lanes, half), BF16))
    packed[...] = dot(pick[...], masked).astype(BF16).reshape(packed.shape)

    for m in range(2):
        for k, copy in enumerate(spread[m]):
            copy.wait_recv()
            gathers[m][1 + k].start()
        if m == 0:
            documents.start()
        for gather in gathers[m][:3]:
            gather.forward()
        if m == 1:
            column[1][0].wait_recv()
            column[1][2].start()
        gathers[m][3].forward()
    swaps[0].start()

    def normalize_one(pos, source):
        floated = source.astype(F32)
        square = jnp.sum(floated * floated, axis=-1, keepdims=True)
        normed1[pos] = (floated * rms_of(square, width)).astype(BF16)

    normalize_one(col, docs[...])
    documents.forward()
    documents.near()
    doc_pair(3).start()
    doc_pair(1).start()
    for gather in gathers[0]:
        gather.near()
        gather.far()

    def matrix1(m):
        return weights1[:, m].reshape(width, hidden1)

    def give1(step):
        pos = wrap(col + step)
        return remote(
            part1.at[pos, 1 - core], joined1.at[pos], share_send.at[2, 0, step], share_recv.at[2, 0, step], sibling
        )

    def up_one(pos):
        pre = dot(normed1[pos], matrix1(0))
        sigma = jax.nn.sigmoid(pre)
        act1[pos] = (pre * sigma).astype(BF16)
        gate1[pos] = (sigma * (1.0 + pre * (1.0 - sigma))).astype(BF16)

    def down_one(step):
        pos = wrap(col + step)
        for number in range(2):
            h = lax.rem(1 - core + number, 2)
            piece = weights1[pl.ds(8 * h, 8), 1].reshape(half, hidden1)
            part1[pos, h] = dot(act1[pos], piece, (1, 1)).astype(BF16)
            if number == 0:
                give1(step).start()

    def join_one(step):
        pos = wrap(col + step)
        give1(step).wait_recv()
        joined1[pos] = (part1[pos, core].astype(F32) + joined1[pos].astype(F32)).astype(BF16)

    up_one(col)
    documents.far()
    doc_pair(2).start()
    documents.drain()
    for step in (3, 1, 2):
        pos = wrap(col + step)
        doc_pair(step).wait()
        normalize_one(pos, normed1[pos])
        up_one(pos)
    shares[0].turn()
    for gather in gathers[1]:
        gather.near()
        gather.far()
    hold = lanes // 2
    reduce1 = Scatter(
        lambda pos, part: joined1.at[pos, pl.ds(part * hold, hold)],
        (through1, summed1, landed1),
        col,
        on_y,
        ring_send.at[9],
        ring_recv.at[9],
    )
    down_one(2)
    down_one(1)
    join_one(2)
    reduce1.first[0].start()
    reduce1.first[1].start()
    down_one(3)
    join_one(1)
    reduce1.first[2].start()
    down_one(0)
    join_one(3)
    reduce1.first[3].start()
    column[0][0].wait_recv()
    column[0][2].start()
    reduce1.forward()
    join_one(0)
    reduce1.finish()
    for part in range(2):
        where = slice(part * hold, (part + 1) * hold)
        out1[where] = (docs[where, left].astype(F32) + reduce1.total(part)).astype(BF16)
    swaps[0].drain()
    packed[...] = dot(pick[...], out1[...]).astype(BF16).reshape(packed.shape)
    swaps[1].start()
    shares[0].own()

    def flat(ref, path, h):
        return ref[path, h].reshape(count, half)

    def piece2(m, h, columns):
        return weights2[2 * h:2 * h + 2, m, :, columns].reshape(half, tile)

    def columns_of(number):
        return pl.ds(pl.multiple_of(number * tile, tile), tile)

    column[1][1].wait_recv()
    column[1][2].wait_recv()

    def incoming_tile(number):
        path, columns = number // 2, columns_of(lax.rem(number, 2))
        value = dot(flat(cot, path, 0), piece2(1, 0, columns)) + dot(
            flat(cot, path, 1), piece2(1, 1, columns)
        )
        stage2[path, :, :, columns] = value.reshape(2, deep, tile)

    each(0, 2, incoming_tile)
    reduce1.drain()
    for step in range(RING):
        give1(step).wait_send()
    shares[1].turn()
    shares[0].partner()
    shares[1].own()

    def normalize_two(path):
        square = sum(
            jnp.sum(jnp.square(flat(rows, path, h).astype(F32)), axis=-1, keepdims=True) for h in range(2)
        )
        factor = rms_of(square, width)
        for h in range(2):
            value = (flat(rows, path, h).astype(F32) * factor).astype(BF16)
            terms1[2 * path:2 * path + 2, h] = value.reshape(2, RING, block, half)
        return factor

    def normed2(path, h):
        return terms1[2 * path:2 * path + 2, h].reshape(count, half)

    def slope_tile(path, first, parts):
        where = slice(first, first + parts)

        def step(number):
            columns = columns_of(number)
            lefts = [
                terms1[2 * path + first:2 * path + first + parts, h].reshape(parts * deep, half) for h in range(2)
            ]
            pre = dot(lefts[0], piece2(0, 0, columns)) + dot(lefts[1], piece2(0, 1, columns))
            sigma = jax.nn.sigmoid(pre)
            incoming = stage2[path, where, :, columns].reshape(parts * deep, tile)
            slope = (incoming * sigma * (1.0 + pre * (1.0 - sigma))).astype(BF16)
            act2[path, where, :, columns] = (pre * sigma).astype(BF16).reshape(parts, deep, tile)
            slopes2[path, where, :, columns] = slope.reshape(parts, deep, tile)

        return step

    factor = normalize_two(0)
    column[0][1].wait_recv()
    column[0][2].wait_recv()
    for m in range(2):
        column[m][0].wait_send()
        column[m][1].wait_send()
    each(0, 2, slope_tile(0, 0, 2))
    shares[1].partner()
    shares[0].finish()
    each(2, 4, incoming_tile)
    shares[1].finish()
    normalize_two(1)

    def give2(spot):
        return remote(
            part1.at[spot, 1 - core], joined1.at[spot], share_send.at[2, 0, 4 + spot], share_recv.at[2, 0, 4 + spot], sibling
        )

    def dn_tiles(path, first, parts):
        for number in range(2):
            h = lax.rem(1 - core + number, 2)
            piece = weights2[pl.ds(2 * h, 2), 0].reshape(half, hidden2)
            left2 = slopes2[path, first:first + parts].reshape(parts * deep, hidden2)
            value = dot(left2, piece, (1, 1)).astype(BF16)
            part1[2 * path + first:2 * path + first + parts, h] = value.reshape(parts, deep, half)
            if number == 0:
                for spot in range(2 * path + first, 2 * path + first + parts):
                    give2(spot).start()

    def dn_of(spot):
        return part1[spot, core].astype(F32) + joined1[spot].astype(F32)

    def to_partner(part):
        return remote(dn_sum.at[part], dn_far.at[part], pair_send.at[6 + part], pair_recv.at[6 + part], partner_chip)

    def dn_out(part):
        give2(2 + part).wait_recv()
        dn_sum[part] = dn_of(2 + part).astype(BF16)
        to_partner(part).start()

    each(0, 2, slope_tile(1, 0, 1))
    dn_tiles(1, 0, 1)
    each(0, 2, slope_tile(1, 1, 1))
    dn_out(0)
    dn_tiles(1, 1, 1)
    dn_out(1)
    dn_tiles(0, 0, 2)

    def term_tiles(m, lefts, right):
        def step(number):
            columns = columns_of(number)
            for h in range(2):
                value = sum(
                    dot(lefts(path, h), right[path, :, :, columns].reshape(count, tile), (0, 0))
                    for path in range(2)
                )
                terms2[2 * h:2 * h + 2, m, :, columns] = value.astype(BF16).reshape(2, deep, tile)

        each(0, 2, step)

    def sums_z(m):
        return [
            remote(terms2.at[across, m], via2.at[m], col_send.at[10 + m], col_recv.at[10 + m], mate_chip),
            remote(terms2.at[mate, m], near2.at[m], col_send.at[12 + m], col_recv.at[12 + m], mate_chip),
            remote(via2.at[m], far2.at[m], col_send.at[14 + m], col_recv.at[14 + m], partner_chip),
        ]

    sums = [sums_z(m) for m in range(2)]
    term_tiles(1, lambda path, h: flat(cot, path, h), act2)
    sums[1][0].start()
    sums[1][1].start()

    for part in range(2):
        give2(part).wait_recv()
        to_partner(part).wait_recv()

    def pieces():
        value = jnp.concatenate([dn_of(part) + dn_far[part].astype(F32) for part in range(2)], axis=0)
        return flat(rows, 0, core).astype(F32) * factor, value

    normed, value = pieces()
    mean = jnp.sum(value * normed, axis=-1, keepdims=True)
    mean_out[...] = jnp.broadcast_to(mean, mean_out.shape)
    swap_mean = remote(mean_out, mean_in, pair_send.at[9], pair_recv.at[9], sibling)
    swap_mean.start()
    swap_mean.wait_recv()
    mean = (mean + mean_in[:, 0:1]) / width
    normed, value = pieces()
    result = flat(cot, 0, core).astype(F32) + factor * (value - normed * mean)
    swaps[1].drain()
    packed[...] = result.astype(BF16).reshape(packed.shape)
    swaps[2].start()
    term_tiles(0, normed2, slopes2)
    sums[0][0].start()
    sums[0][1].start()
    sums[1][0].wait_recv()
    via2[1] = (terms2[partner, 1].astype(F32) + via2[1].astype(F32)).astype(BF16)
    sums[1][2].start()

    each(1, groups, swaps[2].wait)
    upstream[col, core] = dot(pick[...], back[...].reshape(count, half), (0, 0)).astype(BF16)
    lifts = Gather(
        lambda part: upstream.at[col, core, pl.ds(part * hold, hold)],
        lambda pos, part: upstream.at[pos, core, pl.ds(part * hold, hold)],
        col,
        on_y,
        ring_send.at[10],
        ring_recv.at[10],
    )
    lifts.start()

    def lift_pair(step):
        where = upstream.at[wrap(col + step), core]
        return remote(where, where, pair_send.at[10 + step], pair_recv.at[10 + step], sibling)

    lift_pair(0).start()
    lifts.forward()
    lifts.near()
    lift_pair(3).start()
    lift_pair(1).start()

    def slope_one(pos):
        incoming = dot(upstream[pos, 0], weights1[0:8, 1].reshape(half, hidden1)) + dot(
            upstream[pos, 1], weights1[8:16, 1].reshape(half, hidden1)
        )
        joined1[pos] = (incoming * gate1[pos].astype(F32)).astype(BF16)

    lifts.far()
    lift_pair(2).start()
    for step in range(RING):
        lift_pair(step).wait_recv()

    def term_one(m, lefts, right):
        for h in range(2):
            value = dot(lefts(h).reshape(RING * lanes, half), right[...].reshape(RING * lanes, hidden1), (0, 0))
            terms1[2 * h:2 * h + 2, m] = value.astype(BF16).reshape(2, RING, block, hidden1)

    def scatter_x(m):
        return Scatter(
            lambda pos, part: terms1.at[pos, m, pl.ds(2 * part, 2)],
            (through_x.at[m], summed_x.at[m], landed_x.at[m]),
            row,
            lambda pos: (level, pos * RING + col, core),
            ring_send.at[11 + m],
            ring_recv.at[11 + m],
        )

    plane = [scatter_x(m) for m in range(2)]
    term_one(1, lambda h: upstream[:, h], act1)
    plane[1].start()
    each(0, RING, slope_one)
    term_one(0, lambda h: normed1[:, :, h * half:(h + 1) * half], joined1)
    plane[0].start()
    plane[1].forward()
    sums[0][0].wait_recv()
    via2[0] = (terms2[partner, 0].astype(F32) + via2[0].astype(F32)).astype(BF16)
    sums[0][2].start()
    plane[0].forward()

    def along_back(step, m):
        other = wrap(col + step)
        number = 16 + 4 * m + step
        return remote(
            mid.at[m, other], final1.at[m, col], col_send.at[number], col_recv.at[number],
            (level, row * RING + other, core),
        )

    for m in (1, 0):
        plane[m].finish()
        for part in range(2):
            mid[m, 2 * part:2 * part + 2] = plane[m].total(part).astype(BF16)
        for step in (2, 1, 3):
            along_back(step, m).start()
        final1[m, col] = mid[m, col]
    own_side = pl.ds(pl.multiple_of(side * hidden2, hidden2), hidden2)
    other_side = pl.ds(pl.multiple_of((1 - side) * hidden2, hidden2), hidden2)
    for m in (1, 0):
        sums[m][1].wait_recv()
        sum_all[m, 0:deep, own_side] = (terms2[level, m].astype(F32) + near2[m].astype(F32)).astype(BF16)
        sums[m][2].wait_recv()
        sum_all[m, 0:deep, other_side] = far2[m]
    rows2, rows1 = pl.ds(0, deep), pl.ds(deep, block)
    keeps = [
        pltpu.make_async_copy(sum_all.at[:, part], sums_out.at[:, part], local_sem.at[k])
        for k, part in enumerate((rows2, rows1))
    ]
    keeps[0].start()
    for m in (1, 0):
        for step in (1, 3, 2):
            along_back(step, m).wait_recv()
        for q in range(RING):
            sum_all[m, deep:deep + block, q * hidden1:(q + 1) * hidden1] = final1[m, q]
    keeps[1].start()

    for copy in spread[0] + spread[1] + [column[0][2], column[1][2]] + sums[0] + sums[1]:
        copy.wait_send()
    for ring in gathers[0] + gathers[1] + [lifts] + plane + [swaps[2]] + shares:
        ring.drain()
    for step in range(RING):
        lift_pair(step).wait_send()
    for step in (1, 2, 3):
        along_back(step, 0).wait_send()
        along_back(step, 1).wait_send()
        give2(step).wait_send()
    give2(0).wait_send()
    to_partner(0).wait_send()
    to_partner(1).wait_send()
    swap_mean.wait_send()
    for keep in keeps:
        keep.wait()


def outer_step(scales, wt1, mom1, sum1, wt2, mom2, sum2, new_wt1, new_mom1, new_wt2, new_mom2):
    def step(scale, weights, moment, total, new_weights, new_moment):
        delta = total[...].astype(F32) / scale
        moved = MOMENTUM * moment[...] + delta
        new_moment[...] = moved
        new_weights[...] = weights[...] - OUTER_RATE * (delta + MOMENTUM * moved)

    step(scales[1], wt2, mom2, sum2, new_wt2, new_mom2)

    @pl.when((pl.program_id(0) == 0) & (pl.program_id(1) == 0))
    def _():
        step(scales[0], wt1, mom1, sum1, new_wt1, new_mom1)


def local(docs, cot, route, doc_len, wt1, mom1, wt2, mom2):
    blocks, block, width = docs.shape
    groups = lax.axis_size("ba")
    levels = lax.axis_size("aa")
    slots = groups * SLOT
    count, lanes = slots * block, blocks * block
    hidden = wt1.shape[-1]
    whole = pl.BlockSpec(memory_space=pltpu.VMEM)
    anywhere = pl.BlockSpec(memory_space=pl.ANY)
    half, quarter = width // 2, width // 4
    per = count // groups
    small = width // 16
    hidden1, hidden2 = hidden // RING, hidden // 2

    def vmem(*sizes, kind=BF16):
        return pltpu.VMEM(sizes, kind)

    def dma(*sizes):
        return pltpu.SemaphoreType.DMA(sizes)

    hold = lanes // 2
    sums = pl.pallas_call(
        kernel,
        out_shape=jax.ShapeDtypeStruct((2, quarter + small, hidden), BF16),
        in_specs=[whole, whole, whole, whole, anywhere, anywhere],
        out_specs=anywhere,
        scratch_shapes=[
            vmem(count, lanes),
            vmem(2, quarter + small, hidden),
            vmem(2, small, hidden, kind=F32),
            vmem(2, 2, quarter, hidden2, kind=F32),
            vmem(RING, 2, small, hidden1),
            vmem(16, 2, small, hidden1),
            vmem(RING, 2, quarter, hidden2),
            vmem(RING, lanes, width),
            vmem(RING, lanes, hidden1),
            vmem(RING, lanes, hidden1),
            vmem(RING, 2, lanes, half),
            vmem(RING, lanes, half),
            vmem(2, hold, half),
            vmem(2, hold, half),
            vmem(4, hold, half),
            vmem(lanes, half),
            vmem(groups, per, half),
            vmem(2, 2, groups, per, half),
            vmem(2, 2, groups, per, half),
            vmem(groups, per, half),
            vmem(2, 2, quarter, hidden2),
            vmem(2, 2, quarter, hidden2),
            vmem(2, quarter, half),
            vmem(2, quarter, half),
            vmem(count, 128, kind=F32),
            vmem(count, 128, kind=F32),
            vmem(RING, 2, quarter, hidden2),
            vmem(2, quarter, hidden2),
            vmem(2, quarter, hidden2),
            vmem(2, quarter, hidden2),
            vmem(RING, 2, lanes, half),
            vmem(RING, 2, RING, small, hidden1),
            vmem(2, 2, 2, small, hidden1),
            vmem(2, 2, 2, small, hidden1),
            vmem(2, 4, 2, small, hidden1),
            vmem(2, RING, small, hidden1),
            vmem(2, RING, small, hidden1),
            dma(13, 6),
            dma(13, 6),
            dma(3, groups),
            dma(3, groups),
            dma(3, 2, groups),
            dma(3, 2, groups),
            dma(14),
            dma(14),
            dma(24),
            dma(24),
            dma(5),
        ],
        compiler_params=pltpu.CompilerParams(
            collective_id=0, has_side_effects=True, vmem_limit_bytes=VMEM_LIMIT
        ),
        cost_estimate=pl.CostEstimate(flops=100_000_000_000, bytes_accessed=40_000_000, transcendentals=2_000_000),
        name="window",
    )(docs.reshape(lanes, width), cot.reshape(lanes, width), route.T, doc_len[None], wt1[0], wt2[0])

    steps = 2
    once = pl.BlockSpec((2, small, hidden), lambda m, number: (0, 0, 0))
    part = pl.BlockSpec((1, quarter // steps, hidden), lambda m, number: (m, number, 0))
    last = pl.BlockSpec((2, small, hidden), lambda m, number: (0, quarter // small, 0))
    like1, like2 = (jax.ShapeDtypeStruct((2, rows, hidden), F32) for rows in (small, quarter))
    results = pl.pallas_call(
        functools.partial(outer_step, (groups, levels)),
        grid=(2, steps),
        out_shape=[like1, like1, like2, like2],
        in_specs=[once, once, last, part, part, part],
        out_specs=[once, once, part, part],
        compiler_params=pltpu.CompilerParams(vmem_limit_bytes=24 * 1024 * 1024),
        name="outer",
    )(wt1[0], mom1[0], sums, wt2[0], mom2[0], sums)
    return tuple(result[None] for result in results)


def solution(mesh):
    return jax.shard_map(
        local,
        mesh=mesh,
        in_specs=(
            P(("aa", "ba"), None, None),
            P(("aa", "ba"), None, None),
            P(("aa", "ba"), None),
            P(("aa", "ba")),
            P("aa", None, "ba", "ma"),
            P("aa", None, "ba", "ma"),
            P("ba", None, "aa", "ma"),
            P("ba", None, "aa", "ma"),
        ),
        out_specs=(
            P("aa", None, "ba", "ma"),
            P("aa", None, "ba", "ma"),
            P("ba", None, "aa", "ma"),
            P("ba", None, "aa", "ma"),
        ),
        check_vma=False,
    )
```

```python
import functools

import jax
import jax.numpy as jnp
from jax import lax
from jax.experimental import pallas as pl
from jax.experimental.pallas import tpu as pltpu
from jax.sharding import PartitionSpec as P

SLOT = 2
EPS = 1e-05
MOMENTUM = 0.9
OUTER_RATE = 0.7

MESH = pl.DeviceIdType.MESH
BF16 = jnp.bfloat16
F32 = jnp.float32
RING = 4
VMEM_LIMIT = 54 * 1024 * 1024


def dot(left, right, contract=(1, 0)):
    return lax.dot_general(
        left,
        right,
        (((contract[0],), (contract[1],)), ((), ())),
        preferred_element_type=F32,
    )


def wrap(index, size=RING):
    return lax.rem(index + size, size)


def remote(source, target, send, recv, device):
    return pltpu.make_async_remote_copy(
        src_ref=source,
        dst_ref=target,
        send_sem=send,
        recv_sem=recv,
        device_id=device,
        device_id_type=MESH,
    )


def each(first, last, step):
    def body(number, carry):
        step(number)
        return carry

    lax.fori_loop(first, last, body, 0)


class Gather:
    def __init__(self, own, land, rank, device, send, recv):
        up, down = wrap(rank + 1), wrap(rank - 1)

        def copy(number, source, target, to):
            return remote(source, target, send.at[number], recv.at[number], device(to))

        self.direct = [
            copy(0, own(0), land(rank, 0), up),
            copy(1, own(1), land(rank, 1), down),
            copy(2, own(1), land(rank, 1), up),
            copy(3, own(0), land(rank, 0), down),
        ]
        self.passed = [
            copy(4, land(down, 0), land(down, 0), up),
            copy(5, land(up, 1), land(up, 1), down),
        ]

    def start(self):
        for copy in self.direct:
            copy.start()

    def forward(self):
        for near, far in zip(self.direct[:2], self.passed):
            near.wait_recv()
            far.start()

    def near(self):
        for copy in self.direct[2:]:
            copy.wait_recv()

    def far(self):
        for copy in self.passed:
            copy.wait_recv()

    def drain(self):
        for copy in self.direct + self.passed:
            copy.wait_send()


class Scatter:
    def __init__(self, own, bufs, rank, device, send, recv):
        up, down, far = wrap(rank + 1), wrap(rank - 1), wrap(rank + 2)
        through, summed, landed = bufs

        def copy(number, source, target, to):
            return remote(source, target, send.at[number], recv.at[number], device(to))

        self.first = [
            copy(0, own(far, 0), through.at[0], up),
            copy(1, own(far, 1), through.at[1], down),
            copy(2, own(up, 1), landed.at[1], up),
            copy(3, own(down, 0), landed.at[2], down),
        ]
        self.second = [
            copy(4, summed.at[0], landed.at[0], up),
            copy(5, summed.at[1], landed.at[3], down),
        ]
        self.through, self.summed, self.landed = through, summed, landed
        self.own, self.rank = own, rank

    def start(self):
        for copy in self.first:
            copy.start()

    def forward(self):
        for which in range(2):
            self.first[which].wait_recv()
            mine = self.own(wrap(self.rank + 1 - 2 * which), which)[...]
            total = mine.astype(F32) + self.through[which].astype(F32)
            self.summed[which] = total.astype(BF16)
            self.second[which].start()

    def finish(self):
        for copy in self.first[2:] + self.second:
            copy.wait_recv()

    def total(self, half):
        return self.own(self.rank, half)[...].astype(F32) + (
            self.landed[half].astype(F32) + self.landed[2 + half].astype(F32)
        )

    def drain(self):
        for copy in self.first + self.second:
            copy.wait_send()


class Exchange:
    def __init__(self, packed, land, place, send, recv, back=False):
        self.place, self.groups, self.back = place, packed.shape[0], back
        self.packed, self.land, self.send, self.recv = packed, land, send, recv

    def copy(self, step):
        level, base, core = self.place
        target = lax.rem(base + step, self.groups)
        return remote(
            self.packed.at[lax.rem(self.groups - step, self.groups) if self.back else target],
            self.land.at[base if self.back else step],
            self.send.at[step],
            self.recv.at[step],
            (level, target, core),
        )

    def start(self):
        each(1, self.groups, lambda step: self.copy(step).start())
        base = self.place[1]
        if self.back:
            self.land[base] = self.packed[0]
        else:
            self.land[0] = self.packed[base]

    def wait(self, step):
        self.copy(step).wait_recv()

    def drain(self):
        each(1, self.groups, lambda step: self.copy(step).wait_send())


class Share:
    def __init__(self, exchange, rows, place, partner, sibling, send, recv, last_send, last_recv):
        core = place[2]
        self.exchange, self.groups = exchange, exchange.groups

        def copy(path, step):
            mine = rows.at[0, core, step]
            if path == 0:
                return remote(mine, mine, send.at[0, step], recv.at[0, step], sibling)
            return remote(mine, rows.at[1, core, step], send.at[1, step], recv.at[1, step], partner)

        self.copy = copy
        self.count = self.groups // 2

        def last(part):
            where = rows.at[1, core, pl.ds(part * self.count, self.count)]
            return remote(where, where, last_send(part), last_recv(part), sibling)

        self.last = [last(part) for part in range(2)]

    def turn(self):
        def step(number):
            self.copy(1, number).start()
            self.copy(0, number).start()

        def arrived(number):
            self.exchange.wait(number)
            step(number)

        step(0)
        each(1, self.groups, arrived)

    def own(self):
        each(0, self.groups, lambda step: self.copy(0, step).wait_recv())

    def partner(self, part):
        first = part * self.count
        each(first, first + self.count, lambda step: self.copy(1, step).wait_recv())
        self.last[part].start()

    def finish(self, part):
        self.last[part].wait_recv()

    def drain(self):
        def step(number):
            self.copy(0, number).wait_send()
            self.copy(1, number).wait_send()

        each(0, self.groups, step)
        for last in self.last:
            last.wait_send()


def greet(devices):
    barrier = pltpu.get_barrier_semaphore()
    for device in devices:
        pl.semaphore_signal(barrier, inc=1, device_id=device, device_id_type=MESH)
    pl.semaphore_wait(barrier, len(devices))


def doc_of_row(lanes, docs):
    row = lax.broadcasted_iota(jnp.int32, (lanes, docs), 0) // (lanes // docs)
    return (row == lax.broadcasted_iota(jnp.int32, (lanes, docs), 1)).astype(F32)


def slot_matrix(route, pick):
    count, lanes = pick.shape
    docs = route.shape[1]
    block = lanes // docs
    spread = jnp.broadcast_to(route[...].astype(F32), (128, docs))
    by_row = dot(spread, doc_of_row(lanes, docs), (1, 1))[0:docs]
    target = dot(doc_of_row(docs, docs), spread, (1, 1))[:, 0:1]
    own = lax.broadcasted_iota(jnp.int32, (docs, lanes), 1)
    earlier = lax.broadcasted_iota(jnp.int32, (docs, lanes), 0) < own // block
    rank = jnp.sum(jnp.where((by_row == target) & earlier, 1.0, 0.0), axis=0, keepdims=True)
    place = (by_row[0:1] * SLOT + rank) * block + lax.rem(own[0:1], block).astype(F32)
    slots = lax.broadcasted_iota(jnp.int32, (count, lanes), 0).astype(F32)
    pick[...] = jnp.where(slots == place, 1.0, 0.0).astype(BF16)


def live_rows(doc_len, lanes):
    docs = doc_len.shape[1]
    lengths = jnp.broadcast_to(doc_len[...].astype(F32), (128, docs))
    lengths = dot(doc_of_row(lanes, docs), lengths, (1, 1))[:, 0:1]
    position = lax.rem(lax.broadcasted_iota(jnp.int32, (lanes, 1), 0), lanes // docs)
    return position.astype(F32) < lengths


def rms_of(square, width):
    return lax.rsqrt(square / width + EPS)


def kernel(
    docs, cot_docs, route, doc_len, wt1, wt2,
    sums_out,
    pick, sum_all,
    stage1, stage2, own1, weights1, weights2,
    normed1, act1, gate1, part1, joined1, through1, summed1, landed1, out1,
    packed, cot, rows, back,
    act2, slopes2, dn_sum, dn_far, mean_out, mean_in,
    terms2, near2, via2, far2,
    upstream, terms1, through_x, summed_x, landed_x, mid, final1,
    ring_send, ring_recv, swap_send, swap_recv, share_send, share_recv, pair_send, pair_recv,
    col_send, col_recv, local_sem,
):
    level, base, core = lax.axis_index("aa"), lax.axis_index("ba"), lax.axis_index("ma")
    row, col = base // RING, lax.rem(base, RING)
    lanes, width = docs.shape
    groups = packed.shape[0]
    count = groups * packed.shape[1]
    half, quarter = width // 2, width // 4
    block, deep = weights1.shape[2], weights2.shape[2]
    hidden1, hidden2 = weights1.shape[3], weights2.shape[3]
    tile = hidden2 // 2
    mate, partner = level + 1 - 2 * lax.rem(level, 2), RING - 1 - level
    across = RING - 1 - mate
    side = level // 2
    place = (level, base, core)
    sibling = (level, base, 1 - core)
    mate_chip, partner_chip = (mate, base, core), (partner, base, core)

    loads = [
        pltpu.make_async_copy(wt1, stage1, local_sem.at[0]),
    ] + [
        pltpu.make_async_copy(
            wt2.at[m, :, pl.ds(h * hidden2, hidden2)], stage2.at[h, m], local_sem.at[1 + 2 * m + h]
        )
        for m in range(2)
        for h in range(2)
    ]
    for load in loads:
        load.start()
    greet(
        [sibling, mate_chip, partner_chip]
        + [(level, lax.rem(base + step, groups), core) for step in range(1, groups)]
    )

    loads[0].wait()
    for q in range(RING):
        for m in range(2):
            own1[q, m] = stage1[m, :, q * hidden1:(q + 1) * hidden1].astype(BF16)
    weights1[base] = own1[col]

    def along(m, step):
        other = wrap(col + step)
        number = 4 * m + step
        return remote(
            own1.at[other, m],
            weights1.at[base, m],
            share_send.at[2, 1, number],
            share_recv.at[2, 1, number],
            (level, row * RING + other, core),
        )

    def gather_x(m, step, number):
        fixed = wrap(col + step)
        rows_of = lambda part: pl.ds(part * (block // 2), block // 2)
        land = lambda pos, part: weights1.at[pos * RING + fixed, m, rows_of(part)]
        own = (lambda part: own1.at[col, m, rows_of(part)]) if step == 0 else (lambda part: land(row, part))
        device = lambda pos: (level, pos * RING + col, core)
        return Gather(own, land, row, device, ring_send.at[number], ring_recv.at[number])

    spread = [[along(m, step) for step in (1, 3, 2)] for m in range(2)]
    gathers = [[gather_x(m, step, 4 * m + k) for k, step in enumerate((0, 3, 1, 2))] for m in range(2)]
    for m in range(2):
        for copy in spread[m]:
            copy.start()
        gathers[m][0].start()

    rows_half = lanes // 2
    rows_part = rows_half // 2
    on_y = lambda pos: (level, row * RING + pos, core)

    def doc_part(pos, part):
        return normed1.at[pos, pl.ds(pl.multiple_of(core * rows_half + part * rows_part, rows_part), rows_part)]

    documents = Gather(
        lambda part: docs.at[pl.ds(pl.multiple_of(core * rows_half + part * rows_part, rows_part), rows_part)],
        doc_part,
        col,
        on_y,
        ring_send.at[8],
        ring_recv.at[8],
    )
    def doc_pair(step):
        where = normed1.at[wrap(col + step), pl.ds(pl.multiple_of(core * rows_half, rows_half), rows_half)]
        return remote(where, where, pair_send.at[step], pair_recv.at[step], sibling)

    def down_z(m):
        return [
            remote(act2.at[1 - side, m], weights2.at[level, m], col_send.at[4 + m], col_recv.at[4 + m], partner_chip),
            remote(act2.at[side, m], weights2.at[level, m], col_send.at[6 + m], col_recv.at[6 + m], mate_chip),
            remote(weights2.at[partner, m], weights2.at[partner, m], col_send.at[8 + m], col_recv.at[8 + m], mate_chip),
        ]

    column = [down_z(m) for m in range(2)]
    for m in (1, 0):
        for h in range(2):
            loads[1 + 2 * m + h].wait()
            act2[h, m] = stage2[h, m].astype(BF16)
        column[m][0].start()
        column[m][1].start()
        weights2[level, m] = act2[side, m]

    left = pl.ds(pl.multiple_of(core * half, half), half)
    swaps = [
        Exchange(packed, land, place, swap_send.at[k], swap_recv.at[k], k == 2)
        for k, land in enumerate((cot.at[0, core], rows.at[0, core], back))
    ]
    shares = [
        Share(
            swaps[k], buf, place, partner_chip, sibling,
            share_send.at[k], share_recv.at[k],
            lambda part, spots=spots: pair_send.at[spots[part]], lambda part, spots=spots: pair_recv.at[spots[part]],
        )
        for k, (buf, spots) in enumerate(((cot, (4, 0)), (rows, (5, 8))))
    ]
    slot_matrix(route, pick)
    live = live_rows(doc_len, lanes)
    masked = jnp.where(live, cot_docs[:, left], jnp.zeros((lanes, half), BF16))
    packed[...] = dot(pick[...], masked).astype(BF16).reshape(packed.shape)

    for m in range(2):
        for k, copy in enumerate(spread[m]):
            copy.wait_recv()
            gathers[m][1 + k].start()
        if m == 0:
            documents.start()
        for gather in gathers[m][:3]:
            gather.forward()
        if m == 1:
            column[1][0].wait_recv()
            column[1][2].start()
        gathers[m][3].forward()
    swaps[0].start()

    def normalize_one(pos, source):
        floated = source.astype(F32)
        square = jnp.sum(floated * floated, axis=-1, keepdims=True)
        normed1[pos] = (floated * rms_of(square, width)).astype(BF16)

    normalize_one(col, docs[...])
    documents.forward()
    documents.near()
    doc_pair(3).start()
    doc_pair(1).start()
    for gather in gathers[0]:
        gather.near()
        gather.far()

    def matrix1(m):
        return weights1[:, m].reshape(width, hidden1)

    def give1(step):
        pos = wrap(col + step)
        return remote(
            part1.at[pos, 1 - core], joined1.at[pos], share_send.at[2, 0, step], share_recv.at[2, 0, step], sibling
        )

    def up_one(pos):
        pre = dot(normed1[pos], matrix1(0))
        sigma = jax.nn.sigmoid(pre)
        act1[pos] = (pre * sigma).astype(BF16)
        gate1[pos] = (sigma * (1.0 + pre * (1.0 - sigma))).astype(BF16)

    def down_one(step):
        pos = wrap(col + step)
        for number in range(2):
            h = lax.rem(1 - core + number, 2)
            piece = weights1[pl.ds(8 * h, 8), 1].reshape(half, hidden1)
            part1[pos, h] = dot(act1[pos], piece, (1, 1)).astype(BF16)
            if number == 0:
                give1(step).start()

    def join_one(step):
        pos = wrap(col + step)
        give1(step).wait_recv()
        joined1[pos] = (part1[pos, core].astype(F32) + joined1[pos].astype(F32)).astype(BF16)

    up_one(col)
    documents.far()
    doc_pair(2).start()
    documents.drain()
    for step in (3, 1, 2):
        pos = wrap(col + step)
        doc_pair(step).wait()
        normalize_one(pos, normed1[pos])
        up_one(pos)
    shares[0].turn()
    for gather in gathers[1]:
        gather.near()
        gather.far()
    hold = lanes // 2
    reduce1 = Scatter(
        lambda pos, part: joined1.at[pos, pl.ds(part * hold, hold)],
        (through1, summed1, landed1),
        col,
        on_y,
        ring_send.at[9],
        ring_recv.at[9],
    )
    down_one(2)
    down_one(1)
    join_one(2)
    reduce1.first[0].start()
    reduce1.first[1].start()
    down_one(3)
    join_one(1)
    reduce1.first[2].start()
    down_one(0)
    join_one(3)
    reduce1.first[3].start()
    column[0][0].wait_recv()
    column[0][2].start()
    reduce1.forward()
    join_one(0)
    reduce1.finish()
    for part in range(2):
        where = slice(part * hold, (part + 1) * hold)
        out1[where] = (docs[where, left].astype(F32) + reduce1.total(part)).astype(BF16)
    swaps[0].drain()
    packed[...] = dot(pick[...], out1[...]).astype(BF16).reshape(packed.shape)
    swaps[1].start()
    shares[0].own()
    shares[0].partner(0)
    shares[0].partner(1)

    def flat(ref, path, h):
        return ref[path, h].reshape(count, half)

    def piece2(m, h, columns):
        return weights2[2 * h:2 * h + 2, m, :, columns].reshape(half, tile)

    def columns_of(number):
        return pl.ds(pl.multiple_of(number * tile, tile), tile)

    column[1][1].wait_recv()
    column[1][2].wait_recv()

    def incoming_tile(number):
        path, columns = number // 2, columns_of(lax.rem(number, 2))
        value = dot(flat(cot, path, 0), piece2(1, 0, columns)) + dot(
            flat(cot, path, 1), piece2(1, 1, columns)
        )
        stage2[path, :, :, columns] = value.reshape(2, deep, tile)

    each(0, 2, incoming_tile)
    shares[0].finish(0)
    shares[0].finish(1)
    each(2, 4, incoming_tile)
    reduce1.drain()
    for step in range(RING):
        give1(step).wait_send()
    shares[1].turn()
    shares[1].own()
    shares[1].partner(0)

    def normalize_two(path, first, parts):
        each_part = groups // 2

        def pieces_of(h):
            where = slice(first * each_part, (first + parts) * each_part)
            return rows[path, h, where].reshape(parts * deep, half).astype(F32)

        square = sum(jnp.sum(jnp.square(pieces_of(h)), axis=-1, keepdims=True) for h in range(2))
        factor = rms_of(square, width)
        for h in range(2):
            value = (pieces_of(h) * factor).astype(BF16)
            terms1[2 * path + first:2 * path + first + parts, h] = value.reshape(parts, RING, block, half)
        return factor

    def normed2(path, h):
        return terms1[2 * path:2 * path + 2, h].reshape(count, half)

    def slope_tile(path, first, parts):
        where = slice(first, first + parts)

        def step(number):
            columns = columns_of(number)
            lefts = [
                terms1[2 * path + first:2 * path + first + parts, h].reshape(parts * deep, half) for h in range(2)
            ]
            pre = dot(lefts[0], piece2(0, 0, columns)) + dot(lefts[1], piece2(0, 1, columns))
            sigma = jax.nn.sigmoid(pre)
            incoming = stage2[path, where, :, columns].reshape(parts * deep, tile)
            slope = (incoming * sigma * (1.0 + pre * (1.0 - sigma))).astype(BF16)
            act2[path, where, :, columns] = (pre * sigma).astype(BF16).reshape(parts, deep, tile)
            slopes2[path, where, :, columns] = slope.reshape(parts, deep, tile)

        return step

    factor = normalize_two(0, 0, 2)
    column[0][1].wait_recv()
    column[0][2].wait_recv()
    for m in range(2):
        column[m][0].wait_send()
        column[m][1].wait_send()
    each(0, 2, slope_tile(0, 0, 2))

    def give2(spot):
        return remote(
            part1.at[spot, 1 - core], joined1.at[spot], share_send.at[2, 0, 4 + spot], share_recv.at[2, 0, 4 + spot], sibling
        )

    def dn_tiles(path, first, parts):
        for number in range(2):
            h = lax.rem(1 - core + number, 2)
            piece = weights2[pl.ds(2 * h, 2), 0].reshape(half, hidden2)
            left2 = slopes2[path, first:first + parts].reshape(parts * deep, hidden2)
            value = dot(left2, piece, (1, 1)).astype(BF16)
            part1[2 * path + first:2 * path + first + parts, h] = value.reshape(parts, deep, half)
            if number == 0:
                for spot in range(2 * path + first, 2 * path + first + parts):
                    give2(spot).start()

    def dn_of(spot):
        return part1[spot, core].astype(F32) + joined1[spot].astype(F32)

    def to_partner(part):
        return remote(dn_sum.at[part], dn_far.at[part], pair_send.at[6 + part], pair_recv.at[6 + part], partner_chip)

    def dn_out(part):
        give2(2 + part).wait_recv()
        dn_sum[part] = dn_of(2 + part).astype(BF16)
        to_partner(part).start()

    shares[1].finish(0)
    normalize_two(1, 0, 1)
    each(0, 2, slope_tile(1, 0, 1))
    dn_tiles(1, 0, 1)
    shares[1].partner(1)
    dn_out(0)
    shares[1].finish(1)
    normalize_two(1, 1, 1)
    each(0, 2, slope_tile(1, 1, 1))
    dn_tiles(1, 1, 1)
    dn_out(1)
    dn_tiles(0, 0, 2)

    def term_tiles(m, lefts, right):
        def step(number):
            columns = columns_of(number)
            for h in range(2):
                value = sum(
                    dot(lefts(path, h), right[path, :, :, columns].reshape(count, tile), (0, 0))
                    for path in range(2)
                )
                terms2[2 * h:2 * h + 2, m, :, columns] = value.astype(BF16).reshape(2, deep, tile)

        each(0, 2, step)

    def sums_z(m):
        return [
            remote(terms2.at[across, m], via2.at[m], col_send.at[10 + m], col_recv.at[10 + m], mate_chip),
            remote(terms2.at[mate, m], near2.at[m], col_send.at[12 + m], col_recv.at[12 + m], mate_chip),
            remote(via2.at[m], far2.at[m], col_send.at[14 + m], col_recv.at[14 + m], partner_chip),
        ]

    sums = [sums_z(m) for m in range(2)]
    term_tiles(1, lambda path, h: flat(cot, path, h), act2)
    sums[1][0].start()
    sums[1][1].start()

    for part in range(2):
        give2(part).wait_recv()
        to_partner(part).wait_recv()

    def pieces():
        value = jnp.concatenate([dn_of(part) + dn_far[part].astype(F32) for part in range(2)], axis=0)
        return flat(rows, 0, core).astype(F32) * factor, value

    normed, value = pieces()
    mean = jnp.sum(value * normed, axis=-1, keepdims=True)
    mean_out[...] = jnp.broadcast_to(mean, mean_out.shape)
    swap_mean = remote(mean_out, mean_in, pair_send.at[9], pair_recv.at[9], sibling)
    swap_mean.start()
    swap_mean.wait_recv()
    mean = (mean + mean_in[:, 0:1]) / width
    normed, value = pieces()
    result = flat(cot, 0, core).astype(F32) + factor * (value - normed * mean)
    swaps[1].drain()
    packed[...] = result.astype(BF16).reshape(packed.shape)
    swaps[2].start()
    term_tiles(0, normed2, slopes2)
    sums[0][0].start()
    sums[0][1].start()
    sums[1][0].wait_recv()
    via2[1] = (terms2[partner, 1].astype(F32) + via2[1].astype(F32)).astype(BF16)
    sums[1][2].start()

    each(1, groups, swaps[2].wait)
    upstream[col, core] = dot(pick[...], back[...].reshape(count, half), (0, 0)).astype(BF16)
    lifts = Gather(
        lambda part: upstream.at[col, core, pl.ds(part * hold, hold)],
        lambda pos, part: upstream.at[pos, core, pl.ds(part * hold, hold)],
        col,
        on_y,
        ring_send.at[10],
        ring_recv.at[10],
    )
    lifts.start()

    def lift_pair(step):
        where = upstream.at[wrap(col + step), core]
        return remote(where, where, pair_send.at[10 + step], pair_recv.at[10 + step], sibling)

    lift_pair(0).start()
    lifts.forward()
    lifts.near()
    lift_pair(3).start()
    lift_pair(1).start()

    def slope_one(pos):
        incoming = dot(upstream[pos, 0], weights1[0:8, 1].reshape(half, hidden1)) + dot(
            upstream[pos, 1], weights1[8:16, 1].reshape(half, hidden1)
        )
        joined1[pos] = (incoming * gate1[pos].astype(F32)).astype(BF16)

    lifts.far()
    lift_pair(2).start()
    for step in range(RING):
        lift_pair(step).wait_recv()

    def term_one(m, lefts, right):
        for h in range(2):
            value = dot(lefts(h).reshape(RING * lanes, half), right[...].reshape(RING * lanes, hidden1), (0, 0))
            terms1[2 * h:2 * h + 2, m] = value.astype(BF16).reshape(2, RING, block, hidden1)

    def scatter_x(m):
        return Scatter(
            lambda pos, part: terms1.at[pos, m, pl.ds(2 * part, 2)],
            (through_x.at[m], summed_x.at[m], landed_x.at[m]),
            row,
            lambda pos: (level, pos * RING + col, core),
            ring_send.at[11 + m],
            ring_recv.at[11 + m],
        )

    plane = [scatter_x(m) for m in range(2)]
    term_one(1, lambda h: upstream[:, h], act1)
    plane[1].start()
    each(0, RING, slope_one)
    term_one(0, lambda h: normed1[:, :, h * half:(h + 1) * half], joined1)
    plane[0].start()
    plane[1].forward()
    sums[0][0].wait_recv()
    via2[0] = (terms2[partner, 0].astype(F32) + via2[0].astype(F32)).astype(BF16)
    sums[0][2].start()
    plane[0].forward()

    def along_back(step, m):
        other = wrap(col + step)
        number = 16 + 4 * m + step
        return remote(
            mid.at[m, other], final1.at[m, col], col_send.at[number], col_recv.at[number],
            (level, row * RING + other, core),
        )

    for m in (1, 0):
        plane[m].finish()
        for part in range(2):
            mid[m, 2 * part:2 * part + 2] = plane[m].total(part).astype(BF16)
        for step in (2, 1, 3):
            along_back(step, m).start()
        final1[m, col] = mid[m, col]
    own_side = pl.ds(pl.multiple_of(side * hidden2, hidden2), hidden2)
    other_side = pl.ds(pl.multiple_of((1 - side) * hidden2, hidden2), hidden2)
    for m in (1, 0):
        sums[m][1].wait_recv()
        sum_all[m, 0:deep, own_side] = (terms2[level, m].astype(F32) + near2[m].astype(F32)).astype(BF16)
        sums[m][2].wait_recv()
        sum_all[m, 0:deep, other_side] = far2[m]
    rows2, rows1 = pl.ds(0, deep), pl.ds(deep, block)
    keeps = [
        pltpu.make_async_copy(sum_all.at[:, part], sums_out.at[:, part], local_sem.at[k])
        for k, part in enumerate((rows2, rows1))
    ]
    keeps[0].start()
    for m in (1, 0):
        for step in (1, 3, 2):
            along_back(step, m).wait_recv()
        for q in range(RING):
            sum_all[m, deep:deep + block, q * hidden1:(q + 1) * hidden1] = final1[m, q]
    keeps[1].start()

    for copy in spread[0] + spread[1] + [column[0][2], column[1][2]] + sums[0] + sums[1]:
        copy.wait_send()
    for ring in gathers[0] + gathers[1] + [lifts] + plane + [swaps[2]] + shares:
        ring.drain()
    for step in range(RING):
        lift_pair(step).wait_send()
    for step in (1, 2, 3):
        along_back(step, 0).wait_send()
        along_back(step, 1).wait_send()
        give2(step).wait_send()
    give2(0).wait_send()
    to_partner(0).wait_send()
    to_partner(1).wait_send()
    swap_mean.wait_send()
    for keep in keeps:
        keep.wait()


def outer_step(scales, wt1, mom1, sum1, wt2, mom2, sum2, new_wt1, new_mom1, new_wt2, new_mom2):
    def step(scale, weights, moment, total, new_weights, new_moment):
        delta = total[...].astype(F32) / scale
        moved = MOMENTUM * moment[...] + delta
        new_moment[...] = moved
        new_weights[...] = weights[...] - OUTER_RATE * (delta + MOMENTUM * moved)

    step(scales[1], wt2, mom2, sum2, new_wt2, new_mom2)

    @pl.when((pl.program_id(0) == 0) & (pl.program_id(1) == 0))
    def _():
        step(scales[0], wt1, mom1, sum1, new_wt1, new_mom1)


def local(docs, cot, route, doc_len, wt1, mom1, wt2, mom2):
    blocks, block, width = docs.shape
    groups = lax.axis_size("ba")
    levels = lax.axis_size("aa")
    slots = groups * SLOT
    count, lanes = slots * block, blocks * block
    hidden = wt1.shape[-1]
    whole = pl.BlockSpec(memory_space=pltpu.VMEM)
    anywhere = pl.BlockSpec(memory_space=pl.ANY)
    half, quarter = width // 2, width // 4
    per = count // groups
    small = width // 16
    hidden1, hidden2 = hidden // RING, hidden // 2

    def vmem(*sizes, kind=BF16):
        return pltpu.VMEM(sizes, kind)

    def dma(*sizes):
        return pltpu.SemaphoreType.DMA(sizes)

    hold = lanes // 2
    sums = pl.pallas_call(
        kernel,
        out_shape=jax.ShapeDtypeStruct((2, quarter + small, hidden), BF16),
        in_specs=[whole, whole, whole, whole, anywhere, anywhere],
        out_specs=anywhere,
        scratch_shapes=[
            vmem(count, lanes),
            vmem(2, quarter + small, hidden),
            vmem(2, small, hidden, kind=F32),
            vmem(2, 2, quarter, hidden2, kind=F32),
            vmem(RING, 2, small, hidden1),
            vmem(16, 2, small, hidden1),
            vmem(RING, 2, quarter, hidden2),
            vmem(RING, lanes, width),
            vmem(RING, lanes, hidden1),
            vmem(RING, lanes, hidden1),
            vmem(RING, 2, lanes, half),
            vmem(RING, lanes, half),
            vmem(2, hold, half),
            vmem(2, hold, half),
            vmem(4, hold, half),
            vmem(lanes, half),
            vmem(groups, per, half),
            vmem(2, 2, groups, per, half),
            vmem(2, 2, groups, per, half),
            vmem(groups, per, half),
            vmem(2, 2, quarter, hidden2),
            vmem(2, 2, quarter, hidden2),
            vmem(2, quarter, half),
            vmem(2, quarter, half),
            vmem(count, 128, kind=F32),
            vmem(count, 128, kind=F32),
            vmem(RING, 2, quarter, hidden2),
            vmem(2, quarter, hidden2),
            vmem(2, quarter, hidden2),
            vmem(2, quarter, hidden2),
            vmem(RING, 2, lanes, half),
            vmem(RING, 2, RING, small, hidden1),
            vmem(2, 2, 2, small, hidden1),
            vmem(2, 2, 2, small, hidden1),
            vmem(2, 4, 2, small, hidden1),
            vmem(2, RING, small, hidden1),
            vmem(2, RING, small, hidden1),
            dma(13, 6),
            dma(13, 6),
            dma(3, groups),
            dma(3, groups),
            dma(3, 2, groups),
            dma(3, 2, groups),
            dma(14),
            dma(14),
            dma(24),
            dma(24),
            dma(5),
        ],
        compiler_params=pltpu.CompilerParams(
            collective_id=0, has_side_effects=True, vmem_limit_bytes=VMEM_LIMIT
        ),
        cost_estimate=pl.CostEstimate(flops=100_000_000_000, bytes_accessed=40_000_000, transcendentals=2_000_000),
        name="window",
    )(docs.reshape(lanes, width), cot.reshape(lanes, width), route.T, doc_len[None], wt1[0], wt2[0])

    steps = 2
    once = pl.BlockSpec((2, small, hidden), lambda m, number: (0, 0, 0))
    part = pl.BlockSpec((1, quarter // steps, hidden), lambda m, number: (m, number, 0))
    last = pl.BlockSpec((2, small, hidden), lambda m, number: (0, quarter // small, 0))
    like1, like2 = (jax.ShapeDtypeStruct((2, rows, hidden), F32) for rows in (small, quarter))
    results = pl.pallas_call(
        functools.partial(outer_step, (groups, levels)),
        grid=(2, steps),
        out_shape=[like1, like1, like2, like2],
        in_specs=[once, once, last, part, part, part],
        out_specs=[once, once, part, part],
        compiler_params=pltpu.CompilerParams(vmem_limit_bytes=24 * 1024 * 1024),
        name="outer",
    )(wt1[0], mom1[0], sums, wt2[0], mom2[0], sums)
    return tuple(result[None] for result in results)


def solution(mesh):
    return jax.shard_map(
        local,
        mesh=mesh,
        in_specs=(
            P(("aa", "ba"), None, None),
            P(("aa", "ba"), None, None),
            P(("aa", "ba"), None),
            P(("aa", "ba")),
            P("aa", None, "ba", "ma"),
            P("aa", None, "ba", "ma"),
            P("ba", None, "aa", "ma"),
            P("ba", None, "aa", "ma"),
        ),
        out_specs=(
            P("aa", None, "ba", "ma"),
            P("aa", None, "ba", "ma"),
            P("ba", None, "aa", "ma"),
            P("ba", None, "aa", "ma"),
        ),
        check_vma=False,
    )
```

```python
import functools

import jax
import jax.numpy as jnp
from jax import lax
from jax.experimental import pallas as pl
from jax.experimental.pallas import tpu as pltpu
from jax.sharding import PartitionSpec as P

SLOT = 2
EPS = 1e-05
MOMENTUM = 0.9
OUTER_RATE = 0.7

MESH = pl.DeviceIdType.MESH
BF16 = jnp.bfloat16
F32 = jnp.float32
RING = 4
VMEM_LIMIT = 54 * 1024 * 1024


def dot(left, right, contract=(1, 0)):
    return lax.dot_general(
        left,
        right,
        (((contract[0],), (contract[1],)), ((), ())),
        preferred_element_type=F32,
    )


def wrap(index, size=RING):
    return lax.rem(index + size, size)


def remote(source, target, send, recv, device):
    return pltpu.make_async_remote_copy(
        src_ref=source,
        dst_ref=target,
        send_sem=send,
        recv_sem=recv,
        device_id=device,
        device_id_type=MESH,
    )


def each(first, last, step):
    def body(number, carry):
        step(number)
        return carry

    lax.fori_loop(first, last, body, 0)


class Gather:
    def __init__(self, own, land, rank, device, send, recv):
        up, down = wrap(rank + 1), wrap(rank - 1)

        def copy(number, source, target, to):
            return remote(source, target, send.at[number], recv.at[number], device(to))

        self.direct = [
            copy(0, own(0), land(rank, 0), up),
            copy(1, own(1), land(rank, 1), down),
            copy(2, own(1), land(rank, 1), up),
            copy(3, own(0), land(rank, 0), down),
        ]
        self.passed = [
            copy(4, land(down, 0), land(down, 0), up),
            copy(5, land(up, 1), land(up, 1), down),
        ]

    def start(self):
        for copy in self.direct:
            copy.start()

    def forward(self):
        for near, far in zip(self.direct[:2], self.passed):
            near.wait_recv()
            far.start()

    def near(self):
        for copy in self.direct[2:]:
            copy.wait_recv()

    def far(self):
        for copy in self.passed:
            copy.wait_recv()

    def drain(self):
        for copy in self.direct + self.passed:
            copy.wait_send()


class Scatter:
    def __init__(self, own, bufs, rank, device, send, recv):
        up, down, far = wrap(rank + 1), wrap(rank - 1), wrap(rank + 2)
        through, summed, landed = bufs

        def copy(number, source, target, to):
            return remote(source, target, send.at[number], recv.at[number], device(to))

        self.first = [
            copy(0, own(far, 0), through.at[0], up),
            copy(1, own(far, 1), through.at[1], down),
            copy(2, own(up, 1), landed.at[1], up),
            copy(3, own(down, 0), landed.at[2], down),
        ]
        self.second = [
            copy(4, summed.at[0], landed.at[0], up),
            copy(5, summed.at[1], landed.at[3], down),
        ]
        self.through, self.summed, self.landed = through, summed, landed
        self.own, self.rank = own, rank

    def start(self):
        for copy in self.first:
            copy.start()

    def forward(self):
        for which in range(2):
            self.first[which].wait_recv()
            mine = self.own(wrap(self.rank + 1 - 2 * which), which)[...]
            total = mine.astype(F32) + self.through[which].astype(F32)
            self.summed[which] = total.astype(BF16)
            self.second[which].start()

    def finish(self):
        for copy in self.first[2:] + self.second:
            copy.wait_recv()

    def total(self, half):
        return self.own(self.rank, half)[...].astype(F32) + (
            self.landed[half].astype(F32) + self.landed[2 + half].astype(F32)
        )

    def drain(self):
        for copy in self.first + self.second:
            copy.wait_send()


class Exchange:
    def __init__(self, packed, land, place, send, recv, back=False):
        self.place, self.groups, self.back = place, packed.shape[0], back
        self.packed, self.land, self.send, self.recv = packed, land, send, recv

    def copy(self, step):
        level, base, core = self.place
        target = lax.rem(base + step, self.groups)
        return remote(
            self.packed.at[lax.rem(self.groups - step, self.groups) if self.back else target],
            self.land.at[base if self.back else step],
            self.send.at[step],
            self.recv.at[step],
            (level, target, core),
        )

    def start(self):
        each(1, self.groups, lambda step: self.copy(step).start())
        base = self.place[1]
        self.land[0] = self.packed[base]

    def start_back(self, part):
        middle = self.groups // 2
        if part == 0:
            each(middle + 1, self.groups, lambda step: self.copy(step).start())
            self.land[self.place[1]] = self.packed[0]
        else:
            each(1, middle + 1, lambda step: self.copy(step).start())

    def wait(self, step):
        self.copy(step).wait_recv()

    def drain(self):
        each(1, self.groups, lambda step: self.copy(step).wait_send())


class Share:
    def __init__(self, exchange, rows, place, partner, sibling, send, recv, last_send, last_recv):
        core = place[2]
        self.exchange, self.groups = exchange, exchange.groups

        def copy(path, step):
            mine = rows.at[0, core, step]
            if path == 0:
                return remote(mine, mine, send.at[0, step], recv.at[0, step], sibling)
            return remote(mine, rows.at[1, core, step], send.at[1, step], recv.at[1, step], partner)

        self.copy = copy
        self.count = self.groups // 2

        def last(part):
            where = rows.at[1, core, pl.ds(part * self.count, self.count)]
            return remote(where, where, last_send(part), last_recv(part), sibling)

        self.last = [last(part) for part in range(2)]

    def turn(self):
        def step(number):
            self.copy(1, number).start()
            self.copy(0, number).start()

        def arrived(number):
            self.exchange.wait(number)
            step(number)

        step(0)
        each(1, self.groups, arrived)

    def own(self):
        each(0, self.groups, lambda step: self.copy(0, step).wait_recv())

    def partner(self, part):
        first = part * self.count
        each(first, first + self.count, lambda step: self.copy(1, step).wait_recv())
        self.last[part].start()

    def finish(self, part):
        self.last[part].wait_recv()

    def drain(self):
        def step(number):
            self.copy(0, number).wait_send()
            self.copy(1, number).wait_send()

        each(0, self.groups, step)
        for last in self.last:
            last.wait_send()


def greet(devices):
    barrier = pltpu.get_barrier_semaphore()
    for device in devices:
        pl.semaphore_signal(barrier, inc=1, device_id=device, device_id_type=MESH)
    pl.semaphore_wait(barrier, len(devices))


def doc_of_row(lanes, docs):
    row = lax.broadcasted_iota(jnp.int32, (lanes, docs), 0) // (lanes // docs)
    return (row == lax.broadcasted_iota(jnp.int32, (lanes, docs), 1)).astype(F32)


def slot_matrix(route, pick):
    count, lanes = pick.shape
    docs = route.shape[1]
    block = lanes // docs
    spread = jnp.broadcast_to(route[...].astype(F32), (128, docs))
    by_row = dot(spread, doc_of_row(lanes, docs), (1, 1))[0:docs]
    target = dot(doc_of_row(docs, docs), spread, (1, 1))[:, 0:1]
    own = lax.broadcasted_iota(jnp.int32, (docs, lanes), 1)
    earlier = lax.broadcasted_iota(jnp.int32, (docs, lanes), 0) < own // block
    rank = jnp.sum(jnp.where((by_row == target) & earlier, 1.0, 0.0), axis=0, keepdims=True)
    place = (by_row[0:1] * SLOT + rank) * block + lax.rem(own[0:1], block).astype(F32)
    slots = lax.broadcasted_iota(jnp.int32, (count, lanes), 0).astype(F32)
    pick[...] = jnp.where(slots == place, 1.0, 0.0).astype(BF16)


def live_rows(doc_len, lanes):
    docs = doc_len.shape[1]
    lengths = jnp.broadcast_to(doc_len[...].astype(F32), (128, docs))
    lengths = dot(doc_of_row(lanes, docs), lengths, (1, 1))[:, 0:1]
    position = lax.rem(lax.broadcasted_iota(jnp.int32, (lanes, 1), 0), lanes // docs)
    return position.astype(F32) < lengths


def rms_of(square, width):
    return lax.rsqrt(square / width + EPS)


def kernel(
    docs, cot_docs, route, doc_len, wt1, wt2,
    sums_out,
    pick, sum_all,
    stage1, stage2, own1, weights1, weights2,
    normed1, act1, gate1, part1, joined1, through1, summed1, landed1, out1,
    packed, cot, rows, back,
    act2, slopes2, dn_sum, dn_far, mean_out, mean_in,
    terms2, near2, via2, far2,
    upstream, terms1, through_x, summed_x, landed_x, mid, final1,
    ring_send, ring_recv, swap_send, swap_recv, share_send, share_recv, pair_send, pair_recv,
    col_send, col_recv, local_sem,
):
    level, base, core = lax.axis_index("aa"), lax.axis_index("ba"), lax.axis_index("ma")
    row, col = base // RING, lax.rem(base, RING)
    lanes, width = docs.shape
    groups = packed.shape[0]
    count = groups * packed.shape[1]
    half, quarter = width // 2, width // 4
    block, deep = weights1.shape[2], weights2.shape[2]
    hidden1, hidden2 = weights1.shape[3], weights2.shape[3]
    tile = hidden2 // 2
    mate, partner = level + 1 - 2 * lax.rem(level, 2), RING - 1 - level
    across = RING - 1 - mate
    side = level // 2
    place = (level, base, core)
    sibling = (level, base, 1 - core)
    mate_chip, partner_chip = (mate, base, core), (partner, base, core)

    loads = [
        pltpu.make_async_copy(wt1, stage1, local_sem.at[0]),
    ] + [
        pltpu.make_async_copy(
            wt2.at[m, :, pl.ds(h * hidden2, hidden2)], stage2.at[h, m], local_sem.at[1 + 2 * m + h]
        )
        for m in range(2)
        for h in range(2)
    ]
    for load in loads:
        load.start()
    greet(
        [sibling, mate_chip, partner_chip]
        + [(level, lax.rem(base + step, groups), core) for step in range(1, groups)]
    )

    loads[0].wait()
    for q in range(RING):
        for m in range(2):
            own1[q, m] = stage1[m, :, q * hidden1:(q + 1) * hidden1].astype(BF16)
    weights1[base] = own1[col]

    def along(m, step):
        other = wrap(col + step)
        number = 4 * m + step
        return remote(
            own1.at[other, m],
            weights1.at[base, m],
            share_send.at[2, 1, number],
            share_recv.at[2, 1, number],
            (level, row * RING + other, core),
        )

    def gather_x(m, step, number):
        fixed = wrap(col + step)
        rows_of = lambda part: pl.ds(part * (block // 2), block // 2)
        land = lambda pos, part: weights1.at[pos * RING + fixed, m, rows_of(part)]
        own = (lambda part: own1.at[col, m, rows_of(part)]) if step == 0 else (lambda part: land(row, part))
        device = lambda pos: (level, pos * RING + col, core)
        return Gather(own, land, row, device, ring_send.at[number], ring_recv.at[number])

    spread = [[along(m, step) for step in (1, 3, 2)] for m in range(2)]
    gathers = [[gather_x(m, step, 4 * m + k) for k, step in enumerate((0, 3, 1, 2))] for m in range(2)]
    for m in range(2):
        for copy in spread[m]:
            copy.start()
        gathers[m][0].start()

    rows_half = lanes // 2
    rows_part = rows_half // 2
    on_y = lambda pos: (level, row * RING + pos, core)

    def doc_part(pos, part):
        return normed1.at[pos, pl.ds(pl.multiple_of(core * rows_half + part * rows_part, rows_part), rows_part)]

    documents = Gather(
        lambda part: docs.at[pl.ds(pl.multiple_of(core * rows_half + part * rows_part, rows_part), rows_part)],
        doc_part,
        col,
        on_y,
        ring_send.at[8],
        ring_recv.at[8],
    )
    def doc_pair(step):
        where = normed1.at[wrap(col + step), pl.ds(pl.multiple_of(core * rows_half, rows_half), rows_half)]
        return remote(where, where, pair_send.at[step], pair_recv.at[step], sibling)

    def down_z(m):
        return [
            remote(act2.at[1 - side, m], weights2.at[level, m], col_send.at[4 + m], col_recv.at[4 + m], partner_chip),
            remote(act2.at[side, m], weights2.at[level, m], col_send.at[6 + m], col_recv.at[6 + m], mate_chip),
            remote(weights2.at[partner, m], weights2.at[partner, m], col_send.at[8 + m], col_recv.at[8 + m], mate_chip),
        ]

    column = [down_z(m) for m in range(2)]
    for m in (1, 0):
        for h in range(2):
            loads[1 + 2 * m + h].wait()
            act2[h, m] = stage2[h, m].astype(BF16)
        column[m][0].start()
        column[m][1].start()
        weights2[level, m] = act2[side, m]

    left = pl.ds(pl.multiple_of(core * half, half), half)
    swaps = [
        Exchange(packed, land, place, swap_send.at[k], swap_recv.at[k], k == 2)
        for k, land in enumerate((cot.at[0, core], rows.at[0, core], back))
    ]
    shares = [
        Share(
            swaps[k], buf, place, partner_chip, sibling,
            share_send.at[k], share_recv.at[k],
            lambda part, spots=spots: pair_send.at[spots[part]], lambda part, spots=spots: pair_recv.at[spots[part]],
        )
        for k, (buf, spots) in enumerate(((cot, (4, 0)), (rows, (5, 8))))
    ]
    slot_matrix(route, pick)
    live = live_rows(doc_len, lanes)
    masked = jnp.where(live, cot_docs[:, left], jnp.zeros((lanes, half), BF16))
    packed[...] = dot(pick[...], masked).astype(BF16).reshape(packed.shape)

    for m in range(2):
        for k, copy in enumerate(spread[m]):
            copy.wait_recv()
            gathers[m][1 + k].start()
        if m == 0:
            documents.start()
        for gather in gathers[m][:3]:
            gather.forward()
        if m == 1:
            column[1][0].wait_recv()
            column[1][2].start()
        gathers[m][3].forward()
    swaps[0].start()

    def normalize_one(pos, source):
        floated = source.astype(F32)
        square = jnp.sum(floated * floated, axis=-1, keepdims=True)
        normed1[pos] = (floated * rms_of(square, width)).astype(BF16)

    normalize_one(col, docs[...])
    documents.forward()
    documents.near()
    doc_pair(3).start()
    doc_pair(1).start()
    for gather in gathers[0]:
        gather.near()
        gather.far()

    def matrix1(m):
        return weights1[:, m].reshape(width, hidden1)

    def give1(step):
        pos = wrap(col + step)
        return remote(
            part1.at[pos, 1 - core], joined1.at[pos], share_send.at[2, 0, step], share_recv.at[2, 0, step], sibling
        )

    def up_one(pos):
        pre = dot(normed1[pos], matrix1(0))
        sigma = jax.nn.sigmoid(pre)
        act1[pos] = (pre * sigma).astype(BF16)
        gate1[pos] = (sigma * (1.0 + pre * (1.0 - sigma))).astype(BF16)

    def down_one(step):
        pos = wrap(col + step)
        for number in range(2):
            h = lax.rem(1 - core + number, 2)
            piece = weights1[pl.ds(8 * h, 8), 1].reshape(half, hidden1)
            part1[pos, h] = dot(act1[pos], piece, (1, 1)).astype(BF16)
            if number == 0:
                give1(step).start()

    def join_one(step):
        pos = wrap(col + step)
        give1(step).wait_recv()
        joined1[pos] = (part1[pos, core].astype(F32) + joined1[pos].astype(F32)).astype(BF16)

    up_one(col)
    documents.far()
    doc_pair(2).start()
    documents.drain()
    for step in (3, 1, 2):
        pos = wrap(col + step)
        doc_pair(step).wait()
        normalize_one(pos, normed1[pos])
        up_one(pos)
    shares[0].turn()
    for gather in gathers[1]:
        gather.near()
        gather.far()
    hold = lanes // 2
    reduce1 = Scatter(
        lambda pos, part: joined1.at[pos, pl.ds(part * hold, hold)],
        (through1, summed1, landed1),
        col,
        on_y,
        ring_send.at[9],
        ring_recv.at[9],
    )
    down_one(2)
    down_one(1)
    join_one(2)
    reduce1.first[0].start()
    reduce1.first[1].start()
    down_one(3)
    join_one(1)
    reduce1.first[2].start()
    down_one(0)
    join_one(3)
    reduce1.first[3].start()
    column[0][0].wait_recv()
    column[0][2].start()
    reduce1.forward()
    join_one(0)
    reduce1.finish()
    for part in range(2):
        where = slice(part * hold, (part + 1) * hold)
        out1[where] = (docs[where, left].astype(F32) + reduce1.total(part)).astype(BF16)
    swaps[0].drain()
    packed[...] = dot(pick[...], out1[...]).astype(BF16).reshape(packed.shape)
    swaps[1].start()
    shares[0].own()
    shares[0].partner(0)
    shares[0].partner(1)

    def flat(ref, path, h):
        return ref[path, h].reshape(count, half)

    def piece2(m, h, columns):
        return weights2[2 * h:2 * h + 2, m, :, columns].reshape(half, tile)

    def columns_of(number):
        return pl.ds(pl.multiple_of(number * tile, tile), tile)

    column[1][1].wait_recv()
    column[1][2].wait_recv()

    def incoming_tile(number):
        path, columns = number // 2, columns_of(lax.rem(number, 2))
        value = dot(flat(cot, path, 0), piece2(1, 0, columns)) + dot(
            flat(cot, path, 1), piece2(1, 1, columns)
        )
        stage2[path, :, :, columns] = value.reshape(2, deep, tile)

    each(0, 2, incoming_tile)
    shares[0].finish(0)
    shares[0].finish(1)
    each(2, 4, incoming_tile)
    reduce1.drain()
    for step in range(RING):
        give1(step).wait_send()
    shares[1].turn()
    shares[1].own()
    shares[1].partner(0)

    def normalize_two(path, first, parts):
        each_part = groups // 2

        def pieces_of(h):
            where = slice(first * each_part, (first + parts) * each_part)
            return rows[path, h, where].reshape(parts * deep, half).astype(F32)

        square = sum(jnp.sum(jnp.square(pieces_of(h)), axis=-1, keepdims=True) for h in range(2))
        factor = rms_of(square, width)
        for h in range(2):
            value = (pieces_of(h) * factor).astype(BF16)
            terms1[2 * path + first:2 * path + first + parts, h] = value.reshape(parts, RING, block, half)
        return factor

    def normed2(path, h):
        return terms1[2 * path:2 * path + 2, h].reshape(count, half)

    def slope_tile(path, first, parts):
        where = slice(first, first + parts)

        def step(number):
            columns = columns_of(number)
            lefts = [
                terms1[2 * path + first:2 * path + first + parts, h].reshape(parts * deep, half) for h in range(2)
            ]
            pre = dot(lefts[0], piece2(0, 0, columns)) + dot(lefts[1], piece2(0, 1, columns))
            sigma = jax.nn.sigmoid(pre)
            incoming = stage2[path, where, :, columns].reshape(parts * deep, tile)
            slope = (incoming * sigma * (1.0 + pre * (1.0 - sigma))).astype(BF16)
            act2[path, where, :, columns] = (pre * sigma).astype(BF16).reshape(parts, deep, tile)
            slopes2[path, where, :, columns] = slope.reshape(parts, deep, tile)

        return step

    factor = normalize_two(0, 0, 2)
    column[0][1].wait_recv()
    column[0][2].wait_recv()
    for m in range(2):
        column[m][0].wait_send()
        column[m][1].wait_send()
    each(0, 2, slope_tile(0, 0, 2))

    def give2(spot):
        return remote(
            part1.at[spot, 1 - core], joined1.at[spot], share_send.at[2, 0, 4 + spot], share_recv.at[2, 0, 4 + spot], sibling
        )

    def dn_tiles(path, first, parts):
        for number in range(2):
            h = lax.rem(1 - core + number, 2)
            piece = weights2[pl.ds(2 * h, 2), 0].reshape(half, hidden2)
            left2 = slopes2[path, first:first + parts].reshape(parts * deep, hidden2)
            value = dot(left2, piece, (1, 1)).astype(BF16)
            part1[2 * path + first:2 * path + first + parts, h] = value.reshape(parts, deep, half)
            if number == 0:
                for spot in range(2 * path + first, 2 * path + first + parts):
                    give2(spot).start()

    def dn_of(spot):
        return part1[spot, core].astype(F32) + joined1[spot].astype(F32)

    def to_partner(part):
        return remote(dn_sum.at[part], dn_far.at[part], pair_send.at[6 + part], pair_recv.at[6 + part], partner_chip)

    def dn_out(part):
        give2(2 + part).wait_recv()
        dn_sum[part] = dn_of(2 + part).astype(BF16)
        to_partner(part).start()

    shares[1].finish(0)
    normalize_two(1, 0, 1)
    each(0, 2, slope_tile(1, 0, 1))
    dn_tiles(1, 0, 1)
    shares[1].partner(1)
    dn_out(0)
    shares[1].finish(1)
    normalize_two(1, 1, 1)
    each(0, 2, slope_tile(1, 1, 1))
    dn_tiles(1, 1, 1)
    dn_out(1)
    dn_tiles(0, 0, 2)

    def term_tiles(m, lefts, right):
        def step(number):
            columns = columns_of(number)
            for h in range(2):
                value = sum(
                    dot(lefts(path, h), right[path, :, :, columns].reshape(count, tile), (0, 0))
                    for path in range(2)
                )
                terms2[2 * h:2 * h + 2, m, :, columns] = value.astype(BF16).reshape(2, deep, tile)

        each(0, 2, step)

    def sums_z(m):
        return [
            remote(terms2.at[across, m], via2.at[m], col_send.at[10 + m], col_recv.at[10 + m], mate_chip),
            remote(terms2.at[mate, m], near2.at[m], col_send.at[12 + m], col_recv.at[12 + m], mate_chip),
            remote(via2.at[m], far2.at[m], col_send.at[14 + m], col_recv.at[14 + m], partner_chip),
        ]

    sums = [sums_z(m) for m in range(2)]
    term_tiles(1, lambda path, h: flat(cot, path, h), act2)
    sums[1][0].start()
    sums[1][1].start()

    def swap_mean(part):
        where = pl.ds(part * deep, deep)
        return remote(mean_out.at[where], mean_in.at[where], col_send.at[part], col_recv.at[part], sibling)

    swaps[1].drain()
    for part in range(2):
        give2(part).wait_recv()
        to_partner(part).wait_recv()
        where = slice(part * (groups // 2), (part + 1) * (groups // 2))
        lines = slice(part * deep, (part + 1) * deep)
        scale = factor[lines]
        normed = rows[0, core, where].reshape(deep, half).astype(F32) * scale
        value = dn_of(part) + dn_far[part].astype(F32)
        mean = jnp.sum(value * normed, axis=-1, keepdims=True)
        mean_out[lines] = jnp.broadcast_to(mean, (deep, mean_out.shape[1]))
        swap_mean(part).start()
        swap_mean(part).wait_recv()
        mean = (mean + mean_in[lines, 0:1]) / width
        result = cot[0, core, where].reshape(deep, half).astype(F32) + scale * (value - normed * mean)
        packed[where] = result.astype(BF16).reshape(groups // 2, -1, half)
        swaps[2].start_back(part)
    term_tiles(0, normed2, slopes2)
    sums[0][0].start()
    sums[0][1].start()
    sums[1][0].wait_recv()
    via2[1] = (terms2[partner, 1].astype(F32) + via2[1].astype(F32)).astype(BF16)
    sums[1][2].start()

    each(1, groups, swaps[2].wait)
    upstream[col, core] = dot(pick[...], back[...].reshape(count, half), (0, 0)).astype(BF16)
    lifts = Gather(
        lambda part: upstream.at[col, core, pl.ds(part * hold, hold)],
        lambda pos, part: upstream.at[pos, core, pl.ds(part * hold, hold)],
        col,
        on_y,
        ring_send.at[10],
        ring_recv.at[10],
    )
    lifts.start()

    def lift_pair(step):
        where = upstream.at[wrap(col + step), core]
        return remote(where, where, pair_send.at[10 + step], pair_recv.at[10 + step], sibling)

    lift_pair(0).start()
    lifts.forward()
    lifts.near()
    lift_pair(3).start()
    lift_pair(1).start()

    def slope_one(pos):
        incoming = dot(upstream[pos, 0], weights1[0:8, 1].reshape(half, hidden1)) + dot(
            upstream[pos, 1], weights1[8:16, 1].reshape(half, hidden1)
        )
        joined1[pos] = (incoming * gate1[pos].astype(F32)).astype(BF16)

    lifts.far()
    lift_pair(2).start()
    for step in range(RING):
        lift_pair(step).wait_recv()

    def term_one(m, lefts, right):
        for h in range(2):
            value = dot(lefts(h).reshape(RING * lanes, half), right[...].reshape(RING * lanes, hidden1), (0, 0))
            terms1[2 * h:2 * h + 2, m] = value.astype(BF16).reshape(2, RING, block, hidden1)

    def scatter_x(m):
        return Scatter(
            lambda pos, part: terms1.at[pos, m, pl.ds(2 * part, 2)],
            (through_x.at[m], summed_x.at[m], landed_x.at[m]),
            row,
            lambda pos: (level, pos * RING + col, core),
            ring_send.at[11 + m],
            ring_recv.at[11 + m],
        )

    plane = [scatter_x(m) for m in range(2)]
    term_one(1, lambda h: upstream[:, h], act1)
    plane[1].start()
    each(0, RING, slope_one)
    term_one(0, lambda h: normed1[:, :, h * half:(h + 1) * half], joined1)
    plane[0].start()
    plane[1].forward()
    sums[0][0].wait_recv()
    via2[0] = (terms2[partner, 0].astype(F32) + via2[0].astype(F32)).astype(BF16)
    sums[0][2].start()
    plane[0].forward()

    def along_back(step, m):
        other = wrap(col + step)
        number = 16 + 4 * m + step
        return remote(
            mid.at[m, other], final1.at[m, col], col_send.at[number], col_recv.at[number],
            (level, row * RING + other, core),
        )

    for m in (1, 0):
        plane[m].finish()
        for part in range(2):
            mid[m, 2 * part:2 * part + 2] = plane[m].total(part).astype(BF16)
        for step in (2, 1, 3):
            along_back(step, m).start()
        final1[m, col] = mid[m, col]
    own_side = pl.ds(pl.multiple_of(side * hidden2, hidden2), hidden2)
    other_side = pl.ds(pl.multiple_of((1 - side) * hidden2, hidden2), hidden2)
    for m in (1, 0):
        sums[m][1].wait_recv()
        sum_all[m, 0:deep, own_side] = (terms2[level, m].astype(F32) + near2[m].astype(F32)).astype(BF16)
        sums[m][2].wait_recv()
        sum_all[m, 0:deep, other_side] = far2[m]
    rows2, rows1 = pl.ds(0, deep), pl.ds(deep, block)
    keeps = [
        pltpu.make_async_copy(sum_all.at[:, part], sums_out.at[:, part], local_sem.at[k])
        for k, part in enumerate((rows2, rows1))
    ]
    keeps[0].start()
    for m in (1, 0):
        for step in (1, 3, 2):
            along_back(step, m).wait_recv()
        for q in range(RING):
            sum_all[m, deep:deep + block, q * hidden1:(q + 1) * hidden1] = final1[m, q]
    keeps[1].start()

    for copy in spread[0] + spread[1] + [column[0][2], column[1][2]] + sums[0] + sums[1]:
        copy.wait_send()
    for ring in gathers[0] + gathers[1] + [lifts] + plane + [swaps[2]] + shares:
        ring.drain()
    for step in range(RING):
        lift_pair(step).wait_send()
    for step in (1, 2, 3):
        along_back(step, 0).wait_send()
        along_back(step, 1).wait_send()
        give2(step).wait_send()
    give2(0).wait_send()
    to_partner(0).wait_send()
    to_partner(1).wait_send()
    swap_mean(0).wait_send()
    swap_mean(1).wait_send()
    for keep in keeps:
        keep.wait()


def outer_step(scales, wt1, mom1, sum1, wt2, mom2, sum2, new_wt1, new_mom1, new_wt2, new_mom2):
    def step(scale, weights, moment, total, new_weights, new_moment):
        delta = total[...].astype(F32) / scale
        moved = MOMENTUM * moment[...] + delta
        new_moment[...] = moved
        new_weights[...] = weights[...] - OUTER_RATE * (delta + MOMENTUM * moved)

    step(scales[1], wt2, mom2, sum2, new_wt2, new_mom2)

    @pl.when((pl.program_id(0) == 0) & (pl.program_id(1) == 0))
    def _():
        step(scales[0], wt1, mom1, sum1, new_wt1, new_mom1)


def local(docs, cot, route, doc_len, wt1, mom1, wt2, mom2):
    blocks, block, width = docs.shape
    groups = lax.axis_size("ba")
    levels = lax.axis_size("aa")
    slots = groups * SLOT
    count, lanes = slots * block, blocks * block
    hidden = wt1.shape[-1]
    whole = pl.BlockSpec(memory_space=pltpu.VMEM)
    anywhere = pl.BlockSpec(memory_space=pl.ANY)
    half, quarter = width // 2, width // 4
    per = count // groups
    small = width // 16
    hidden1, hidden2 = hidden // RING, hidden // 2

    def vmem(*sizes, kind=BF16):
        return pltpu.VMEM(sizes, kind)

    def dma(*sizes):
        return pltpu.SemaphoreType.DMA(sizes)

    hold = lanes // 2
    sums = pl.pallas_call(
        kernel,
        out_shape=jax.ShapeDtypeStruct((2, quarter + small, hidden), BF16),
        in_specs=[whole, whole, whole, whole, anywhere, anywhere],
        out_specs=anywhere,
        scratch_shapes=[
            vmem(count, lanes),
            vmem(2, quarter + small, hidden),
            vmem(2, small, hidden, kind=F32),
            vmem(2, 2, quarter, hidden2, kind=F32),
            vmem(RING, 2, small, hidden1),
            vmem(16, 2, small, hidden1),
            vmem(RING, 2, quarter, hidden2),
            vmem(RING, lanes, width),
            vmem(RING, lanes, hidden1),
            vmem(RING, lanes, hidden1),
            vmem(RING, 2, lanes, half),
            vmem(RING, lanes, half),
            vmem(2, hold, half),
            vmem(2, hold, half),
            vmem(4, hold, half),
            vmem(lanes, half),
            vmem(groups, per, half),
            vmem(2, 2, groups, per, half),
            vmem(2, 2, groups, per, half),
            vmem(groups, per, half),
            vmem(2, 2, quarter, hidden2),
            vmem(2, 2, quarter, hidden2),
            vmem(2, quarter, half),
            vmem(2, quarter, half),
            vmem(count, 128, kind=F32),
            vmem(count, 128, kind=F32),
            vmem(RING, 2, quarter, hidden2),
            vmem(2, quarter, hidden2),
            vmem(2, quarter, hidden2),
            vmem(2, quarter, hidden2),
            vmem(RING, 2, lanes, half),
            vmem(RING, 2, RING, small, hidden1),
            vmem(2, 2, 2, small, hidden1),
            vmem(2, 2, 2, small, hidden1),
            vmem(2, 4, 2, small, hidden1),
            vmem(2, RING, small, hidden1),
            vmem(2, RING, small, hidden1),
            dma(13, 6),
            dma(13, 6),
            dma(3, groups),
            dma(3, groups),
            dma(3, 2, groups),
            dma(3, 2, groups),
            dma(14),
            dma(14),
            dma(24),
            dma(24),
            dma(5),
        ],
        compiler_params=pltpu.CompilerParams(
            collective_id=0, has_side_effects=True, vmem_limit_bytes=VMEM_LIMIT
        ),
        cost_estimate=pl.CostEstimate(flops=100_000_000_000, bytes_accessed=40_000_000, transcendentals=2_000_000),
        name="window",
    )(docs.reshape(lanes, width), cot.reshape(lanes, width), route.T, doc_len[None], wt1[0], wt2[0])

    steps = 2
    once = pl.BlockSpec((2, small, hidden), lambda m, number: (0, 0, 0))
    part = pl.BlockSpec((1, quarter // steps, hidden), lambda m, number: (m, number, 0))
    last = pl.BlockSpec((2, small, hidden), lambda m, number: (0, quarter // small, 0))
    like1, like2 = (jax.ShapeDtypeStruct((2, rows, hidden), F32) for rows in (small, quarter))
    results = pl.pallas_call(
        functools.partial(outer_step, (groups, levels)),
        grid=(2, steps),
        out_shape=[like1, like1, like2, like2],
        in_specs=[once, once, last, part, part, part],
        out_specs=[once, once, part, part],
        compiler_params=pltpu.CompilerParams(vmem_limit_bytes=24 * 1024 * 1024),
        name="outer",
    )(wt1[0], mom1[0], sums, wt2[0], mom2[0], sums)
    return tuple(result[None] for result in results)


def solution(mesh):
    return jax.shard_map(
        local,
        mesh=mesh,
        in_specs=(
            P(("aa", "ba"), None, None),
            P(("aa", "ba"), None, None),
            P(("aa", "ba"), None),
            P(("aa", "ba")),
            P("aa", None, "ba", "ma"),
            P("aa", None, "ba", "ma"),
            P("ba", None, "aa", "ma"),
            P("ba", None, "aa", "ma"),
        ),
        out_specs=(
            P("aa", None, "ba", "ma"),
            P("aa", None, "ba", "ma"),
            P("ba", None, "aa", "ma"),
            P("ba", None, "aa", "ma"),
        ),
        check_vma=False,
    )
```

```python
import functools

import jax
import jax.numpy as jnp
from jax import lax
from jax.experimental import pallas as pl
from jax.experimental.pallas import tpu as pltpu
from jax.sharding import PartitionSpec as P

SLOT = 2
EPS = 1e-05
MOMENTUM = 0.9
OUTER_RATE = 0.7

MESH = pl.DeviceIdType.MESH
BF16 = jnp.bfloat16
F32 = jnp.float32
RING = 4
VMEM_LIMIT = 54 * 1024 * 1024


def dot(left, right, contract=(1, 0)):
    return lax.dot_general(
        left,
        right,
        (((contract[0],), (contract[1],)), ((), ())),
        preferred_element_type=F32,
    )


def wrap(index, size=RING):
    return lax.rem(index + size, size)


def remote(source, target, send, recv, device):
    return pltpu.make_async_remote_copy(
        src_ref=source,
        dst_ref=target,
        send_sem=send,
        recv_sem=recv,
        device_id=device,
        device_id_type=MESH,
    )


def each(first, last, step):
    def body(number, carry):
        step(number)
        return carry

    lax.fori_loop(first, last, body, 0)


class Gather:
    def __init__(self, own, land, rank, device, send, recv):
        up, down = wrap(rank + 1), wrap(rank - 1)

        def copy(number, source, target, to):
            return remote(source, target, send.at[number], recv.at[number], device(to))

        self.direct = [
            copy(0, own(0), land(rank, 0), up),
            copy(1, own(1), land(rank, 1), down),
            copy(2, own(1), land(rank, 1), up),
            copy(3, own(0), land(rank, 0), down),
        ]
        self.passed = [
            copy(4, land(down, 0), land(down, 0), up),
            copy(5, land(up, 1), land(up, 1), down),
        ]

    def start(self):
        for copy in self.direct:
            copy.start()

    def forward(self):
        for near, far in zip(self.direct[:2], self.passed):
            near.wait_recv()
            far.start()

    def near(self):
        for copy in self.direct[2:]:
            copy.wait_recv()

    def far(self):
        for copy in self.passed:
            copy.wait_recv()

    def drain(self):
        for copy in self.direct + self.passed:
            copy.wait_send()


class Scatter:
    def __init__(self, own, bufs, rank, device, send, recv):
        up, down, far = wrap(rank + 1), wrap(rank - 1), wrap(rank + 2)
        through, summed, landed = bufs

        def copy(number, source, target, to):
            return remote(source, target, send.at[number], recv.at[number], device(to))

        self.first = [
            copy(0, own(far, 0), through.at[0], up),
            copy(1, own(far, 1), through.at[1], down),
            copy(2, own(up, 1), landed.at[1], up),
            copy(3, own(down, 0), landed.at[2], down),
        ]
        self.second = [
            copy(4, summed.at[0], landed.at[0], up),
            copy(5, summed.at[1], landed.at[3], down),
        ]
        self.through, self.summed, self.landed = through, summed, landed
        self.own, self.rank = own, rank

    def start(self):
        for copy in self.first:
            copy.start()

    def forward(self):
        for which in range(2):
            self.first[which].wait_recv()
            mine = self.own(wrap(self.rank + 1 - 2 * which), which)[...]
            total = mine.astype(F32) + self.through[which].astype(F32)
            self.summed[which] = total.astype(BF16)
            self.second[which].start()

    def finish(self):
        for copy in self.first[2:] + self.second:
            copy.wait_recv()

    def total(self, half):
        return self.own(self.rank, half)[...].astype(F32) + (
            self.landed[half].astype(F32) + self.landed[2 + half].astype(F32)
        )

    def drain(self):
        for copy in self.first + self.second:
            copy.wait_send()


class Exchange:
    def __init__(self, packed, land, place, send, recv, back=False):
        self.place, self.groups, self.back = place, packed.shape[0], back
        self.packed, self.land, self.send, self.recv = packed, land, send, recv

    def copy(self, step):
        level, base, core = self.place
        target = lax.rem(base + step, self.groups)
        return remote(
            self.packed.at[lax.rem(self.groups - step, self.groups) if self.back else target],
            self.land.at[base if self.back else step],
            self.send.at[step],
            self.recv.at[step],
            (level, target, core),
        )

    def start(self):
        each(1, self.groups, lambda step: self.copy(step).start())
        base = self.place[1]
        self.land[0] = self.packed[base]

    def start_back(self, part):
        middle = self.groups // 2
        if part == 0:
            each(middle + 1, self.groups, lambda step: self.copy(step).start())
            self.land[self.place[1]] = self.packed[0]
        else:
            each(1, middle + 1, lambda step: self.copy(step).start())

    def wait(self, step):
        self.copy(step).wait_recv()

    def drain(self):
        each(1, self.groups, lambda step: self.copy(step).wait_send())


class Share:
    def __init__(self, exchange, rows, place, partner, sibling, send, recv, last_send, last_recv):
        core = place[2]
        self.exchange, self.groups = exchange, exchange.groups

        def copy(path, step):
            mine = rows.at[0, core, step]
            if path == 0:
                return remote(mine, mine, send.at[0, step], recv.at[0, step], sibling)
            return remote(mine, rows.at[1, core, step], send.at[1, step], recv.at[1, step], partner)

        self.copy = copy
        self.count = self.groups // 2

        def last(part):
            where = rows.at[1, core, pl.ds(part * self.count, self.count)]
            return remote(where, where, last_send(part), last_recv(part), sibling)

        self.last = [last(part) for part in range(2)]

    def turn(self):
        def step(number):
            self.copy(1, number).start()
            self.copy(0, number).start()

        def arrived(number):
            self.exchange.wait(number)
            step(number)

        step(0)
        each(1, self.groups, arrived)

    def own(self):
        each(0, self.groups, lambda step: self.copy(0, step).wait_recv())

    def partner(self, part):
        first = part * self.count
        each(first, first + self.count, lambda step: self.copy(1, step).wait_recv())
        self.last[part].start()

    def finish(self, part):
        self.last[part].wait_recv()

    def drain(self):
        def step(number):
            self.copy(0, number).wait_send()
            self.copy(1, number).wait_send()

        each(0, self.groups, step)
        for last in self.last:
            last.wait_send()


def greet(devices):
    barrier = pltpu.get_barrier_semaphore()
    for device in devices:
        pl.semaphore_signal(barrier, inc=1, device_id=device, device_id_type=MESH)
    pl.semaphore_wait(barrier, len(devices))


def doc_of_row(lanes, docs):
    row = lax.broadcasted_iota(jnp.int32, (lanes, docs), 0) // (lanes // docs)
    return (row == lax.broadcasted_iota(jnp.int32, (lanes, docs), 1)).astype(F32)


def slot_matrix(route, pick):
    count, lanes = pick.shape
    docs = route.shape[1]
    block = lanes // docs
    spread = jnp.broadcast_to(route[...].astype(F32), (128, docs))
    by_row = dot(spread, doc_of_row(lanes, docs), (1, 1))[0:docs]
    target = dot(doc_of_row(docs, docs), spread, (1, 1))[:, 0:1]
    own = lax.broadcasted_iota(jnp.int32, (docs, lanes), 1)
    earlier = lax.broadcasted_iota(jnp.int32, (docs, lanes), 0) < own // block
    rank = jnp.sum(jnp.where((by_row == target) & earlier, 1.0, 0.0), axis=0, keepdims=True)
    place = (by_row[0:1] * SLOT + rank) * block + lax.rem(own[0:1], block).astype(F32)
    slots = lax.broadcasted_iota(jnp.int32, (count, lanes), 0).astype(F32)
    pick[...] = jnp.where(slots == place, 1.0, 0.0).astype(BF16)


def live_rows(doc_len, lanes):
    docs = doc_len.shape[1]
    lengths = jnp.broadcast_to(doc_len[...].astype(F32), (128, docs))
    lengths = dot(doc_of_row(lanes, docs), lengths, (1, 1))[:, 0:1]
    position = lax.rem(lax.broadcasted_iota(jnp.int32, (lanes, 1), 0), lanes // docs)
    return position.astype(F32) < lengths


def rms_of(square, width):
    return lax.rsqrt(square / width + EPS)


def kernel(
    docs, cot_docs, route, doc_len, wt1, wt2,
    sums_out,
    pick, sum_all,
    stage1, stage2, own1, weights1, weights2,
    normed1, act1, gate1, part1, joined1, through1, summed1, landed1, out1,
    packed, cot, rows, back,
    act2, slopes2, dn_sum, dn_far, mean_out, mean_in,
    terms2, near2, via2, far2,
    upstream, terms1, through_x, summed_x, landed_x, mid, final1,
    ring_send, ring_recv, swap_send, swap_recv, share_send, share_recv, pair_send, pair_recv,
    col_send, col_recv, local_sem,
):
    level, base, core = lax.axis_index("aa"), lax.axis_index("ba"), lax.axis_index("ma")
    row, col = base // RING, lax.rem(base, RING)
    lanes, width = docs.shape
    groups = packed.shape[0]
    count = groups * packed.shape[1]
    half, quarter = width // 2, width // 4
    block, deep = weights1.shape[2], weights2.shape[2]
    hidden1, hidden2 = weights1.shape[3], weights2.shape[3]
    tile = hidden2 // 2
    mate, partner = level + 1 - 2 * lax.rem(level, 2), RING - 1 - level
    across = RING - 1 - mate
    side = level // 2
    place = (level, base, core)
    sibling = (level, base, 1 - core)
    mate_chip, partner_chip = (mate, base, core), (partner, base, core)

    loads = [
        pltpu.make_async_copy(wt1, stage1, local_sem.at[0]),
    ] + [
        pltpu.make_async_copy(
            wt2.at[m, :, pl.ds(h * hidden2, hidden2)], stage2.at[h, m], local_sem.at[1 + 2 * m + h]
        )
        for m in range(2)
        for h in range(2)
    ]
    for load in loads:
        load.start()
    greet(
        [sibling, mate_chip, partner_chip]
        + [(level, lax.rem(base + step, groups), core) for step in range(1, groups)]
    )

    loads[0].wait()
    for q in range(RING):
        for m in range(2):
            own1[q, m] = stage1[m, :, q * hidden1:(q + 1) * hidden1].astype(BF16)
    weights1[base] = own1[col]

    def along(m, step):
        other = wrap(col + step)
        number = 4 * m + step
        return remote(
            own1.at[other, m],
            weights1.at[base, m],
            share_send.at[2, 1, number],
            share_recv.at[2, 1, number],
            (level, row * RING + other, core),
        )

    def gather_x(m, step, number):
        fixed = wrap(col + step)
        rows_of = lambda part: pl.ds(part * (block // 2), block // 2)
        land = lambda pos, part: weights1.at[pos * RING + fixed, m, rows_of(part)]
        own = (lambda part: own1.at[col, m, rows_of(part)]) if step == 0 else (lambda part: land(row, part))
        device = lambda pos: (level, pos * RING + col, core)
        return Gather(own, land, row, device, ring_send.at[number], ring_recv.at[number])

    spread = [[along(m, step) for step in (1, 3, 2)] for m in range(2)]
    gathers = [[gather_x(m, step, 4 * m + k) for k, step in enumerate((0, 3, 1, 2))] for m in range(2)]
    for m in range(2):
        for copy in spread[m]:
            copy.start()
        gathers[m][0].start()

    rows_half = lanes // 2
    rows_part = rows_half // 2
    on_y = lambda pos: (level, row * RING + pos, core)

    def doc_part(pos, part):
        return normed1.at[pos, pl.ds(pl.multiple_of(core * rows_half + part * rows_part, rows_part), rows_part)]

    documents = Gather(
        lambda part: docs.at[pl.ds(pl.multiple_of(core * rows_half + part * rows_part, rows_part), rows_part)],
        doc_part,
        col,
        on_y,
        ring_send.at[8],
        ring_recv.at[8],
    )
    def doc_pair(step):
        where = normed1.at[wrap(col + step), pl.ds(pl.multiple_of(core * rows_half, rows_half), rows_half)]
        return remote(where, where, pair_send.at[step], pair_recv.at[step], sibling)

    def down_z(m):
        return [
            remote(act2.at[1 - side, m], weights2.at[level, m], col_send.at[4 + m], col_recv.at[4 + m], partner_chip),
            remote(act2.at[side, m], weights2.at[level, m], col_send.at[6 + m], col_recv.at[6 + m], mate_chip),
            remote(weights2.at[partner, m], weights2.at[partner, m], col_send.at[8 + m], col_recv.at[8 + m], mate_chip),
        ]

    column = [down_z(m) for m in range(2)]
    for m in (1, 0):
        for h in range(2):
            loads[1 + 2 * m + h].wait()
            act2[h, m] = stage2[h, m].astype(BF16)
        column[m][0].start()
        column[m][1].start()
        weights2[level, m] = act2[side, m]

    left = pl.ds(pl.multiple_of(core * half, half), half)
    swaps = [
        Exchange(packed, land, place, swap_send.at[k], swap_recv.at[k], k == 2)
        for k, land in enumerate((cot.at[0, core], rows.at[0, core], back))
    ]
    shares = [
        Share(
            swaps[k], buf, place, partner_chip, sibling,
            share_send.at[k], share_recv.at[k],
            lambda part, spots=spots: pair_send.at[spots[part]], lambda part, spots=spots: pair_recv.at[spots[part]],
        )
        for k, (buf, spots) in enumerate(((cot, (4, 0)), (rows, (5, 8))))
    ]
    slot_matrix(route, pick)
    live = live_rows(doc_len, lanes)
    masked = jnp.where(live, cot_docs[:, left], jnp.zeros((lanes, half), BF16))
    packed[...] = dot(pick[...], masked).astype(BF16).reshape(packed.shape)

    for m in range(2):
        for k, copy in enumerate(spread[m]):
            copy.wait_recv()
            gathers[m][1 + k].start()
        if m == 0:
            documents.start()
        for gather in gathers[m][:3]:
            gather.forward()
        if m == 1:
            column[1][0].wait_recv()
            column[1][2].start()
        gathers[m][3].forward()
    swaps[0].start()

    def normalize_one(pos, source):
        floated = source.astype(F32)
        square = jnp.sum(floated * floated, axis=-1, keepdims=True)
        normed1[pos] = (floated * rms_of(square, width)).astype(BF16)

    normalize_one(col, docs[...])
    documents.forward()
    documents.near()
    doc_pair(3).start()
    doc_pair(1).start()
    for gather in gathers[0]:
        gather.near()
        gather.far()

    def matrix1(m):
        return weights1[:, m].reshape(width, hidden1)

    def give1(step):
        pos = wrap(col + step)
        return remote(
            part1.at[pos, 1 - core], joined1.at[pos], share_send.at[2, 0, step], share_recv.at[2, 0, step], sibling
        )

    def up_one(pos):
        pre = dot(normed1[pos], matrix1(0))
        sigma = jax.nn.sigmoid(pre)
        act1[pos] = (pre * sigma).astype(BF16)
        gate1[pos] = (sigma * (1.0 + pre * (1.0 - sigma))).astype(BF16)

    def down_one(step):
        pos = wrap(col + step)
        for number in range(2):
            h = lax.rem(1 - core + number, 2)
            piece = weights1[pl.ds(8 * h, 8), 1].reshape(half, hidden1)
            part1[pos, h] = dot(act1[pos], piece, (1, 1)).astype(BF16)
            if number == 0:
                give1(step).start()

    def join_one(step):
        pos = wrap(col + step)
        give1(step).wait_recv()
        joined1[pos] = (part1[pos, core].astype(F32) + joined1[pos].astype(F32)).astype(BF16)

    up_one(col)
    documents.far()
    doc_pair(2).start()
    documents.drain()
    for step in (3, 1, 2):
        pos = wrap(col + step)
        doc_pair(step).wait()
        normalize_one(pos, normed1[pos])
        up_one(pos)
    shares[0].turn()
    for gather in gathers[1]:
        gather.near()
        gather.far()
    hold = lanes // 2
    reduce1 = Scatter(
        lambda pos, part: joined1.at[pos, pl.ds(part * hold, hold)],
        (through1, summed1, landed1),
        col,
        on_y,
        ring_send.at[9],
        ring_recv.at[9],
    )
    down_one(2)
    down_one(1)
    join_one(2)
    reduce1.first[0].start()
    reduce1.first[1].start()
    down_one(3)
    join_one(1)
    reduce1.first[2].start()
    down_one(0)
    join_one(3)
    reduce1.first[3].start()
    column[0][0].wait_recv()
    column[0][2].start()
    reduce1.forward()
    join_one(0)
    reduce1.finish()
    for part in range(2):
        where = slice(part * hold, (part + 1) * hold)
        out1[where] = (docs[where, left].astype(F32) + reduce1.total(part)).astype(BF16)
    swaps[0].drain()
    packed[...] = dot(pick[...], out1[...]).astype(BF16).reshape(packed.shape)
    swaps[1].start()
    shares[0].own()
    shares[0].partner(0)
    shares[0].partner(1)

    def flat(ref, path, h):
        return ref[path, h].reshape(count, half)

    def piece2(m, h, columns):
        return weights2[2 * h:2 * h + 2, m, :, columns].reshape(half, tile)

    def columns_of(number):
        return pl.ds(pl.multiple_of(number * tile, tile), tile)

    column[1][1].wait_recv()
    column[1][2].wait_recv()

    def incoming_tile(number):
        path, columns = number // 2, columns_of(lax.rem(number, 2))
        value = dot(flat(cot, path, 0), piece2(1, 0, columns)) + dot(
            flat(cot, path, 1), piece2(1, 1, columns)
        )
        stage2[path, :, :, columns] = value.reshape(2, deep, tile)

    each(0, 2, incoming_tile)
    shares[0].finish(0)
    shares[0].finish(1)
    each(2, 4, incoming_tile)
    reduce1.drain()
    for step in range(RING):
        give1(step).wait_send()
    shares[1].turn()
    shares[1].own()
    shares[1].partner(0)

    def normalize_two(path, first, parts):
        each_part = groups // 2

        def pieces_of(h):
            where = slice(first * each_part, (first + parts) * each_part)
            return rows[path, h, where].reshape(parts * deep, half).astype(F32)

        square = sum(jnp.sum(jnp.square(pieces_of(h)), axis=-1, keepdims=True) for h in range(2))
        factor = rms_of(square, width)
        for h in range(2):
            value = (pieces_of(h) * factor).astype(BF16)
            terms1[2 * path + first:2 * path + first + parts, h] = value.reshape(parts, RING, block, half)
        return factor

    def normed2(path, h):
        return terms1[2 * path:2 * path + 2, h].reshape(count, half)

    def slope_tile(path, first, parts):
        where = slice(first, first + parts)

        def step(number):
            columns = columns_of(number)
            lefts = [
                terms1[2 * path + first:2 * path + first + parts, h].reshape(parts * deep, half) for h in range(2)
            ]
            pre = dot(lefts[0], piece2(0, 0, columns)) + dot(lefts[1], piece2(0, 1, columns))
            sigma = jax.nn.sigmoid(pre)
            incoming = stage2[path, where, :, columns].reshape(parts * deep, tile)
            slope = (incoming * sigma * (1.0 + pre * (1.0 - sigma))).astype(BF16)
            act2[path, where, :, columns] = (pre * sigma).astype(BF16).reshape(parts, deep, tile)
            slopes2[path, where, :, columns] = slope.reshape(parts, deep, tile)

        return step

    factor = normalize_two(0, 0, 2)
    column[0][1].wait_recv()
    column[0][2].wait_recv()
    for m in range(2):
        column[m][0].wait_send()
        column[m][1].wait_send()
    each(0, 2, slope_tile(0, 0, 2))

    def give2(spot):
        return remote(
            part1.at[spot, 1 - core], joined1.at[spot], share_send.at[2, 0, 4 + spot], share_recv.at[2, 0, 4 + spot], sibling
        )

    def dn_tiles(path, first, parts):
        for number in range(2):
            h = lax.rem(1 - core + number, 2)
            piece = weights2[pl.ds(2 * h, 2), 0].reshape(half, hidden2)
            left2 = slopes2[path, first:first + parts].reshape(parts * deep, hidden2)
            value = dot(left2, piece, (1, 1)).astype(BF16)
            part1[2 * path + first:2 * path + first + parts, h] = value.reshape(parts, deep, half)
            if number == 0:
                for spot in range(2 * path + first, 2 * path + first + parts):
                    give2(spot).start()

    def dn_of(spot):
        return part1[spot, core].astype(F32) + joined1[spot].astype(F32)

    def to_partner(part):
        return remote(dn_sum.at[part], dn_far.at[part], pair_send.at[6 + part], pair_recv.at[6 + part], partner_chip)

    def dn_out(part):
        give2(2 + part).wait_recv()
        dn_sum[part] = dn_of(2 + part).astype(BF16)
        to_partner(part).start()

    shares[1].finish(0)
    normalize_two(1, 0, 1)
    each(0, 2, slope_tile(1, 0, 1))
    dn_tiles(1, 0, 1)
    shares[1].partner(1)
    dn_out(0)
    shares[1].finish(1)
    normalize_two(1, 1, 1)
    each(0, 2, slope_tile(1, 1, 1))
    dn_tiles(1, 1, 1)
    dn_out(1)
    dn_tiles(0, 0, 2)

    def term_tiles(m, lefts, right):
        def step(number):
            columns = columns_of(number)
            for h in range(2):
                value = sum(
                    dot(lefts(path, h), right[path, :, :, columns].reshape(count, tile), (0, 0))
                    for path in range(2)
                )
                terms2[2 * h:2 * h + 2, m, :, columns] = value.astype(BF16).reshape(2, deep, tile)

        each(0, 2, step)

    def sums_z(m):
        return [
            remote(terms2.at[across, m], via2.at[m], col_send.at[10 + m], col_recv.at[10 + m], mate_chip),
            remote(terms2.at[mate, m], near2.at[m], col_send.at[12 + m], col_recv.at[12 + m], mate_chip),
            remote(via2.at[m], far2.at[m], col_send.at[14 + m], col_recv.at[14 + m], partner_chip),
        ]

    sums = [sums_z(m) for m in range(2)]
    term_tiles(1, lambda path, h: flat(cot, path, h), act2)
    sums[1][0].start()
    sums[1][1].start()

    def swap_mean(part):
        where = pl.ds(part * deep, deep)
        return remote(mean_out.at[where], mean_in.at[where], col_send.at[part], col_recv.at[part], sibling)

    swaps[1].drain()
    for part in range(2):
        give2(part).wait_recv()
        to_partner(part).wait_recv()
        where = slice(part * (groups // 2), (part + 1) * (groups // 2))
        lines = slice(part * deep, (part + 1) * deep)
        scale = factor[lines]
        normed = rows[0, core, where].reshape(deep, half).astype(F32) * scale
        value = dn_of(part) + dn_far[part].astype(F32)
        mean = jnp.sum(value * normed, axis=-1, keepdims=True)
        mean_out[lines] = jnp.broadcast_to(mean, (deep, mean_out.shape[1]))
        swap_mean(part).start()
        swap_mean(part).wait_recv()
        mean = (mean + mean_in[lines, 0:1]) / width
        result = cot[0, core, where].reshape(deep, half).astype(F32) + scale * (value - normed * mean)
        packed[where] = result.astype(BF16).reshape(groups // 2, -1, half)
        swaps[2].start_back(part)
    term_tiles(0, normed2, slopes2)
    sums[0][0].start()
    sums[0][1].start()
    sums[1][0].wait_recv()
    via2[1] = (terms2[partner, 1].astype(F32) + via2[1].astype(F32)).astype(BF16)
    sums[1][2].start()

    each(1, groups, swaps[2].wait)
    upstream[col, core] = dot(pick[...], back[...].reshape(count, half), (0, 0)).astype(BF16)
    lifts = Gather(
        lambda part: upstream.at[col, core, pl.ds(part * hold, hold)],
        lambda pos, part: upstream.at[pos, core, pl.ds(part * hold, hold)],
        col,
        on_y,
        ring_send.at[10],
        ring_recv.at[10],
    )
    lifts.start()

    def lift_pair(step):
        where = upstream.at[wrap(col + step), core]
        return remote(where, where, pair_send.at[10 + step], pair_recv.at[10 + step], sibling)

    lift_pair(0).start()
    lifts.forward()
    lifts.near()
    lift_pair(3).start()
    lift_pair(1).start()

    def slope_one(pos):
        incoming = dot(upstream[pos, 0], weights1[0:8, 1].reshape(half, hidden1)) + dot(
            upstream[pos, 1], weights1[8:16, 1].reshape(half, hidden1)
        )
        joined1[pos] = (incoming * gate1[pos].astype(F32)).astype(BF16)


    def add_term(step):
        pos = wrap(col + step)
        lift_pair(step).wait_recv()
        for h in range(2):
            value = dot(upstream[pos, h], act1[pos], (0, 0)).reshape(2, deep, hidden1)
            if step != 0:
                value = value + stage2[h, :, :, 0:hidden1]
            if step == 2:
                terms1[2 * h:2 * h + 2, 1] = value.astype(BF16).reshape(2, RING, block, hidden1)
            else:
                stage2[h, :, :, 0:hidden1] = value

    add_term(0)
    add_term(3)
    add_term(1)
    lifts.far()
    lift_pair(2).start()
    add_term(2)

    def term_one(m, lefts, right):
        for h in range(2):
            value = dot(lefts(h).reshape(RING * lanes, half), right[...].reshape(RING * lanes, hidden1), (0, 0))
            terms1[2 * h:2 * h + 2, m] = value.astype(BF16).reshape(2, RING, block, hidden1)

    def scatter_x(m):
        return Scatter(
            lambda pos, part: terms1.at[pos, m, pl.ds(2 * part, 2)],
            (through_x.at[m], summed_x.at[m], landed_x.at[m]),
            row,
            lambda pos: (level, pos * RING + col, core),
            ring_send.at[11 + m],
            ring_recv.at[11 + m],
        )

    plane = [scatter_x(m) for m in range(2)]
    plane[1].start()
    each(0, RING, slope_one)
    term_one(0, lambda h: normed1[:, :, h * half:(h + 1) * half], joined1)
    plane[0].start()
    plane[1].forward()
    sums[0][0].wait_recv()
    via2[0] = (terms2[partner, 0].astype(F32) + via2[0].astype(F32)).astype(BF16)
    sums[0][2].start()
    plane[0].forward()

    def along_back(step, m):
        other = wrap(col + step)
        number = 16 + 4 * m + step
        return remote(
            mid.at[m, other], final1.at[m, col], col_send.at[number], col_recv.at[number],
            (level, row * RING + other, core),
        )

    for m in (1, 0):
        plane[m].finish()
        for part in range(2):
            mid[m, 2 * part:2 * part + 2] = plane[m].total(part).astype(BF16)
        for step in (2, 1, 3):
            along_back(step, m).start()
        final1[m, col] = mid[m, col]
    own_side = pl.ds(pl.multiple_of(side * hidden2, hidden2), hidden2)
    other_side = pl.ds(pl.multiple_of((1 - side) * hidden2, hidden2), hidden2)
    for m in (1, 0):
        sums[m][1].wait_recv()
        sum_all[m, 0:deep, own_side] = (terms2[level, m].astype(F32) + near2[m].astype(F32)).astype(BF16)
        sums[m][2].wait_recv()
        sum_all[m, 0:deep, other_side] = far2[m]
    rows2, rows1 = pl.ds(0, deep), pl.ds(deep, block)
    keeps = [
        pltpu.make_async_copy(sum_all.at[:, part], sums_out.at[:, part], local_sem.at[k])
        for k, part in enumerate((rows2, rows1))
    ]
    keeps[0].start()
    for m in (1, 0):
        for step in (1, 3, 2):
            along_back(step, m).wait_recv()
        for q in range(RING):
            sum_all[m, deep:deep + block, q * hidden1:(q + 1) * hidden1] = final1[m, q]
    keeps[1].start()

    for copy in spread[0] + spread[1] + [column[0][2], column[1][2]] + sums[0] + sums[1]:
        copy.wait_send()
    for ring in gathers[0] + gathers[1] + [lifts] + plane + [swaps[2]] + shares:
        ring.drain()
    for step in range(RING):
        lift_pair(step).wait_send()
    for step in (1, 2, 3):
        along_back(step, 0).wait_send()
        along_back(step, 1).wait_send()
        give2(step).wait_send()
    give2(0).wait_send()
    to_partner(0).wait_send()
    to_partner(1).wait_send()
    swap_mean(0).wait_send()
    swap_mean(1).wait_send()
    for keep in keeps:
        keep.wait()


def outer_step(scales, wt1, mom1, sum1, wt2, mom2, sum2, new_wt1, new_mom1, new_wt2, new_mom2):
    def step(scale, weights, moment, total, new_weights, new_moment):
        delta = total[...].astype(F32) / scale
        moved = MOMENTUM * moment[...] + delta
        new_moment[...] = moved
        new_weights[...] = weights[...] - OUTER_RATE * (delta + MOMENTUM * moved)

    step(scales[1], wt2, mom2, sum2, new_wt2, new_mom2)

    @pl.when((pl.program_id(0) == 0) & (pl.program_id(1) == 0))
    def _():
        step(scales[0], wt1, mom1, sum1, new_wt1, new_mom1)


def local(docs, cot, route, doc_len, wt1, mom1, wt2, mom2):
    blocks, block, width = docs.shape
    groups = lax.axis_size("ba")
    levels = lax.axis_size("aa")
    slots = groups * SLOT
    count, lanes = slots * block, blocks * block
    hidden = wt1.shape[-1]
    whole = pl.BlockSpec(memory_space=pltpu.VMEM)
    anywhere = pl.BlockSpec(memory_space=pl.ANY)
    half, quarter = width // 2, width // 4
    per = count // groups
    small = width // 16
    hidden1, hidden2 = hidden // RING, hidden // 2

    def vmem(*sizes, kind=BF16):
        return pltpu.VMEM(sizes, kind)

    def dma(*sizes):
        return pltpu.SemaphoreType.DMA(sizes)

    hold = lanes // 2
    sums = pl.pallas_call(
        kernel,
        out_shape=jax.ShapeDtypeStruct((2, quarter + small, hidden), BF16),
        in_specs=[whole, whole, whole, whole, anywhere, anywhere],
        out_specs=anywhere,
        scratch_shapes=[
            vmem(count, lanes),
            vmem(2, quarter + small, hidden),
            vmem(2, small, hidden, kind=F32),
            vmem(2, 2, quarter, hidden2, kind=F32),
            vmem(RING, 2, small, hidden1),
            vmem(16, 2, small, hidden1),
            vmem(RING, 2, quarter, hidden2),
            vmem(RING, lanes, width),
            vmem(RING, lanes, hidden1),
            vmem(RING, lanes, hidden1),
            vmem(RING, 2, lanes, half),
            vmem(RING, lanes, half),
            vmem(2, hold, half),
            vmem(2, hold, half),
            vmem(4, hold, half),
            vmem(lanes, half),
            vmem(groups, per, half),
            vmem(2, 2, groups, per, half),
            vmem(2, 2, groups, per, half),
            vmem(groups, per, half),
            vmem(2, 2, quarter, hidden2),
            vmem(2, 2, quarter, hidden2),
            vmem(2, quarter, half),
            vmem(2, quarter, half),
            vmem(count, 128, kind=F32),
            vmem(count, 128, kind=F32),
            vmem(RING, 2, quarter, hidden2),
            vmem(2, quarter, hidden2),
            vmem(2, quarter, hidden2),
            vmem(2, quarter, hidden2),
            vmem(RING, 2, lanes, half),
            vmem(RING, 2, RING, small, hidden1),
            vmem(2, 2, 2, small, hidden1),
            vmem(2, 2, 2, small, hidden1),
            vmem(2, 4, 2, small, hidden1),
            vmem(2, RING, small, hidden1),
            vmem(2, RING, small, hidden1),
            dma(13, 6),
            dma(13, 6),
            dma(3, groups),
            dma(3, groups),
            dma(3, 2, groups),
            dma(3, 2, groups),
            dma(14),
            dma(14),
            dma(24),
            dma(24),
            dma(5),
        ],
        compiler_params=pltpu.CompilerParams(
            collective_id=0, has_side_effects=True, vmem_limit_bytes=VMEM_LIMIT
        ),
        cost_estimate=pl.CostEstimate(flops=100_000_000_000, bytes_accessed=40_000_000, transcendentals=2_000_000),
        name="window",
    )(docs.reshape(lanes, width), cot.reshape(lanes, width), route.T, doc_len[None], wt1[0], wt2[0])

    steps = 2
    once = pl.BlockSpec((2, small, hidden), lambda m, number: (0, 0, 0))
    part = pl.BlockSpec((1, quarter // steps, hidden), lambda m, number: (m, number, 0))
    last = pl.BlockSpec((2, small, hidden), lambda m, number: (0, quarter // small, 0))
    like1, like2 = (jax.ShapeDtypeStruct((2, rows, hidden), F32) for rows in (small, quarter))
    results = pl.pallas_call(
        functools.partial(outer_step, (groups, levels)),
        grid=(2, steps),
        out_shape=[like1, like1, like2, like2],
        in_specs=[once, once, last, part, part, part],
        out_specs=[once, once, part, part],
        compiler_params=pltpu.CompilerParams(vmem_limit_bytes=24 * 1024 * 1024),
        name="outer",
    )(wt1[0], mom1[0], sums, wt2[0], mom2[0], sums)
    return tuple(result[None] for result in results)


def solution(mesh):
    return jax.shard_map(
        local,
        mesh=mesh,
        in_specs=(
            P(("aa", "ba"), None, None),
            P(("aa", "ba"), None, None),
            P(("aa", "ba"), None),
            P(("aa", "ba")),
            P("aa", None, "ba", "ma"),
            P("aa", None, "ba", "ma"),
            P("ba", None, "aa", "ma"),
            P("ba", None, "aa", "ma"),
        ),
        out_specs=(
            P("aa", None, "ba", "ma"),
            P("aa", None, "ba", "ma"),
            P("ba", None, "aa", "ma"),
            P("ba", None, "aa", "ma"),
        ),
        check_vma=False,
    )
```
